32 devices in a mesh: seq: 16 (over z, x, core), batch: 2 (over y).
Axes of the slice: x: 2, y: 2, z: 4, core: 2. Of those that a mesh axis runs over, the one named last changes fastest.
Arguments:
- tokens: bfloat16 [4, 2048, 768], P('batch', 'seq'), may hold values from -6 to 6
- cotangent: bfloat16 [4, 2048, 768], P('batch', 'seq'), may hold values from -6 to 6
- gains: float32 [2, 768], replicated, may hold values from 0.5 to 1.5
- mixing: bfloat16 [3, 768, 192], P(None, ('seq', 'batch')), may hold values from -0.4375 to 0.4375
- twiddle: bfloat16 [3, 192, 4, 4], replicated, may hold values from -3 to 3
- expand: bfloat16 [2, 768, 768], P(None, ('seq', 'batch')), may hold values from -0.4375 to 0.4375
- spread: bfloat16 [2, 768, 4, 4], replicated, may hold values from -3 to 3
- shrink: bfloat16 [3072, 192], P(('seq', 'batch')), may hold values from -0.21875 to 0.21875
- squeeze: bfloat16 [192, 4, 4], replicated, may hold values from -3 to 3
- kernel: float32 [3, 1536], replicated, may hold values from -3 to 3
- lifting: float32 [5, 128], replicated, may hold values from -16 to 16
- phases: float32 [128], replicated, may hold values from -3.140625 to 3.140625
- mapping: float32 [128, 128], replicated, may hold values from -1 to 1
- readout: float32 [128, 768], replicated, may hold values from -0.09375 to 0.09375
- damping: float32 [768], replicated, may hold values from 0.00048828125 to 0.03
Outputs:
- layer_output: bfloat16 [4, 2048, 768], P('batch', 'seq')
- tokens_grad: float32 [4, 2048, 768], P('batch', 'seq')
- gains_grad: float32 [2, 768], replicated
- mixing_grad: float32 [3, 768, 192], P(None, ('seq', 'batch'))
- twiddle_grad: float32 [3, 192, 4, 4], replicated
- expand_grad: float32 [2, 768, 768], P(None, ('seq', 'batch'))
- spread_grad: float32 [2, 768, 4, 4], replicated
- shrink_grad: float32 [3072, 192], P(('seq', 'batch'))
- squeeze_grad: float32 [192, 4, 4], replicated
- kernel_grad: float32 [3, 1536], replicated
- lifting_grad: float32 [5, 128], replicated
- phases_grad: float32 [128], replicated
- mapping_grad: float32 [128, 128], replicated
- readout_grad: float32 [128, 768], replicated
The draws below stay inside these ranges and needn't reach their ends.
All inputs are finite; a program needn't handle non-finite values.
Results may differ from the reference program's by a relative error of at most 0.012.
Values may be sent and summed in bfloat16 or wider, within the bound.
No kernel may reach another device: no remote copies, remote signals or barrier semaphores. Data moves between devices by JAX's collectives and lax.ppermute only.
A program may use at most 448 MiB of HBM per device.

```python
import math
import jax
import jax.numpy as jnp
from jax import lax

D = 768
FF = 3072
ORDER = 128
BLOCKS = 4
FEATS = 5
LENGTH = 2048
SEQS = 4


def level_of(rng, shape, pieces, least, top_value):
    level = 1.0
    for position, shards_of in pieces:
        draws = jax.random.uniform(jax.random.fold_in(jax.random.fold_in(rng, 6), position), (shards_of,), jnp.float32, least / len(pieces), top_value / len(pieces))
        level = level * jnp.repeat(jnp.exp(draws), shape[position] // shards_of).reshape((-1,) + (1,) * (len(shape) - 1 - position))
    return level


def gaussian(own_key, dims, scale, reach, cuts=(), kind=jnp.bfloat16):
    factor_of = level_of(own_key, dims, cuts, -0.22, 0.18) if cuts else 1.0
    array = jax.random.normal(own_key, dims, jnp.float32) * scale * factor_of
    return jnp.minimum(jnp.maximum(array, -reach), reach).astype(kind)


def setup_inputs(seed: int = 0) -> dict:
    splits = jax.random.split(jax.random.key(seed), 16)
    return {
        "tokens": gaussian(splits[0], (SEQS, LENGTH, D), 1.0, 6.0, ((0, 2), (1, 16))),
        "cotangent": gaussian(splits[1], (SEQS, LENGTH, D), 1.0, 6.0, ((0, 2), (1, 16))),
        "gains": jnp.clip(1.0 + 0.1 * jax.random.normal(splits[2], (2, D), jnp.float32), 0.5, 1.5),
        "mixing": gaussian(splits[3], (3, D, D // BLOCKS), (D // BLOCKS) ** -0.5, 0.4375, ((1, 32),)),
        "twiddle": gaussian(splits[4], (3, D // BLOCKS, BLOCKS, BLOCKS), BLOCKS ** -0.5, 3.0),
        "expand": gaussian(splits[5], (2, D, FF // BLOCKS), (D // BLOCKS) ** -0.5, 0.4375, ((1, 32),)),
        "spread": gaussian(splits[6], (2, FF // BLOCKS, BLOCKS, BLOCKS), BLOCKS ** -0.5, 3.0),
        "shrink": gaussian(splits[7], (FF, D // BLOCKS), (FF // BLOCKS) ** -0.5, 0.21875, ((0, 32),)),
        "squeeze": gaussian(splits[8], (D // BLOCKS, BLOCKS, BLOCKS), BLOCKS ** -0.5, 3.0),
        "kernel": gaussian(splits[9], (3, 2 * D), 0.6, 3.0, (), jnp.float32),
        "lifting": jnp.clip(jax.random.uniform(splits[10], (FEATS, ORDER), jnp.float32, -16.0, 16.0), -16.0, 16.0),
        "phases": jnp.clip(jax.random.uniform(splits[11], (ORDER,), jnp.float32, -3.140625, 3.140625), -3.140625, 3.140625),
        "mapping": jnp.clip(jax.random.uniform(splits[12], (ORDER, ORDER), jnp.float32, -1.0, 1.0), -1.0, 1.0),
        "readout": gaussian(splits[13], (ORDER, D), (ORDER * LENGTH // 64) ** -0.5, 0.09375, (), jnp.float32),
        "damping": jnp.clip(jnp.exp(jax.random.uniform(splits[14], (D,), jnp.float32, math.log(0.00048828125), math.log(0.03))), 0.00048828125, 0.03),
    }


HIGHEST = lax.Precision.HIGHEST

@jax.custom_vjp
def low(v):
    return lax.optimization_barrier(v.astype(jnp.bfloat16)).astype(jnp.float32)

@jax.custom_vjp
def low_back(v):
    return v

def low_keep(v):
    return (low(v), None)

def low_pass(kept, grad):
    return (grad,)

def back_keep(v):
    return (v, None)

def back_low(kept, grad):
    return (low(grad),)
low.defvjp(low_keep, low_pass)
low_back.defvjp(back_keep, back_low)

def features(length):
    positions = jnp.arange(length, dtype=jnp.int32)
    columns = [positions.astype(jnp.float32) / length]
    for harmonic in (1, 2):
        phase_now = 2.0 * math.pi / length * (harmonic * positions % length).astype(jnp.float32)
        columns.append(jnp.cos(phase_now))
        columns.append(jnp.sin(phase_now))
    return jnp.stack(columns, 1)

def make_filter(lifting, phases, mapping, readout, damping, length):
    positions = jnp.arange(length, dtype=jnp.int32).astype(jnp.float32)
    layer_one = jnp.sin(jnp.dot(features(length), lifting, precision=HIGHEST) + phases)
    layer_two = jnp.sin(jnp.dot(layer_one, mapping, precision=HIGHEST))
    return jnp.dot(layer_two, readout, precision=HIGHEST) * jnp.exp(-positions[:, None] * damping[None, :])

def layer_norm(values):
    average = lax.optimization_barrier(jnp.mean(values, -1, keepdims=True))
    centred = values - average
    variance = lax.optimization_barrier(jnp.mean(centred * centred, -1, keepdims=True))
    return centred * lax.rsqrt(variance + 1e-05)

def monarch(rounded, inner, outer):
    leading = rounded.shape[0]
    width_in = inner.shape[0] // BLOCKS
    width_out = inner.shape[1]
    section_one = jnp.einsum('rai,aij->raj', rounded.reshape(leading, BLOCKS, width_in), inner.reshape(BLOCKS, width_in, width_out), precision=HIGHEST)
    section_one = low_back(section_one)
    section_two = jnp.einsum('raj,jab->rbj', section_one, outer, precision=HIGHEST)
    return section_two.reshape(leading, BLOCKS * width_out)

def short_conv(values, taps):
    padded = jnp.pad(values, ((2, 0), (0, 0)))
    return taps[0] * padded[2:] + taps[1] * padded[1:-1] + taps[2] * padded[:-2]

def causal_conv(values, response):
    padded_len = 2 * values.shape[0]
    product = jnp.fft.rfft(values, n=padded_len, axis=0) * jnp.fft.rfft(response, n=padded_len, axis=0)
    return jnp.fft.irfft(product, n=padded_len, axis=0)[:values.shape[0]]

def sequence_layer(sequence, response, weights):
    norm_gains, mixing_all, twiddle_all, expand_all, spread_all, shrink_all, squeeze_all, kernel_all, lifting_all, phases_all, mapping_all, readout_all = weights
    width = sequence.shape[1]
    norm_one = low(layer_norm(sequence) * norm_gains[0])
    signal = low(monarch(norm_one, mixing_all[0], twiddle_all[0]))
    switch = low(monarch(norm_one, mixing_all[1], twiddle_all[1]))
    conv_in = low(low_back(short_conv(signal, kernel_all[:, :width])))
    gate_seq = low_back(short_conv(switch, kernel_all[:, width:]))
    long_out = low_back(causal_conv(conv_in, response))
    gated = low(gate_seq * long_out)
    residual = sequence + monarch(gated, mixing_all[2], twiddle_all[2])
    norm_two = low(layer_norm(residual) * norm_gains[1])
    gate_pre = monarch(norm_two, expand_all[0], spread_all[0])
    up_pre = monarch(norm_two, expand_all[1], spread_all[1])
    hidden = low(jax.nn.gelu(gate_pre) * up_pre)
    return residual + monarch(hidden, shrink_all, squeeze_all)

def reference(tokens, cotangent, gains, mixing, twiddle, expand, spread, shrink, squeeze, kernel, lifting, phases, mapping, readout, damping):
    weights = (gains, mixing.astype(jnp.float32), twiddle.astype(jnp.float32), expand.astype(jnp.float32), spread.astype(jnp.float32), shrink.astype(jnp.float32), squeeze.astype(jnp.float32), kernel, lifting, phases, mapping, readout)
    inputs = tokens.astype(jnp.float32)

    def forward(inputs_now, weights_now):
        response = make_filter(weights_now[8], weights_now[9], weights_now[10], weights_now[11], damping, LENGTH)

        def one_sequence(sequence):
            return sequence_layer(sequence, response, weights_now)
        return lax.map(jax.checkpoint(one_sequence), inputs_now)
    result, pull_back = jax.vjp(forward, inputs, weights)
    tokens_grad, weight_grads = pull_back(cotangent.astype(jnp.float32))
    return (result.astype(jnp.bfloat16), tokens_grad, weight_grads[0], weight_grads[1], weight_grads[2], weight_grads[3], weight_grads[4], weight_grads[5], weight_grads[6], weight_grads[7], weight_grads[8], weight_grads[9], weight_grads[10], weight_grads[11])
```

```python
import functools
import math

import jax
import jax.numpy as jnp
import numpy as np
from jax import lax
from jax.experimental import pallas as pl
from jax.experimental.pallas import tpu as pltpu
from jax.sharding import PartitionSpec as P

BLOCKS = 4
BOTH = ("seq", "batch")
F32 = jnp.float32
BF16 = jnp.bfloat16
HIGHEST = lax.Precision.HIGHEST
NN = ((1,), (0,))
NT = ((1,), (1,))
TN = ((0,), (0,))
ROUND_Z = (0, 4, 8, 12)
ROUND_XC = (0, 2, 1, 3)


def mm(left, right, dims=NN, precision=None):
    return lax.dot_general(
        left, right, (dims, ((), ())), preferred_element_type=F32, precision=precision
    )


def call(body, outs, operands, scratch=(), scalars=0, limit=48, flops=0):
    specs = [
        pl.BlockSpec(memory_space=pltpu.SMEM if k < scalars else pltpu.VMEM)
        for k in range(len(operands))
    ]
    return pl.pallas_call(
        body,
        out_shape=[jax.ShapeDtypeStruct(shape, kind) for shape, kind in outs],
        in_specs=specs,
        out_specs=[pl.BlockSpec(memory_space=pltpu.VMEM) for _ in outs],
        scratch_shapes=list(scratch),
        compiler_params=pltpu.CompilerParams(vmem_limit_bytes=limit << 20),
        cost_estimate=pl.CostEstimate(flops=int(flops), bytes_accessed=1 << 20, transcendentals=0),
    )(*operands)


def packed_tables(points):
    size = 2 * points
    place = np.arange(size)[:, None].astype(np.int64)
    bins = np.arange(points)[None, :]
    angle = 2.0 * np.pi / size * ((place * bins) % size)
    forward = np.concatenate([np.cos(angle), -np.sin(angle)], 1)
    forward[:, points] = np.where(np.arange(size) % 2 == 0, 1.0, -1.0)
    weight = np.where(np.arange(size) % points == 0, 1.0, 2.0) / size
    backward = (forward * weight[None, :]).T
    return forward.astype(np.float32), np.ascontiguousarray(backward).astype(np.float32)


def split_table(table):
    high = table.astype(jnp.bfloat16)
    low = (table - high.astype(np.float32)).astype(jnp.bfloat16)
    return high, low


def feature_rows(length):
    place = np.arange(length)
    rows = [place / length]
    for harmonic in (1, 2):
        angle = 2.0 * np.pi / length * ((harmonic * place) % length)
        rows += [np.cos(angle), np.sin(angle)]
    rows += [np.ones(length), np.zeros(length), np.zeros(length)]
    return np.stack(rows).astype(np.float32)


def spread_matrix(pieces, span):
    width = pieces * span
    out = np.zeros((BLOCKS, pieces, BLOCKS, span, width), np.float32)
    for b in range(BLOCKS):
        for piece in range(pieces):
            for k in range(span):
                out[b, piece, b, k, piece * span + k] = 1.0
    return out.reshape(BLOCKS, pieces * BLOCKS * span, width).astype(jnp.bfloat16)


def normalize_rows(values):
    centred = values - jnp.mean(values, -1, keepdims=True)
    factor = lax.rsqrt(jnp.mean(centred * centred, -1, keepdims=True) + 1e-05)
    return centred * factor, factor


def sincos(angle):
    turns = jnp.floor(angle * (2.0 / math.pi) + 0.5)
    rest = angle - turns * 1.5703125
    rest = rest - turns * 4.837512969970703125e-4
    rest = rest - turns * 7.54978995489188216e-8
    square = rest * rest
    sine = rest + rest * square * (
        -1.6666654611e-1 + square * (8.3321608736e-3 + square * -1.9515295891e-4)
    )
    cosine = (
        1.0
        - 0.5 * square
        + square
        * square
        * (4.166664568298827e-2 + square * (-1.388731625493765e-3 + square * 2.443315711809948e-5))
    )
    quarter = turns - 4.0 * jnp.floor(turns * 0.25)
    odd = (quarter == 1.0) | (quarter == 3.0)
    sine_sign = jnp.where(quarter >= 2.0, -1.0, 1.0)
    cosine_sign = jnp.where((quarter == 1.0) | (quarter == 2.0), -1.0, 1.0)
    return (
        jnp.where(odd, cosine, sine) * sine_sign,
        jnp.where(odd, sine, cosine) * cosine_sign,
    )


def parts_of(values):
    width = values.shape[1] // BLOCKS
    return [values[:, k * width : (k + 1) * width] for k in range(BLOCKS)]


def mix(sectioned, rows):
    return [
        sum(sectioned[a] * rows[4 * a + b : 4 * a + b + 1, :] for a in range(BLOCKS))
        for b in range(BLOCKS)
    ]


def unmix(upstream, rows):
    return [
        sum(upstream[b] * rows[4 * a + b : 4 * a + b + 1, :] for b in range(BLOCKS))
        for a in range(BLOCKS)
    ]


def mix_grad(sectioned, upstream):
    return jnp.concatenate(
        [
            jnp.sum(sectioned[a] * upstream[b], 0, keepdims=True)
            for a in range(BLOCKS)
            for b in range(BLOCKS)
        ],
        0,
    )


def lane_of(shape):
    return lax.broadcasted_iota(jnp.int32, shape, len(shape) - 1)


def row_of(shape):
    return lax.broadcasted_iota(jnp.int32, shape, 0)


def time_rows(block_ref, span):
    pieces, rows, _ = block_ref.shape
    return jnp.concatenate(
        [
            block_ref[n].astype(F32)[s * span : (s + 1) * span]
            for s in range(rows // span)
            for n in range(pieces)
        ],
        1,
    )


def later_lanes(values, steps, length):
    total = values.shape[1]
    moved = pltpu.roll(values, total - steps, 1)
    return jnp.where(lane_of(values.shape) % length < length - steps, moved, 0.0)


def earlier_lanes(values, steps, length):
    moved = pltpu.roll(values, steps, 1)
    return jnp.where(lane_of(values.shape) % length >= steps, moved, 0.0)


def to_blocks(lanes_now, out_ref, length):
    pieces, _, width = out_ref.shape
    seqs = lanes_now.shape[1] // length
    for n in range(pieces):
        out_ref[n] = jnp.concatenate(
            [
                lanes_now[:, s * length + n * width : s * length + (n + 1) * width]
                for s in range(seqs)
            ],
            0,
        ).astype(BF16)


def spectrum(block_ref, high_ref, low_ref):
    pieces, rows, width = block_ref.shape
    flat = block_ref[...].reshape(pieces * rows, width)
    out = mm(flat, high_ref[...]) + mm(flat, low_ref[...])
    return out.reshape(pieces, rows, 2 * width)


def nyquist_split(spec):
    half = spec.shape[-1] // 2
    real, imaginary = spec[..., :half], spec[..., half:]
    first = lane_of(real.shape) == 0
    return jnp.where(first, 0.0, imaginary), jnp.where(first, imaginary, real)


def norm_body(tok_ref, halo_ref, gains_ref, norm_ref, halo_out):
    gain = gains_ref[0:1, :]
    norm_ref[...] = (normalize_rows(tok_ref[...].astype(F32))[0] * gain).astype(BF16)
    halo_out[...] = (normalize_rows(halo_ref[...].astype(F32))[0] * gain).astype(BF16)


def filter_body(
    lift_ref, map_ref, read_ref, damp_ref, feat_ref, table_ref, s1, c1, s2, c2, spec_ref
):
    sine_one, cosine_one = sincos(mm(lift_ref[...], feat_ref[...], TN, HIGHEST))
    s1[...] = sine_one
    c1[...] = cosine_one
    sine_two, cosine_two = sincos(mm(map_ref[...], sine_one, TN, HIGHEST))
    s2[...] = sine_two
    c2[...] = cosine_two
    shape = (read_ref.shape[1], sine_two.shape[1])
    place = lane_of(shape).astype(F32)
    response = mm(read_ref[...], sine_two, TN, HIGHEST) * jnp.exp(-place * damp_ref[...])
    pieces, span, doubled = spec_ref.shape
    width = doubled // 2
    zero = jnp.zeros((span, width), F32)
    rows = []
    for k in range(pieces):
        now = response[:, k * width : (k + 1) * width]
        before = response[:, (k - 1) * width : k * width] if k else zero
        rows.append(
            jnp.concatenate([now, jnp.where(lane_of(before.shape) == 0, 0.0, before)], 1)
        )
    spec = mm(jnp.concatenate(rows, 0), table_ref[...], NN, HIGHEST)
    spec_ref[...] = spec.reshape(pieces, span, doubled)


def value_body(fast, *refs):
    if fast:
        me_ref, own_ref, other_ref, norm_ref, perm_ref, full_ref, out_ref, gather = refs
        rows = own_ref.shape[1]
        me = me_ref[0]
        for core, held in enumerate((own_ref, other_ref)):
            for r in range(held.shape[0]):
                distance = 2 * core + (0, 4, 1, 5)[r // 4] + 2 * ROUND_Z[r % 4]
                owner = jnp.bitwise_xor(me, distance)
                gather[pl.ds(pl.multiple_of(owner * rows, 8), rows), :] = held[r].astype(F32)
        full_ref[...] = gather[...].astype(BF16)
    else:
        inner_ref, norm_ref, perm_ref, full_ref, out_ref = refs
        full_ref[...] = inner_ref[...]
    width = full_ref.shape[1]
    norm = parts_of(norm_ref[...])
    first = [
        mm(norm[a], full_ref[a * width : (a + 1) * width, :]).astype(BF16) for a in range(BLOCKS)
    ]
    send_pieces(first, perm_ref, out_ref)


def send_pieces(parts, perm_ref, out_ref):
    pieces, rows, width = out_ref.shape
    seqs = parts[0].shape[0] // width
    span = rows // seqs
    turned = [
        sum(
            mm(perm_ref[k], parts[k][s * width : (s + 1) * width], NT) for k in range(BLOCKS)
        )
        for s in range(seqs)
    ]
    for n in range(pieces):
        out_ref[n] = jnp.concatenate(
            [turned[s][n * span : (n + 1) * span] for s in range(seqs)], 0
        ).astype(BF16)


def receive_pieces(in_ref, perm_ref):
    pieces, rows, width = in_ref.shape
    seqs = rows * pieces // (BLOCKS * perm_ref.shape[2])
    span = rows // seqs
    held = [in_ref[n].astype(F32) for n in range(pieces)]
    turned = [
        jnp.concatenate([h[s * span : (s + 1) * span] for h in held], 0).T.astype(BF16)
        for s in range(seqs)
    ]
    return [
        jnp.concatenate([mm(turned[s], perm_ref[k]) for s in range(seqs)], 0)
        for k in range(BLOCKS)
    ]


def earlier_rows(values, halo, steps):
    moved = pltpu.roll(values, steps, 0)
    row = row_of(values.shape)
    for k in range(steps):
        moved = jnp.where(row == k, halo[2 - steps + k : 3 - steps + k], moved)
    return moved


def later_rows(values, halo, steps):
    count = values.shape[0]
    moved = pltpu.roll(values, count - steps, 0)
    row = row_of(values.shape)
    for k in range(steps):
        moved = jnp.where(row == count - steps + k, halo[k : k + 1], moved)
    return moved


def per_sequence(function, values, halo, seqs, steps):
    count = values.shape[0] // seqs
    return jnp.concatenate(
        [
            function(values[s * count : (s + 1) * count], halo[2 * s : 2 * s + 2], steps)
            for s in range(seqs)
        ],
        0,
    )


def switch_body(seqs, norm_ref, halo_ref, full_ref, tw_ref, taps_ref, sect_ref, sw_ref, sh_ref, gate_ref):
    width = norm_ref.shape[1] // BLOCKS
    norm, halo = parts_of(norm_ref[...]), parts_of(halo_ref[...])
    inner = [full_ref[a * width : (a + 1) * width, :][:, :width] for a in range(BLOCKS)]
    first = [mm(norm[a], inner[a]) for a in range(BLOCKS)]
    for a in range(BLOCKS):
        sect_ref[a] = first[a]
    rows = tw_ref[...]
    switch = mix(first, rows)
    edge = mix([mm(halo[a], inner[a]) for a in range(BLOCKS)], rows)
    for b in range(BLOCKS):
        sw_ref[b] = switch[b].astype(BF16)
        sh_ref[b] = edge[b].astype(BF16)
        now = switch[b].astype(BF16).astype(F32)
        before = edge[b].astype(BF16).astype(F32)
        taps = taps_ref[b]
        gate_ref[b] = (
            taps[0:1] * now
            + taps[1:2] * per_sequence(earlier_rows, now, before, seqs, 1)
            + taps[2:3] * per_sequence(earlier_rows, now, before, seqs, 2)
        )


def convolve(spec_ref, b_ref, c_ref, x_ref, y_ref):
    pieces, rows, doubled = x_ref.shape
    span = spec_ref.shape[1]
    half = doubled // 2
    zero = jnp.zeros((span, half), F32)
    seqs = rows // span

    def outer(i, carry):
        def inner(j, totals):
            k = i - j
            a_now, b_now, c_now = spec_ref[k, :, :half], b_ref[k], c_ref[k]
            out = []
            for s in range(seqs):
                real = x_ref[j, s * span : (s + 1) * span, :half]
                imag = x_ref[j, s * span : (s + 1) * span, half:]
                out.append(totals[2 * s] + a_now * real - b_now * imag)
                out.append(totals[2 * s + 1] + b_now * real + c_now * imag)
            return tuple(out)

        totals = lax.fori_loop(0, i + 1, inner, (zero,) * (2 * seqs))
        for s in range(seqs):
            y_ref[i, s * span : (s + 1) * span, :half] = totals[2 * s]
            y_ref[i, s * span : (s + 1) * span, half:] = totals[2 * s + 1]
        return carry

    lax.fori_loop(0, pieces, outer, 0)


def correlate(spec_ref, b_ref, c_ref, g_ref, y_ref):
    pieces, rows, doubled = g_ref.shape
    span = spec_ref.shape[1]
    half = doubled // 2
    zero = jnp.zeros((span, half), F32)
    seqs = rows // span

    def outer(j, carry):
        def inner(i, totals):
            k = i - j
            a_now, b_now, c_now = spec_ref[k, :, :half], b_ref[k], c_ref[k]
            out = []
            for s in range(seqs):
                real = g_ref[i, s * span : (s + 1) * span, :half]
                imag = g_ref[i, s * span : (s + 1) * span, half:]
                out.append(totals[2 * s] + a_now * real + b_now * imag)
                out.append(totals[2 * s + 1] + c_now * imag - b_now * real)
            return tuple(out)

        totals = lax.fori_loop(j, pieces, inner, (zero,) * (2 * seqs))
        for s in range(seqs):
            y_ref[j, s * span : (s + 1) * span, :half] = totals[2 * s]
            y_ref[j, s * span : (s + 1) * span, half:] = totals[2 * s + 1]
        return carry

    lax.fori_loop(0, pieces, outer, 0)


def conv_body(
    length, sect_ref, mix_ref, taps_ref, spec_ref, high_ref, low_ref, back_ref,
    out_ref, cin_ref, signal_ref, x_ref, y_ref, b_ref, c_ref,
):
    span = spec_ref.shape[1]
    lanes_now = time_rows(sect_ref, span).astype(BF16)
    signal = mm(mix_ref[...], lanes_now).astype(BF16)
    signal_ref[...] = signal
    signal = signal.astype(F32)
    conv_in = (
        taps_ref[:, 0:1] * signal
        + taps_ref[:, 1:2] * earlier_lanes(signal, 1, length)
        + taps_ref[:, 2:3] * earlier_lanes(signal, 2, length)
    )
    to_blocks(conv_in, cin_ref, length)
    x_ref[...] = spectrum(cin_ref, high_ref, low_ref)
    b_ref[...], c_ref[...] = nyquist_split(spec_ref[...])
    convolve(spec_ref, b_ref, c_ref, x_ref, y_ref)
    pieces, rows, doubled = y_ref.shape
    out = mm(y_ref[...].reshape(pieces * rows, doubled), back_ref[...], NN, HIGHEST)
    out_ref[...] = out.astype(BF16).reshape(pieces, rows, doubled // 2)


def middle_body(
    seqs, long_ref, gate_ref, tok_ref, cot_ref, gains_ref, full_ref, tw_ref, sp_ref, sq_ref, perm_ref,
    layer_ref, lg_ref, swg_ref, res_ref, hid_ref, n2_ref, gated_ref, fgate_ref, fup_ref,
    fdown_ref, fmerge_ref, spg_ref, sqg_ref, twg_ref, gain_ref, fg, fu, act, ug, hg,
):
    rows, total = tok_ref.shape
    width = total // BLOCKS
    wide = fg.shape[2]
    base = 2 * wide
    gate = [gate_ref[b] for b in range(BLOCKS)]
    long_out = receive_pieces(long_ref, perm_ref)
    gated = [(gate[b] * long_out[b]).astype(BF16) for b in range(BLOCKS)]
    for b in range(BLOCKS):
        gated_ref[b] = gated[b]
    at = [slice(a * width, (a + 1) * width) for a in range(BLOCKS)]
    merge = [full_ref[at[a], 3 * wide :][:, width:] for a in range(BLOCKS)]
    sect_merge = [mm(gated[a], merge[a]) for a in range(BLOCKS)]
    merged = mix(sect_merge, tw_ref[...])
    tokens = parts_of(tok_ref[...].astype(F32))
    residual = [tokens[b] + merged[b] for b in range(BLOCKS)]
    mean = sum(jnp.sum(r, -1, keepdims=True) for r in residual) / total
    centred = [r - mean for r in residual]
    variance = sum(jnp.sum(c * c, -1, keepdims=True) for c in centred) / total
    factor = lax.rsqrt(variance + 1e-05)
    normed = [c * factor for c in centred]
    gain = parts_of(gains_ref[1:2, :])
    for a in range(BLOCKS):
        n2_now = (normed[a] * gain[a]).astype(BF16)
        n2_ref[a] = n2_now
        fg[a] = mm(n2_now, full_ref[at[a], :wide])
        fu[a] = mm(n2_now, full_ref[at[a], wide : 2 * wide])

    step = 16
    lanes = 128

    def forward_chunk(l, r):
        here = pl.ds(pl.multiple_of(l * lanes, lanes), lanes)
        down = pl.ds(pl.multiple_of(r * step, step), step)
        g_rows, u_rows = sp_ref[0, :, here], sp_ref[1, :, here]
        gate_pre = mix([fg[a, down, here] for a in range(BLOCKS)], g_rows)
        up_pre = mix([fu[a, down, here] for a in range(BLOCKS)], u_rows)
        for b in range(BLOCKS):
            v, u = gate_pre[b], up_pre[b]
            square = v * v
            bent = jnp.tanh(0.7978845608 * v * (1.0 + 0.044715 * square))
            half = 0.5 + 0.5 * bent
            active = v * half
            slope = half + 0.5 * v * (1.0 - bent * bent) * (
                0.7978845608 + (3 * 0.044715 * 0.7978845608) * square
            )
            hid_ref[b, down, here] = (active * u).astype(BF16)
            act[b, down, here] = active
            ug[b, down, here] = u * slope

    def forward_lane(l, carry):
        def forward_row(r, inner_carry):
            forward_chunk(l, r)
            return inner_carry

        return lax.fori_loop(0, rows // step, forward_row, carry)

    lax.fori_loop(0, wide // lanes, forward_lane, 0)

    shrink = []
    for a in range(BLOCKS):
        held = full_ref[at[a], base : base + wide]
        shrink.append(jnp.concatenate(parts_of(held), 0))
    sect_down = [mm(hid_ref[a], shrink[a]) for a in range(BLOCKS)]
    lowered = mix(sect_down, sq_ref[...])
    layer_ref[...] = jnp.concatenate(
        [(residual[b] + lowered[b]).astype(BF16) for b in range(BLOCKS)], 1
    )
    upstream = parts_of(cot_ref[...].astype(F32))
    sqg_ref[...] = mix_grad(sect_down, upstream)
    back_down = unmix(upstream, sq_ref[...])
    for a in range(BLOCKS):
        now = back_down[a].astype(BF16)
        fdown_ref[a] = now
        hg[a] = mm(now, shrink[a], NT)

    def backward_lane(l, carry):
        here = pl.ds(pl.multiple_of(l * lanes, lanes), lanes)
        g_rows, u_rows = sp_ref[0, :, here], sp_ref[1, :, here]

        def backward_row(r, sums):
            down = pl.ds(pl.multiple_of(r * step, step), step)
            hidden = [hg[b, down, here] for b in range(BLOCKS)]
            gate_grad = [hidden[b] * ug[b, down, here] for b in range(BLOCKS)]
            up_grad = [hidden[b] * act[b, down, here] for b in range(BLOCKS)]
            for a, value in enumerate(unmix(gate_grad, g_rows)):
                fgate_ref[a, down, here] = value.astype(BF16)
            for a, value in enumerate(unmix(up_grad, u_rows)):
                fup_ref[a, down, here] = value.astype(BF16)
            out = []
            for held, grads, start in ((fg, gate_grad, 0), (fu, up_grad, 16)):
                for a in range(BLOCKS):
                    value = held[a, down, here]
                    for b in range(BLOCKS):
                        product = value * grads[b]
                        out.append(sums[start + 4 * a + b] + product[:8] + product[8:])
            return tuple(out)

        zero = jnp.zeros((8, lanes), F32)
        sums = lax.fori_loop(0, rows // step, backward_row, (zero,) * 32)
        for k in range(32):
            spg_ref[k // 16, pl.ds(k % 16, 1), here] = jnp.sum(sums[k], 0, keepdims=True)
        return carry

    lax.fori_loop(0, wide // lanes, backward_lane, 0)

    n2_grad = [
        mm(fgate_ref[a], full_ref[at[a], :wide], NT)
        + mm(fup_ref[a], full_ref[at[a], wide : 2 * wide], NT)
        for a in range(BLOCKS)
    ]
    scaled = [n2_grad[a] * gain[a] for a in range(BLOCKS)]
    plain = sum(jnp.sum(v, -1, keepdims=True) for v in scaled) / total
    joint = sum(jnp.sum(scaled[a] * normed[a], -1, keepdims=True) for a in range(BLOCKS)) / total
    res_grad = [
        upstream[a] + factor * (scaled[a] - plain - normed[a] * joint) for a in range(BLOCKS)
    ]
    gain_ref[...] = jnp.concatenate(
        [jnp.sum(n2_grad[a] * normed[a], 0, keepdims=True) for a in range(BLOCKS)], 0
    )
    for a in range(BLOCKS):
        res_ref[a] = res_grad[a]
    twg_ref[...] = mix_grad(sect_merge, res_grad)
    back_merge = [v.astype(BF16) for v in unmix(res_grad, tw_ref[...])]
    long_grad = []
    for a in range(BLOCKS):
        fmerge_ref[a] = back_merge[a]
        gated_grad = mm(back_merge[a], merge[a], NT)
        long_grad.append((gated_grad * gate[a]).astype(BF16))
        swg_ref[a] = (gated_grad * long_out[a]).astype(BF16)
    send_pieces(long_grad, perm_ref, lg_ref)


def switch_back_body(
    seqs, swg_ref, next_ref, sw_ref, sh_ref, sect_ref, full_ref, tw_ref, taps_ref,
    n1_ref, fsw_ref, twg_ref, kg_ref,
):
    width = swg_ref.shape[2]
    back = []
    for b in range(BLOCKS):
        grad = swg_ref[b].astype(F32)
        after = next_ref[b].astype(F32)
        taps = taps_ref[b]
        back.append(
            taps[0:1] * grad
            + taps[1:2] * per_sequence(later_rows, grad, after, seqs, 1)
            + taps[2:3] * per_sequence(later_rows, grad, after, seqs, 2)
        )
        now, before = sw_ref[b].astype(F32), sh_ref[b].astype(F32)
        shifted = [now] + [per_sequence(earlier_rows, now, before, seqs, m) for m in (1, 2)]
        kg_ref[b] = jnp.concatenate(
            [jnp.sum(value * grad, 0, keepdims=True) for value in shifted], 0
        )
    twg_ref[...] = mix_grad([sect_ref[a] for a in range(BLOCKS)], back)
    first = unmix(back, tw_ref[...])
    for a in range(BLOCKS):
        now = first[a].astype(BF16)
        fsw_ref[a] = now
        n1_ref[a] = mm(now, full_ref[a * width : (a + 1) * width, :][:, :width], NT)


def weight_grad_body(
    fast, me_ref, n2_ref, fgate_ref, fup_ref, hid_ref, fdown_ref, gated_ref, fmerge_ref,
    norm_ref, fsw_ref, small_ref, *outs,
):
    norm = parts_of(norm_ref[...])
    count, rows, _ = small_ref.shape
    share = count // BLOCKS
    width = n2_ref.shape[2]
    for a in range(BLOCKS):
        shrink = mm(hid_ref[a], fdown_ref[a], TN)
        held = jnp.concatenate(
            [mm(n2_ref[a], fgate_ref[a], TN), mm(n2_ref[a], fup_ref[a], TN)]
            + [shrink[g * width : (g + 1) * width] for g in range(BLOCKS)]
            + [mm(norm[a], fsw_ref[a], TN), mm(gated_ref[a], fmerge_ref[a], TN)],
            1,
        )
        if not fast:
            outs[0][a * width : (a + 1) * width, :] = held
            continue
        half = outs[0].shape[2]
        for k in range(share):
            owner = a * share + k
            block = held[k * rows : (k + 1) * rows]
            apart = jnp.bitwise_xor(me_ref[0], owner)
            bits = [jnp.bitwise_and(lax.shift_right_logical(apart, n), 1) for n in range(5)]
            left = bits[1] * 16 + bits[0] * 8 + bits[2] * 4 + bits[3] * 2 + bits[4]
            right = bits[1] * 16 + bits[2] * 8 + bits[0] * 4 + bits[3] * 2 + bits[4]
            outs[0][left] = block[:, :half].astype(BF16)
            outs[1][right] = jnp.concatenate([block[:, half:], small_ref[owner]], 1).astype(BF16)


def conv_back_body(
    length, g_ref, mix_ref, taps_ref, spec_ref, high_ref, low_ref, back_ref,
    out_ref, cg_ref, sg_ref, x_ref, y_ref, b_ref, c_ref,
):
    span = spec_ref.shape[1]
    x_ref[...] = spectrum(g_ref, high_ref, low_ref)
    b_ref[...], c_ref[...] = nyquist_split(spec_ref[...])
    correlate(spec_ref, b_ref, c_ref, x_ref, y_ref)
    pieces, rows, doubled = y_ref.shape
    flat = mm(y_ref[...].reshape(pieces * rows, doubled), back_ref[...], NN, HIGHEST)
    flat = flat.astype(BF16).astype(F32)
    grad = jnp.concatenate(
        [
            flat[n * rows + s * span : n * rows + (s + 1) * span]
            for s in range(rows // span)
            for n in range(pieces)
        ],
        1,
    )
    cg_ref[...] = grad.astype(BF16)
    signal_grad = (
        taps_ref[:, 0:1] * grad
        + taps_ref[:, 1:2] * later_lanes(grad, 1, length)
        + taps_ref[:, 2:3] * later_lanes(grad, 2, length)
    )
    sg_ref[...] = signal_grad
    to_blocks(mm(mix_ref[...].astype(F32), signal_grad, TN, HIGHEST), out_ref, length)


def filter_back_body(
    length, g_ref, cin_ref, sect_ref, signal_ref, cg_ref, sg_ref, s1, c1, s2, c2, read_ref, map_ref,
    damp_ref, feat_ref, high_ref, low_ref, back_ref, same_ref, pick_ref,
    m_ref, q_ref, x_ref, b_ref, c_ref, gs_ref, p_ref,
):
    pieces, span, doubled = p_ref.shape
    half = doubled // 2
    x_ref[...] = spectrum(cin_ref, high_ref, low_ref)
    b_ref[...], c_ref[...] = nyquist_split(x_ref[...])
    gs_ref[...] = spectrum(g_ref, high_ref, low_ref)
    seqs = x_ref.shape[1] // span
    zero = jnp.zeros((span, half), F32)

    def outer(k, carry):
        def inner(j, totals):
            real, imag = totals
            for s in range(seqs):
                at = slice(s * span, (s + 1) * span)
                a_now, b_now, c_now = x_ref[j, at, :half], b_ref[j, at], c_ref[j, at]
                g_real, g_imag = gs_ref[j + k, at, :half], gs_ref[j + k, at, half:]
                real = real + a_now * g_real + b_now * g_imag
                imag = imag + c_now * g_imag - b_now * g_real
            return real, imag

        real, imag = lax.fori_loop(0, pieces - k, inner, (zero, zero))
        p_ref[k, :, :half] = real
        p_ref[k, :, half:] = imag
        return carry

    lax.fori_loop(0, pieces, outer, 0)
    flat = mm(p_ref[...].reshape(pieces * span, doubled), back_ref[...], NN, HIGHEST)
    chunks = []
    for k in range(pieces):
        now = flat[k * span : (k + 1) * span, :half]
        if k + 1 < pieces:
            after = flat[(k + 1) * span : (k + 2) * span, half:]
            now = now + jnp.where(lane_of(after.shape) == 0, 0.0, after)
        chunks.append(now)
    response_grad = jnp.concatenate(chunks, 1)
    place = lane_of(response_grad.shape).astype(F32)
    response_grad = response_grad * jnp.exp(-place * damp_ref[...])
    readout_grad = mm(response_grad, s2[...], NT, HIGHEST)
    pre_two = mm(read_ref[...], response_grad, NN, HIGHEST) * c2[...]
    order = s1.shape[0]
    m_ref[:order, :] = mm(s1[...], pre_two, NT, HIGHEST)
    pre_one = mm(map_ref[...], pre_two, NN, HIGHEST) * c1[...]
    m_ref[order:, :] = mm(feat_ref[...], pre_one, NT, HIGHEST)

    sect = time_rows(sect_ref, span)
    tw = mm(sect, sg_ref[...], NT, HIGHEST) * same_ref[...]
    tw = mm(pick_ref[...], tw, NN, HIGHEST)
    cg = cg_ref[...].astype(F32)
    signal = signal_ref[...].astype(F32)
    ones = jnp.ones((8, cg.shape[1]), F32)
    row = row_of(tw.shape)
    for m in range(3):
        moved = signal if m == 0 else earlier_lanes(signal, m, length)
        tw = jnp.where(row == BLOCKS + m, mm(ones, moved * cg, NT, HIGHEST), tw)
    q_ref[:span, :] = readout_grad
    q_ref[span:, :] = jnp.concatenate([tw, jnp.zeros((8, q_ref.shape[1] - span), F32)], 1)


def last_body(
    fast, fg_ref, perm_ref, inner_ref, norm_ref, n1_ref, res_ref, tok_ref, gains_ref, out_ref, *pay
):
    width = inner_ref.shape[1]
    first = [v.astype(BF16) for v in receive_pieces(fg_ref, perm_ref)]
    norm = parts_of(norm_ref[...])
    normed, factor = normalize_rows(tok_ref[...].astype(F32))
    normed = parts_of(normed)
    gain = parts_of(gains_ref[0:1, :])
    grads = [
        mm(first[a], inner_ref[a * width : (a + 1) * width, :], NT) + n1_ref[a]
        for a in range(BLOCKS)
    ]
    scaled = [grads[a] * gain[a] for a in range(BLOCKS)]
    total = width * BLOCKS
    plain = sum(jnp.sum(v, -1, keepdims=True) for v in scaled) / total
    joint = sum(jnp.sum(scaled[a] * normed[a], -1, keepdims=True) for a in range(BLOCKS)) / total
    out_ref[...] = jnp.concatenate(
        [res_ref[a] + factor * (scaled[a] - plain - normed[a] * joint) for a in range(BLOCKS)], 1
    )
    gain_grad = [jnp.sum(grads[a] * normed[a], 0, keepdims=True) for a in range(BLOCKS)]
    weight = [mm(norm[a], first[a], TN) for a in range(BLOCKS)]
    if not fast:
        for a in range(BLOCKS):
            pay[0][a * width : (a + 1) * width, :] = weight[a]
            pay[1][a : a + 1, :] = gain_grad[a]
        return
    count, rows, _ = pay[0].shape
    share = count // BLOCKS
    held = rows - 8
    tail = jnp.concatenate(gain_grad + [jnp.zeros((4, width), F32)], 0)
    for a in range(BLOCKS):
        for k in range(share):
            block = weight[a][k * held : (k + 1) * held]
            pay[0][a * share + k] = jnp.concatenate([block, tail], 0).astype(BF16)


def hop(values, distance):
    pieces = lax.axis_size("seq")
    return lax.ppermute(values, "seq", [(n, n ^ distance) for n in range(pieces)])


def hop_y(values):
    return lax.ppermute(values, "batch", [(0, 1), (1, 0)])


def hop_xy(values):
    return lax.ppermute(values, BOTH, [(n, n ^ 5) for n in range(2 * lax.axis_size("seq"))])


def per_device(
    tokens,
    cotangent,
    gains,
    mixing,
    twiddle,
    expand,
    spread,
    shrink,
    squeeze,
    kernel,
    lifting,
    phases,
    mapping,
    readout,
    damping,
):
    seqs, share, total = tokens.shape
    pieces, groups = lax.axis_size("seq"), lax.axis_size("batch")
    devices = pieces * groups
    place = lax.axis_index("seq")
    me = (place * groups + lax.axis_index("batch")).astype(jnp.int32).reshape(1)
    rows = seqs * share
    length = pieces * share
    width = total // BLOCKS
    wide = expand.shape[2]
    span = width // pieces
    chans = BLOCKS * span
    owned = mixing.shape[1]
    octet = devices // BLOCKS
    order = mapping.shape[0]
    fast = pieces == 16 and groups == 2 and owned % 8 == 0

    table, table_back = packed_tables(share)
    high, low = split_table(table[:share])
    perm = spread_matrix(pieces, span)
    feats = feature_rows(length)
    same = np.tile(np.eye(span, dtype=np.float32), (BLOCKS, BLOCKS))
    pick = np.zeros((8, chans), np.float32)
    for a in range(BLOCKS):
        pick[a, a * span : (a + 1) * span] = 1.0

    if fast:
        held = jnp.stack([mixing[0]] + [hop(mixing[0], d) for d in ROUND_Z[1:]])
        held = jnp.concatenate([held, hop(held, 2), hop_y(held), hop_xy(held)], 0)
        inner_parts = (held, hop(held, 1))
    else:
        inner_parts = (lax.all_gather(mixing[0], BOTH, axis=0, tiled=True),)
    expand_own = expand.reshape(2, owned, octet, BLOCKS, owned).swapaxes(2, 3)
    expand_own = expand_own.reshape(2, owned, wide)
    shrink_own = shrink.reshape(BLOCKS, owned, width).swapaxes(0, 1).reshape(owned, BLOCKS * width)
    packed = jnp.concatenate(
        [expand_own[0], expand_own[1], shrink_own, mixing[1], mixing[2]], 1
    )
    full = lax.all_gather(packed, BOTH, axis=0, tiled=True)
    pair = full[:, 3 * wide :]

    tok = tokens.reshape(rows, total)
    cot = cotangent.reshape(rows, total)
    halo = lax.ppermute(
        tokens[:, share - 2 :], "seq", [(n, n + 1) for n in range(pieces - 1)]
    ).reshape(2 * seqs, total)
    halo = jnp.pad(halo, ((0, 16 - 2 * seqs), (0, 0)))
    norm, norm_halo = call(norm_body, [((rows, total), BF16), ((16, total), BF16)], [tok, halo, gains])

    lift = jnp.concatenate([lifting, phases[None], jnp.zeros((2, order), F32)], 0)
    own_cols = jnp.concatenate([readout, damping[None], kernel[:, :total]], 0)
    own_cols = own_cols.reshape(order + 4, BLOCKS, pieces, span)
    own_cols = lax.dynamic_index_in_dim(own_cols, place, 2, False).reshape(order + 4, chans)
    read_own = own_cols[:order]
    turned = own_cols[order:].T
    damp_own, taps_own = turned[:, :1], turned[:, 1:]
    s1, c1, s2, c2, spec = call(
        filter_body,
        [((order, length), F32)] * 4 + [((pieces, chans, 2 * share), F32)],
        [lift, mapping, read_own, damp_own, feats, table],
        flops=5e9,
    )
    tw_rows = twiddle.astype(F32).transpose(0, 2, 3, 1).reshape(3, 16, width)
    sq_rows = squeeze.astype(F32).transpose(1, 2, 0).reshape(16, width)
    sp_rows = spread.astype(F32).reshape(2, octet, BLOCKS, owned, 16)
    sp_rows = sp_rows.transpose(0, 4, 2, 1, 3).reshape(2, 16, wide)
    tw_own = lax.dynamic_slice_in_dim(twiddle[0], place * span, span, 0)
    mix_own = jnp.einsum("jab,jk->bjak", tw_own, jnp.eye(span, dtype=BF16)).reshape(chans, chans)
    taps_sw = kernel[:, total:].reshape(3, BLOCKS, width).swapaxes(0, 1)

    blocks = (pieces, seqs * chans, share)
    inner, sect_out = call(
        functools.partial(value_body, fast),
        [((total, width), BF16), (blocks, BF16)],
        ([me] if fast else []) + list(inner_parts) + [norm, perm],
        scratch=[pltpu.VMEM((total, width), F32)] if fast else [],
        scalars=1 if fast else 0,
        flops=1e9,
    )
    sect_in = lax.all_to_all(sect_out, "seq", 0, 0, tiled=True)
    spectra = (pieces, seqs * chans, 2 * share)
    conv_scratch = [
        pltpu.VMEM(spectra, F32),
        pltpu.VMEM(spectra, F32),
        pltpu.VMEM((pieces, chans, share), F32),
        pltpu.VMEM((pieces, chans, share), F32),
    ]
    long_out, conv_in, signal = call(
        functools.partial(conv_body, length),
        [(blocks, BF16), (blocks, BF16), ((chans, seqs * length), BF16)],
        [sect_in, mix_own, taps_own, spec, high, low, table_back[:, :share]],
        scratch=conv_scratch,
        flops=3e9,
    )
    long_in = lax.all_to_all(long_out, "seq", 0, 0, tiled=True)

    quad = (BLOCKS, rows, width)
    sect_sw, switch, switch_edge, gate_seq = call(
        functools.partial(switch_body, seqs),
        [(quad, F32), (quad, BF16), ((BLOCKS, 16, width), BF16), (quad, F32)],
        [norm, norm_halo, pair, tw_rows[1], taps_sw],
        flops=2e9,
    )

    broad = (BLOCKS, rows, wide)
    (
        layer, lg_out, switch_grad, res_grad, hidden, norm_two, gated, fgate, fup, fdown, fmerge,
        spread_part, squeeze_part, merge_part, gain_part,
    ) = call(
        functools.partial(middle_body, seqs),
        [
            ((rows, total), BF16), (blocks, BF16), (quad, BF16), (quad, F32), (broad, BF16),
            (quad, BF16), (quad, BF16), (broad, BF16), (broad, BF16), (quad, BF16), (quad, BF16),
            ((2, 16, wide), F32), ((16, width), F32), ((16, width), F32), ((BLOCKS, width), F32),
        ],
        [long_in, gate_seq, tok, cot, gains, full, tw_rows[2], sp_rows, sq_rows, perm],
        scratch=[pltpu.VMEM(broad, F32)] * 5,
        limit=56,
        flops=2e10,
    )
    lg_in = lax.all_to_all(lg_out, "seq", 0, 0, tiled=True)

    first_rows = switch_grad.reshape(BLOCKS, seqs, share, width)[:, :, :2]
    after = lax.ppermute(first_rows, "seq", [(n + 1, n) for n in range(pieces - 1)])
    after = after.reshape(BLOCKS, 2 * seqs, width)
    n1_sw, fsw, switch_part, taps_part = call(
        functools.partial(switch_back_body, seqs),
        [(quad, F32), (quad, BF16), ((16, width), F32), ((BLOCKS, 3, width), F32)],
        [switch_grad, after, switch, switch_edge, sect_sw, pair, tw_rows[1], taps_sw],
        flops=2e9,
    )

    small_parts = (spread_part, squeeze_part, merge_part, switch_part, gain_part, taps_part)
    small_sizes = [p.size for p in small_parts]
    small = jnp.concatenate([p.reshape(-1) for p in small_parts])
    lot = 128 * devices
    each = -(-small.size // lot)
    packed_width = 3 * wide + 2 * width
    small = jnp.pad(small, (0, each * lot - small.size)).reshape(devices, each, 128)
    small_rows = jnp.pad(small, ((0, 0), (0, max(owned - each, 0)), (0, 0)))[:, :owned]
    if fast:
        half = (packed_width + 128) // 2
        grad_shapes = [((devices, owned, half), BF16)] * 2
    else:
        grad_shapes = [((total, packed_width), F32)]
    grads = call(
        functools.partial(weight_grad_body, fast),
        grad_shapes,
        [me, norm_two, fgate, fup, hidden, fdown, gated, fmerge, norm, fsw, small_rows],
        scalars=1,
        flops=1e10,
    )
    if fast:
        left, right = grads
        orders = ((1, 1), ("y", 2), (2, "y"), (4, 4), (8, 8))
        left, right = left.astype(BF16), right.astype(BF16)
        for k, (d_left, d_right) in enumerate(orders):
            n = left.shape[0] // 2
            kind = F32 if k == len(orders) - 1 else BF16
            pair_now = []
            for value, d in ((left, d_left), (right, d_right)):
                sent = hop_y(value[n:]) if d == "y" else hop(value[n:], d)
                pair_now.append((value[:n].astype(F32) + sent.astype(F32)).astype(kind))
            left, right = pair_now
        owner_grads = jnp.concatenate([left[0], right[0]], 1)
    else:
        owner_grads = lax.psum_scatter(grads[0], BOTH, scatter_dimension=0, tiled=True)

    fg_out, conv_grad, signal_grad = call(
        functools.partial(conv_back_body, length),
        [(blocks, BF16), ((chans, seqs * length), BF16), ((chans, seqs * length), F32)],
        [lg_in, mix_own, taps_own, spec, high, low, table_back[:, :share]],
        scratch=conv_scratch,
        flops=3e9,
    )
    fg_in = lax.all_to_all(fg_out, "seq", 0, 0, tiled=True)

    q_rows = chans + 8
    m_part, q_part = call(
        functools.partial(filter_back_body, length),
        [((order + 8, order), F32), ((q_rows, order), F32)],
        [
            lg_in, conv_in, sect_in, signal, conv_grad, signal_grad, s1, c1, s2, c2, read_own,
            mapping, damp_own, feats, high, low, table_back, same, pick,
        ],
        scratch=[
            pltpu.VMEM(spectra, F32),
            pltpu.VMEM(blocks, F32),
            pltpu.VMEM(blocks, F32),
            pltpu.VMEM(spectra, F32),
            pltpu.VMEM((pieces, chans, 2 * share), F32),
        ],
        flops=5e9,
    )

    if fast:
        last_shapes = [((devices, owned + 8, width), BF16)]
    else:
        last_shapes = [((total, width), F32), ((BLOCKS, width), F32)]
    tokens_grad, *pay = call(
        functools.partial(last_body, fast),
        [((rows, total), F32)] + last_shapes,
        [fg_in, perm, inner, norm, n1_sw, res_grad, tok, gains],
        flops=2e9,
    )
    if fast:
        value_sum = jnp.sum(lax.all_to_all(pay[0], BOTH, 0, 0, tiled=True).astype(F32), 0)
        value_grad, gain_one = value_sum[:owned], value_sum[owned : owned + BLOCKS]
    else:
        value_grad = lax.psum_scatter(pay[0], BOTH, scatter_dimension=0, tiled=True)
        gain_one = lax.psum(pay[1], BOTH)

    if fast:
        small_own = owner_grads[:each, packed_width:]
        m_rows, part_rows = order + 8, order + 8 + q_rows
        both = jnp.concatenate([m_part, q_part, small_own], 0)
        came = hop_y(both)
        both_mq = both[:part_rows] + came[:part_rows]
        m_sum = both_mq[:m_rows]
        rest = jnp.concatenate([both_mq[m_rows:], small_own, came[part_rows:]], 0)
        got = [hop(jnp.concatenate([m_sum, rest], 0), d) for d in ROUND_Z[1:]]
        m_sum = m_sum + sum(g[:m_rows] for g in got)
        rest = jnp.concatenate([rest] + [g[m_rows:] for g in got], 0)
        sent = jnp.concatenate([m_sum, rest], 0)
        got = [hop(sent, d) for d in ROUND_XC[1:]]
        m_sum = m_sum + sum(g[:m_rows] for g in got)
        rest = jnp.stack([rest] + [g[m_rows:] for g in got])
        rest = rest.reshape(pieces, -1, order)
        where_of = np.zeros(pieces, np.int32)
        for n, outer_d in enumerate(ROUND_XC):
            for k, inner_d in enumerate(ROUND_Z):
                where_of[outer_d ^ inner_d] = 4 * n + k
        index = jnp.asarray(where_of)[jnp.bitwise_xor(jnp.arange(pieces, dtype=jnp.int32), place)]
        rest = jnp.take(rest, index, axis=0)
        q_all = rest[:, :q_rows]
        small_pair = rest[:, q_rows:].reshape(pieces, 2, each, 128)
        mine = lax.axis_index("batch")
        small_pair = jnp.where(mine == 0, small_pair, small_pair[:, ::-1])
        small_all = small_pair.reshape(-1)
    else:
        m_sum = lax.psum(m_part, BOTH)
        q_all = lax.all_gather(lax.psum(q_part, "batch"), "seq", axis=0, tiled=False)
        small_all = lax.psum(small.reshape(-1), BOTH)
    taken, start = [], 0
    for part, size in zip(small_parts, small_sizes):
        taken.append(small_all[start : start + size].reshape(part.shape))
        start += size
    spread_sum, squeeze_sum, merge_sum, switch_sum, gain_two, taps_sum = taken
    spread_grad = spread_sum.reshape(2, 16, BLOCKS, octet, owned).transpose(0, 3, 2, 4, 1)
    spread_grad = spread_grad.reshape(2, wide, BLOCKS, BLOCKS)
    squeeze_grad = squeeze_sum.T.reshape(width, BLOCKS, BLOCKS)
    twiddle_value = q_all[:, chans : chans + BLOCKS, :chans].reshape(pieces, BLOCKS, BLOCKS, span)
    twiddle_value = twiddle_value.transpose(0, 3, 1, 2).reshape(width, BLOCKS, BLOCKS)
    twiddle_grad = jnp.stack(
        [twiddle_value]
        + [v.T.reshape(width, BLOCKS, BLOCKS) for v in (switch_sum, merge_sum)]
    )
    taps_value = q_all[:, chans + BLOCKS : chans + BLOCKS + 3, :chans]
    taps_value = taps_value.reshape(pieces, 3, BLOCKS, span).transpose(1, 2, 0, 3)
    kernel_grad = jnp.concatenate(
        [taps_value.reshape(3, total), taps_sum.swapaxes(0, 1).reshape(3, total)], 1
    )
    readout_grad = q_all[:, :chans].reshape(pieces, BLOCKS, span, order)
    readout_grad = readout_grad.transpose(3, 1, 0, 2).reshape(order, total)
    gains_grad = jnp.stack([gain_one.reshape(total), gain_two.reshape(total)])

    def natural(grad):
        return grad.reshape(owned, BLOCKS, octet, owned).swapaxes(1, 2).reshape(owned, wide)

    expand_grad = jnp.stack(
        [natural(owner_grads[:, :wide]), natural(owner_grads[:, wide : 2 * wide])]
    )
    shrink_grad = owner_grads[:, 2 * wide : 3 * wide].reshape(owned, BLOCKS, width)
    shrink_grad = shrink_grad.swapaxes(0, 1).reshape(BLOCKS * owned, width)
    mixing_grad = jnp.stack(
        [
            value_grad,
            owner_grads[:, 3 * wide : 3 * wide + width],
            owner_grads[:, 3 * wide + width : packed_width],
        ]
    )
    return (
        layer.reshape(seqs, share, total),
        tokens_grad.reshape(seqs, share, total),
        gains_grad,
        mixing_grad,
        twiddle_grad,
        expand_grad,
        spread_grad,
        shrink_grad,
        squeeze_grad,
        kernel_grad,
        m_sum[order : order + lifting.shape[0]],
        m_sum[order + lifting.shape[0]],
        m_sum[:order],
        readout_grad,
    )


def solution(mesh):
    return jax.shard_map(
        per_device,
        mesh=mesh,
        in_specs=(
            P("batch", "seq", None),
            P("batch", "seq", None),
            P(),
            P(None, ("seq", "batch"), None),
            P(),
            P(None, ("seq", "batch"), None),
            P(),
            P(("seq", "batch"), None),
            P(),
            P(),
            P(),
            P(),
            P(),
            P(),
            P(),
        ),
        out_specs=(
            P("batch", "seq", None),
            P("batch", "seq", None),
            P(),
            P(None, ("seq", "batch"), None),
            P(),
            P(None, ("seq", "batch"), None),
            P(),
            P(("seq", "batch"), None),
            P(),
            P(),
            P(),
            P(),
            P(),
            P(),
        ),
        check_vma=False,
    )
```

```python
import functools
import math

import jax
import jax.numpy as jnp
import numpy as np
from jax import lax
from jax.experimental import pallas as pl
from jax.experimental.pallas import tpu as pltpu
from jax.sharding import PartitionSpec as P

BLOCKS = 4
BOTH = ("seq", "batch")
F32 = jnp.float32
BF16 = jnp.bfloat16
HIGHEST = lax.Precision.HIGHEST
LIMIT = 60
NN = ((1,), (0,))
NT = ((1,), (1,))
TN = ((0,), (0,))


def mm(left, right, dims=NN, precision=None):
    return lax.dot_general(
        left, right, (dims, ((), ())), preferred_element_type=F32, precision=precision
    )


def call(body, outs, operands, micros, scratch=(), scalars=0, limit=LIMIT):
    specs = [
        pl.BlockSpec(memory_space=pltpu.SMEM if k < scalars else pltpu.VMEM)
        for k in range(len(operands))
    ]
    return pl.pallas_call(
        body,
        out_shape=[jax.ShapeDtypeStruct(shape, kind) for shape, kind in outs],
        in_specs=specs,
        out_specs=[pl.BlockSpec(memory_space=pltpu.VMEM) for _ in outs],
        scratch_shapes=list(scratch),
        compiler_params=pltpu.CompilerParams(vmem_limit_bytes=limit << 20),
        cost_estimate=pl.CostEstimate(
            flops=int(micros * 1.15e9), bytes_accessed=1 << 16, transcendentals=0
        ),
    )(*operands)


def packed_tables(points):
    size = 2 * points
    place = np.arange(size)[:, None].astype(np.int64)
    bins = np.arange(points)[None, :]
    angle = 2.0 * np.pi / size * ((place * bins) % size)
    forward = np.concatenate([np.cos(angle), -np.sin(angle)], 1)
    forward[:, points] = np.where(np.arange(size) % 2 == 0, 1.0, -1.0)
    weight = np.where(np.arange(size) % points == 0, 1.0, 2.0) / size
    backward = (forward * weight[None, :]).T
    return forward.astype(np.float32), np.ascontiguousarray(backward).astype(np.float32)


def split_table(table):
    high = table.astype(jnp.bfloat16)
    low = (table - high.astype(np.float32)).astype(jnp.bfloat16)
    return high, low


def feature_rows(length):
    place = np.arange(length)
    rows = [place / length]
    for harmonic in (1, 2):
        angle = 2.0 * np.pi / length * ((harmonic * place) % length)
        rows += [np.cos(angle), np.sin(angle)]
    rows += [np.ones(length), np.zeros(length), np.zeros(length)]
    return np.stack(rows).astype(np.float32)


def spread_matrix(pieces, span):
    width = pieces * span
    out = np.zeros((BLOCKS, pieces, BLOCKS, span, width), np.float32)
    for b in range(BLOCKS):
        for piece in range(pieces):
            for k in range(span):
                out[b, piece, b, k, piece * span + k] = 1.0
    return out.reshape(BLOCKS, pieces * BLOCKS * span, width).astype(jnp.bfloat16)


def normalize_rows(values):
    centred = values - jnp.mean(values, -1, keepdims=True)
    factor = lax.rsqrt(jnp.mean(centred * centred, -1, keepdims=True) + 1e-05)
    return centred * factor, factor


def sincos(angle):
    turns = jnp.floor(angle * (2.0 / math.pi) + 0.5)
    rest = angle - turns * 1.5703125
    rest = rest - turns * 4.837512969970703125e-4
    rest = rest - turns * 7.54978995489188216e-8
    square = rest * rest
    sine = rest + rest * square * (
        -1.6666654611e-1 + square * (8.3321608736e-3 + square * -1.9515295891e-4)
    )
    cosine = (
        1.0
        - 0.5 * square
        + square
        * square
        * (4.166664568298827e-2 + square * (-1.388731625493765e-3 + square * 2.443315711809948e-5))
    )
    quarter = turns - 4.0 * jnp.floor(turns * 0.25)
    odd = (quarter == 1.0) | (quarter == 3.0)
    sine_sign = jnp.where(quarter >= 2.0, -1.0, 1.0)
    cosine_sign = jnp.where((quarter == 1.0) | (quarter == 2.0), -1.0, 1.0)
    return (
        jnp.where(odd, cosine, sine) * sine_sign,
        jnp.where(odd, sine, cosine) * cosine_sign,
    )


def parts_of(values):
    width = values.shape[1] // BLOCKS
    return [values[:, k * width : (k + 1) * width] for k in range(BLOCKS)]


def mix(sectioned, rows):
    return [
        sum(sectioned[a] * rows[4 * a + b : 4 * a + b + 1, :] for a in range(BLOCKS))
        for b in range(BLOCKS)
    ]


def unmix(upstream, rows):
    return [
        sum(upstream[b] * rows[4 * a + b : 4 * a + b + 1, :] for b in range(BLOCKS))
        for a in range(BLOCKS)
    ]


def mix_grad(sectioned, upstream):
    return jnp.concatenate(
        [
            jnp.sum(sectioned[a] * upstream[b], 0, keepdims=True)
            for a in range(BLOCKS)
            for b in range(BLOCKS)
        ],
        0,
    )


def lane_of(shape):
    return lax.broadcasted_iota(jnp.int32, shape, len(shape) - 1)


def row_of(shape):
    return lax.broadcasted_iota(jnp.int32, shape, 0)


def time_rows(block_ref, span):
    pieces, rows, _ = block_ref.shape
    return jnp.concatenate(
        [
            block_ref[n].astype(F32)[s * span : (s + 1) * span]
            for s in range(rows // span)
            for n in range(pieces)
        ],
        1,
    )


def later_lanes(values, steps, length):
    total = values.shape[1]
    moved = pltpu.roll(values, total - steps, 1)
    return jnp.where(lane_of(values.shape) % length < length - steps, moved, 0.0)


def earlier_lanes(values, steps, length):
    moved = pltpu.roll(values, steps, 1)
    return jnp.where(lane_of(values.shape) % length >= steps, moved, 0.0)


def to_pieces(lanes_now, out_ref, length):
    pieces, _, width = out_ref.shape
    seqs = lanes_now.shape[1] // length
    for n in range(pieces):
        out_ref[n] = jnp.concatenate(
            [
                lanes_now[:, s * length + n * width : s * length + (n + 1) * width]
                for s in range(seqs)
            ],
            0,
        ).astype(BF16)


def spectrum(flat, high_ref, low_ref, out_ref):
    out = mm(flat, high_ref[...]) + mm(flat, low_ref[...])
    out_ref[...] = out.reshape(out_ref.shape)


def mm3(left, right, dims=NN):
    left_high, right_high = left.astype(BF16), right.astype(BF16)
    left_low = (left - left_high.astype(F32)).astype(BF16)
    right_low = (right - right_high.astype(F32)).astype(BF16)
    return (
        mm(left_high, right_low, dims) + mm(left_low, right_high, dims)
    ) + mm(left_high, right_high, dims)


def nyquist_split(spec):
    half = spec.shape[-1] // 2
    real, imaginary = spec[..., :half], spec[..., half:]
    first = lane_of(real.shape) == 0
    return jnp.where(first, 0.0, imaginary), jnp.where(first, imaginary, real)


def norm_body(tok_ref, gains_ref, norm_ref):
    norm = normalize_rows(tok_ref[...].astype(F32))[0] * gains_ref[0:1, :]
    norm_ref[...] = norm.astype(BF16)


def filter_body(
    lift_ref, map_ref, read_ref, damp_ref, feat_ref, table_ref, s1, c1, s2, c2, spec_ref
):
    sine_one, cosine_one = sincos(mm(lift_ref[...], feat_ref[...], TN, HIGHEST))
    s1[...] = sine_one
    c1[...] = cosine_one
    sine_two, cosine_two = sincos(mm(map_ref[...], sine_one, TN, HIGHEST))
    s2[...] = sine_two
    c2[...] = cosine_two
    shape = (read_ref.shape[1], sine_two.shape[1])
    place = lane_of(shape).astype(F32)
    response = mm(read_ref[...], sine_two, TN, HIGHEST) * jnp.exp(-place * damp_ref[...])
    pieces, span, doubled = spec_ref.shape
    width = doubled // 2
    zero = jnp.zeros((span, width), F32)
    rows = []
    for k in range(pieces):
        now = response[:, k * width : (k + 1) * width]
        before = response[:, (k - 1) * width : k * width] if k else zero
        rows.append(
            jnp.concatenate([now, jnp.where(lane_of(before.shape) == 0, 0.0, before)], 1)
        )
    spec = mm(jnp.concatenate(rows, 0), table_ref[...], NN, HIGHEST)
    spec_ref[...] = spec.reshape(pieces, span, doubled)


def value_body(packed, *refs):
    if packed:
        held_ref, norm_ref, perm_ref, full_ref, out_ref = refs
        rows = held_ref.shape[1] * 3 // 5
        share = held_ref.shape[0] // BLOCKS
        inner = []
        for a in range(BLOCKS):
            blocks = []
            for k in range(a * share, (a + 1) * share):
                held = held_ref[k].astype(F32)
                blocks.append(unpack_rows(held, rows))
            inner.append(jnp.concatenate(blocks, 0).astype(BF16))
            full_ref[a * rows * share : (a + 1) * rows * share, :] = inner[a]
    else:
        inner_ref, norm_ref, perm_ref, full_ref, out_ref = refs
        full_ref[...] = inner_ref[...]
        width = full_ref.shape[1]
        inner = [full_ref[a * width : (a + 1) * width, :] for a in range(BLOCKS)]
    norm = parts_of(norm_ref[...])
    first = [mm(norm[a], inner[a]).astype(BF16) for a in range(BLOCKS)]
    send_pieces(first, perm_ref, out_ref)


def pack_rows(values):
    rows = values.shape[0]
    rest = [values[k : k + 8, 128:] for k in range(0, rows, 8)] + [jnp.zeros_like(values[:8, 128:])]
    pairs = [jnp.concatenate(rest[k : k + 2], 1) for k in range(0, rows // 8, 2)]
    return jnp.concatenate([values[:, :128]] + pairs, 0)


def unpack_rows(held, rows):
    rest = []
    for k in range(rows // 8):
        start = rows + 8 * (k // 2)
        rest.append(held[start : start + 8, 64 * (k % 2) : 64 * (k % 2) + 64])
    return jnp.concatenate([held[:rows], jnp.concatenate(rest, 0)], 1)


def gather_body(
    me_ref, left_own, left_other, right_own, right_other, full_ref, pair_ref
):
    rows, cut = left_own.shape[1:]
    start = full_ref.shape[1] - pair_ref.shape[1]
    count = 2 * left_own.shape[0]
    per = 2 if rows % 16 else 1
    for k in range(0, count, per):
        blocks = []
        for owner in range(k, k + per):
            bits = apart_bits(me_ref, owner)
            deep = bits[3] + 2 * bits[4]
            left = bits[0] * 8 + bits[2] * 4 + deep
            right = bits[2] * 8 + bits[0] * 4 + deep
            near = bits[1] == 0
            blocks.append(
                jnp.concatenate(
                    [
                        jnp.where(near, left_own[left].astype(F32), left_other[left].astype(F32)),
                        jnp.where(
                            near, right_own[right].astype(F32), right_other[right].astype(F32)
                        ),
                    ],
                    1,
                )
            )
        block = jnp.concatenate(blocks, 0).astype(BF16)
        full_ref[k * rows : (k + per) * rows, :] = block
        pair_ref[k * rows : (k + per) * rows, :] = block[:, start:]


def send_pieces(parts, perm_ref, out_ref):
    pieces, rows, width = out_ref.shape
    seqs = parts[0].shape[0] // width
    span = rows // seqs
    turned = [
        sum(
            mm(perm_ref[k], parts[k][s * width : (s + 1) * width], NT) for k in range(BLOCKS)
        )
        for s in range(seqs)
    ]
    for n in range(pieces):
        out_ref[n] = jnp.concatenate(
            [turned[s][n * span : (n + 1) * span] for s in range(seqs)], 0
        ).astype(BF16)


def receive_pieces(in_ref, perm_ref):
    pieces, rows, width = in_ref.shape
    seqs = rows * pieces // (BLOCKS * perm_ref.shape[2])
    span = rows // seqs
    held = [in_ref[n].astype(F32) for n in range(pieces)]
    turned = [
        jnp.concatenate([h[s * span : (s + 1) * span] for h in held], 0).T.astype(BF16)
        for s in range(seqs)
    ]
    return [
        jnp.concatenate([mm(turned[s], perm_ref[k]) for s in range(seqs)], 0)
        for k in range(BLOCKS)
    ]


def earlier_rows(values, halo, steps):
    moved = pltpu.roll(values, steps, 0)
    row = row_of(values.shape)
    for k in range(steps):
        moved = jnp.where(row == k, halo[2 - steps + k : 3 - steps + k], moved)
    return moved


def later_rows(values, halo, steps):
    count = values.shape[0]
    moved = pltpu.roll(values, count - steps, 0)
    row = row_of(values.shape)
    for k in range(steps):
        moved = jnp.where(row == count - steps + k, halo[k : k + 1], moved)
    return moved


def per_sequence(function, values, halo, seqs, steps):
    count = values.shape[0] // seqs
    return jnp.concatenate(
        [
            function(values[s * count : (s + 1) * count], halo[2 * s : 2 * s + 2], steps)
            for s in range(seqs)
        ],
        0,
    )


def switch_body(
    seqs, norm_ref, halo_ref, gains_ref, full_ref, tw_ref, taps_ref, sect_ref, sw_ref, sh_ref, gate_ref
):
    width = norm_ref.shape[1] // BLOCKS
    edge_norm = normalize_rows(halo_ref[...].astype(F32))[0] * gains_ref[0:1, :]
    norm, halo = parts_of(norm_ref[...]), parts_of(edge_norm.astype(BF16))
    inner = [full_ref[a * width : (a + 1) * width, :][:, :width] for a in range(BLOCKS)]
    first = [mm(norm[a], inner[a]) for a in range(BLOCKS)]
    for a in range(BLOCKS):
        sect_ref[a] = first[a]
    rows = tw_ref[...]
    switch = mix(first, rows)
    edge = mix([mm(halo[a], inner[a]) for a in range(BLOCKS)], rows)
    for b in range(BLOCKS):
        sw_ref[b] = switch[b].astype(BF16)
        sh_ref[b] = edge[b].astype(BF16)
        now = switch[b].astype(BF16).astype(F32)
        before = edge[b].astype(BF16).astype(F32)
        taps = taps_ref[b]
        gate_ref[b] = (
            taps[0:1] * now
            + taps[1:2] * per_sequence(earlier_rows, now, before, seqs, 1)
            + taps[2:3] * per_sequence(earlier_rows, now, before, seqs, 2)
        )


def convolve(spec_ref, b_ref, c_ref, x_ref, y_ref):
    pieces, rows, doubled = x_ref.shape
    span = spec_ref.shape[1]
    half = doubled // 2
    zero = jnp.zeros((span, half), F32)
    seqs = rows // span

    def outer(i, carry):
        def inner(j, totals):
            k = i - j
            a_now, b_now, c_now = spec_ref[k, :, :half], b_ref[k], c_ref[k]
            out = []
            for s in range(seqs):
                real = x_ref[j, s * span : (s + 1) * span, :half]
                imag = x_ref[j, s * span : (s + 1) * span, half:]
                out.append(totals[2 * s] + a_now * real - b_now * imag)
                out.append(totals[2 * s + 1] + b_now * real + c_now * imag)
            return tuple(out)

        totals = lax.fori_loop(0, i + 1, inner, (zero,) * (2 * seqs))
        for s in range(seqs):
            y_ref[i, s * span : (s + 1) * span, :half] = totals[2 * s]
            y_ref[i, s * span : (s + 1) * span, half:] = totals[2 * s + 1]
        return carry

    lax.fori_loop(0, pieces, outer, 0)


def correlate(spec_ref, b_ref, c_ref, g_ref, y_ref):
    pieces, rows, doubled = g_ref.shape
    span = spec_ref.shape[1]
    half = doubled // 2
    zero = jnp.zeros((span, half), F32)
    seqs = rows // span

    def outer(j, carry):
        def inner(i, totals):
            k = i - j
            a_now, b_now, c_now = spec_ref[k, :, :half], b_ref[k], c_ref[k]
            out = []
            for s in range(seqs):
                real = g_ref[i, s * span : (s + 1) * span, :half]
                imag = g_ref[i, s * span : (s + 1) * span, half:]
                out.append(totals[2 * s] + a_now * real + b_now * imag)
                out.append(totals[2 * s + 1] + c_now * imag - b_now * real)
            return tuple(out)

        totals = lax.fori_loop(j, pieces, inner, (zero,) * (2 * seqs))
        for s in range(seqs):
            y_ref[j, s * span : (s + 1) * span, :half] = totals[2 * s]
            y_ref[j, s * span : (s + 1) * span, half:] = totals[2 * s + 1]
        return carry

    lax.fori_loop(0, pieces, outer, 0)


def conv_body(
    length, sect_ref, mix_ref, taps_ref, spec_ref, high_ref, low_ref, back_ref,
    out_ref, cin_ref, signal_ref, x_ref, y_ref, b_ref, c_ref,
):
    span = spec_ref.shape[1]
    lanes_now = time_rows(sect_ref, span).astype(BF16)
    signal = mm(mix_ref[...], lanes_now).astype(BF16)
    signal_ref[...] = signal
    signal = signal.astype(F32)
    conv_in = (
        taps_ref[:, 0:1] * signal
        + taps_ref[:, 1:2] * earlier_lanes(signal, 1, length)
        + taps_ref[:, 2:3] * earlier_lanes(signal, 2, length)
    )
    to_pieces(conv_in, cin_ref, length)
    spectrum(cin_ref[...].reshape(-1, cin_ref.shape[2]), high_ref, low_ref, x_ref)
    b_ref[...], c_ref[...] = nyquist_split(spec_ref[...])
    convolve(spec_ref, b_ref, c_ref, x_ref, y_ref)
    pieces, rows, doubled = y_ref.shape
    out = mm3(y_ref[...].reshape(pieces * rows, doubled), back_ref[...]).astype(BF16)
    out_ref[...] = out.reshape(out_ref.shape)


def middle_body(
    fast, seqs, me_ref, long_ref, gate_ref, tok_ref, cot_ref, gains_ref, full_ref, tw_ref, sp_ref, sq_ref,
    perm_ref, layer_ref, lg_ref, swg_ref, res_ref, spg_ref, sqg_ref, twg_ref, gain_ref, *refs,
):
    *weight_outs, fg, fu, act, ug, hg, hid_ref, fgate_ref, fup_ref = refs
    rows, total = tok_ref.shape
    width = total // BLOCKS
    wide = fg.shape[2]
    base = 2 * wide
    gate = [gate_ref[b] for b in range(BLOCKS)]
    long_out = receive_pieces(long_ref, perm_ref)
    gated = [(gate[b] * long_out[b]).astype(BF16) for b in range(BLOCKS)]
    at = [slice(a * width, (a + 1) * width) for a in range(BLOCKS)]
    merge = [full_ref[at[a], 3 * wide :][:, width:] for a in range(BLOCKS)]
    sect_merge = [mm(gated[a], merge[a]) for a in range(BLOCKS)]
    merged = mix(sect_merge, tw_ref[...])
    tokens = parts_of(tok_ref[...].astype(F32))
    residual = [tokens[b] + merged[b] for b in range(BLOCKS)]
    mean = sum(jnp.sum(r, -1, keepdims=True) for r in residual) / total
    centred = [r - mean for r in residual]
    variance = sum(jnp.sum(c * c, -1, keepdims=True) for c in centred) / total
    factor = lax.rsqrt(variance + 1e-05)
    normed = [c * factor for c in centred]
    gain = parts_of(gains_ref[1:2, :])
    norm_two = [(normed[a] * gain[a]).astype(BF16) for a in range(BLOCKS)]
    for a in range(BLOCKS):
        fg[a] = mm(norm_two[a], full_ref[at[a], :wide])
        fu[a] = mm(norm_two[a], full_ref[at[a], wide : 2 * wide])

    step = 16
    lanes = 128

    def forward_chunk(l, r):
        here = pl.ds(pl.multiple_of(l * lanes, lanes), lanes)
        down = pl.ds(pl.multiple_of(r * step, step), step)
        g_rows, u_rows = sp_ref[0, :, here], sp_ref[1, :, here]
        gate_pre = mix([fg[a, down, here] for a in range(BLOCKS)], g_rows)
        up_pre = mix([fu[a, down, here] for a in range(BLOCKS)], u_rows)
        for b in range(BLOCKS):
            v, u = gate_pre[b], up_pre[b]
            square = v * v
            bent = jnp.tanh(0.7978845608 * v * (1.0 + 0.044715 * square))
            half = 0.5 + 0.5 * bent
            active = v * half
            slope = half + 0.5 * v * (1.0 - bent * bent) * (
                0.7978845608 + (3 * 0.044715 * 0.7978845608) * square
            )
            hid_ref[b, down, here] = (active * u).astype(BF16)
            act[b, down, here] = active
            ug[b, down, here] = u * slope

    def forward_lane(l, carry):
        def forward_row(r, inner_carry):
            forward_chunk(l, r)
            return inner_carry

        return lax.fori_loop(0, rows // step, forward_row, carry)

    lax.fori_loop(0, wide // lanes, forward_lane, 0)

    shrink = []
    for a in range(BLOCKS):
        held = full_ref[at[a], base : base + wide]
        shrink.append(jnp.concatenate(parts_of(held), 0))
    sect_down = [mm(hid_ref[a], shrink[a]) for a in range(BLOCKS)]
    lowered = mix(sect_down, sq_ref[...])
    layer_ref[...] = jnp.concatenate(
        [(residual[b] + lowered[b]).astype(BF16) for b in range(BLOCKS)], 1
    )
    upstream = parts_of(cot_ref[...].astype(F32))
    sqg_ref[...] = mix_grad(sect_down, upstream)
    back_down = unmix(upstream, sq_ref[...])
    back_down = [v.astype(BF16) for v in back_down]
    for a in range(BLOCKS):
        hg[a] = mm(back_down[a], shrink[a], NT)

    def backward_lane(l, carry):
        here = pl.ds(pl.multiple_of(l * lanes, lanes), lanes)
        g_rows, u_rows = sp_ref[0, :, here], sp_ref[1, :, here]

        def backward_row(r, sums):
            down = pl.ds(pl.multiple_of(r * step, step), step)
            hidden = [hg[b, down, here] for b in range(BLOCKS)]
            gate_grad = [hidden[b] * ug[b, down, here] for b in range(BLOCKS)]
            up_grad = [hidden[b] * act[b, down, here] for b in range(BLOCKS)]
            for a, value in enumerate(unmix(gate_grad, g_rows)):
                fgate_ref[a, down, here] = value.astype(BF16)
            for a, value in enumerate(unmix(up_grad, u_rows)):
                fup_ref[a, down, here] = value.astype(BF16)
            out = []
            for held, grads, start in ((fg, gate_grad, 0), (fu, up_grad, 16)):
                for a in range(BLOCKS):
                    value = held[a, down, here]
                    for b in range(BLOCKS):
                        product = value * grads[b]
                        out.append(sums[start + 4 * a + b] + product[:8] + product[8:])
            return tuple(out)

        zero = jnp.zeros((8, lanes), F32)
        sums = lax.fori_loop(0, rows // step, backward_row, (zero,) * 32)
        for k in range(32):
            spg_ref[k // 16, pl.ds(k % 16, 1), here] = jnp.sum(sums[k], 0, keepdims=True)
        return carry

    lax.fori_loop(0, wide // lanes, backward_lane, 0)

    n2_grad = [
        mm(fgate_ref[a], full_ref[at[a], :wide], NT)
        + mm(fup_ref[a], full_ref[at[a], wide : 2 * wide], NT)
        for a in range(BLOCKS)
    ]
    scaled = [n2_grad[a] * gain[a] for a in range(BLOCKS)]
    plain = sum(jnp.sum(v, -1, keepdims=True) for v in scaled) / total
    joint = sum(jnp.sum(scaled[a] * normed[a], -1, keepdims=True) for a in range(BLOCKS)) / total
    res_grad = [
        upstream[a] + factor * (scaled[a] - plain - normed[a] * joint) for a in range(BLOCKS)
    ]
    gain_ref[...] = jnp.concatenate(
        [jnp.sum(n2_grad[a] * normed[a], 0, keepdims=True) for a in range(BLOCKS)], 0
    )
    for a in range(BLOCKS):
        res_ref[a] = res_grad[a]
    twg_ref[...] = mix_grad(sect_merge, res_grad)
    back_merge = [v.astype(BF16) for v in unmix(res_grad, tw_ref[...])]
    long_grad = []
    for a in range(BLOCKS):
        gated_grad = mm(back_merge[a], merge[a], NT)
        long_grad.append((gated_grad * gate[a]).astype(BF16))
        swg_ref[a] = (gated_grad * long_out[a]).astype(BF16)
    send_pieces(long_grad, perm_ref, lg_ref)

    for a in range(BLOCKS):
        from_hidden = mm(hid_ref[a], back_down[a], TN)
        held = jnp.concatenate(
            [mm(norm_two[a], fgate_ref[a], TN), mm(norm_two[a], fup_ref[a], TN)]
            + [from_hidden[g * width : (g + 1) * width] for g in range(BLOCKS)]
            + [mm(gated[a], back_merge[a], TN)],
            1,
        )
        put_blocks(fast, me_ref, weight_outs, a, held, 2 * wide)


def switch_back_body(
    fast, seqs, me_ref, swg_ref, next_ref, sw_ref, sh_ref, sect_ref, full_ref, tw_ref, taps_ref,
    norm_ref, spg_ref, sqg_ref, mg_ref, gain_ref, n1_ref, small_ref, *outs,
):
    width = swg_ref.shape[2]
    back, taps_grad = [], []
    for b in range(BLOCKS):
        grad = swg_ref[b].astype(F32)
        after = next_ref[b].astype(F32)
        taps = taps_ref[b]
        back.append(
            taps[0:1] * grad
            + taps[1:2] * per_sequence(later_rows, grad, after, seqs, 1)
            + taps[2:3] * per_sequence(later_rows, grad, after, seqs, 2)
        )
        now, before = sw_ref[b].astype(F32), sh_ref[b].astype(F32)
        shifted = [now] + [per_sequence(earlier_rows, now, before, seqs, m) for m in (1, 2)]
        taps_grad += [jnp.sum(value * grad, 0, keepdims=True) for value in shifted]
    tw_grad = mix_grad([sect_ref[a] for a in range(BLOCKS)], back)
    rest = [sqg_ref[...], mg_ref[...], tw_grad, jnp.concatenate([gain_ref[...]] + taps_grad, 0)]
    small = jnp.concatenate([spg_ref[0], spg_ref[1], jnp.concatenate(rest, 1)], 0)
    count = small_ref.shape[0]
    small_ref[...] = jnp.concatenate([small[:count], small[count:]], 1).astype(BF16)
    first = unmix(back, tw_ref[...])
    norm = parts_of(norm_ref[...])
    for a in range(BLOCKS):
        now = first[a].astype(BF16)
        n1_ref[a] = mm(now, full_ref[a * width : (a + 1) * width, :][:, :width], NT)
        put_blocks(fast, me_ref, outs, a, mm(norm[a], now, TN), 0)


def apart_bits(me_ref, owner):
    apart = jnp.bitwise_xor(me_ref[0], owner)
    return [jnp.bitwise_and(lax.shift_right_logical(apart, n), 1) for n in range(5)]


def put_blocks(fast, me_ref, outs, a, held, start):
    width = held.shape[0]
    if not fast:
        outs[0][a * width : (a + 1) * width, :] = held
        return
    keep_ref, send_ref = outs
    rows = keep_ref.shape[1]
    for k in range(width // rows):
        block = held[k * rows : (k + 1) * rows].astype(BF16)
        bits = apart_bits(me_ref, a * (width // rows) + k)
        deep = bits[3] * 2 + bits[4]
        for ref, core in ((keep_ref, 0), (send_ref, 1)):

            @pl.when(bits[1] == core)
            def _(ref=ref, block=block, bits=bits, deep=deep):
                if start:
                    ref[bits[0] * 8 + bits[2] * 4 + deep, :, :start] = block[:, :start]
                ref[bits[2] * 8 + bits[0] * 4 + deep, :, start:] = block[:, start:]


def conv_back_body(
    length, g_ref, mix_ref, taps_ref, spec_ref, high_ref, low_ref, back_ref,
    out_ref, cg_ref, sg_ref, x_ref, y_ref, b_ref, c_ref,
):
    span = spec_ref.shape[1]
    spectrum(g_ref[...].reshape(-1, g_ref.shape[2]), high_ref, low_ref, x_ref)
    b_ref[...], c_ref[...] = nyquist_split(spec_ref[...])
    correlate(spec_ref, b_ref, c_ref, x_ref, y_ref)
    pieces, rows, doubled = y_ref.shape
    flat = mm3(y_ref[...].reshape(pieces * rows, doubled), back_ref[...])
    flat = flat.astype(BF16).astype(F32)
    grad = jnp.concatenate(
        [
            flat[n * rows + s * span : n * rows + (s + 1) * span]
            for s in range(rows // span)
            for n in range(pieces)
        ],
        1,
    )
    cg_ref[...] = grad.astype(BF16)
    signal_grad = (
        taps_ref[:, 0:1] * grad
        + taps_ref[:, 1:2] * later_lanes(grad, 1, length)
        + taps_ref[:, 2:3] * later_lanes(grad, 2, length)
    )
    sg_ref[...] = signal_grad
    to_pieces(mm(mix_ref[...].astype(F32), signal_grad, TN, HIGHEST), out_ref, length)


def filter_back_body(
    length, g_ref, cin_ref, sect_ref, signal_ref, cg_ref, sg_ref, s1, c1, s2, c2, read_ref, map_ref,
    damp_ref, feat_ref, high_ref, low_ref, back_ref, same_ref, pick_ref,
    m_ref, q_ref, x_ref, b_ref, c_ref, gs_ref, p_ref,
):
    pieces, span, doubled = p_ref.shape
    half = doubled // 2
    spectrum(cin_ref[...].reshape(-1, half), high_ref, low_ref, x_ref)
    b_ref[...], c_ref[...] = nyquist_split(x_ref[...])
    spectrum(g_ref[...].reshape(-1, half), high_ref, low_ref, gs_ref)
    seqs = x_ref.shape[1] // span
    zero = jnp.zeros((span, half), F32)

    def outer(k, carry):
        def inner(j, totals):
            real, imag = totals
            for s in range(seqs):
                at = slice(s * span, (s + 1) * span)
                a_now, b_now, c_now = x_ref[j, at, :half], b_ref[j, at], c_ref[j, at]
                g_real, g_imag = gs_ref[j + k, at, :half], gs_ref[j + k, at, half:]
                real = real + a_now * g_real + b_now * g_imag
                imag = imag + c_now * g_imag - b_now * g_real
            return real, imag

        real, imag = lax.fori_loop(0, pieces - k, inner, (zero, zero))
        p_ref[k, :, :half] = real
        p_ref[k, :, half:] = imag
        return carry

    lax.fori_loop(0, pieces, outer, 0)
    flat = mm3(p_ref[...].reshape(pieces * span, doubled), back_ref[...])
    chunks = []
    for k in range(pieces):
        now = flat[k * span : (k + 1) * span, :half]
        if k + 1 < pieces:
            after = flat[(k + 1) * span : (k + 2) * span, half:]
            now = now + jnp.where(lane_of(after.shape) == 0, 0.0, after)
        chunks.append(now)
    response_grad = jnp.concatenate(chunks, 1)
    place = lane_of(response_grad.shape).astype(F32)
    response_grad = response_grad * jnp.exp(-place * damp_ref[...])
    readout_grad = mm3(response_grad, s2[...], NT)
    pre_two = mm3(read_ref[...], response_grad) * c2[...]
    order = s1.shape[0]
    m_ref[:order, :] = mm3(s1[...], pre_two, NT)
    pre_one = mm3(map_ref[...], pre_two) * c1[...]
    m_ref[order:, :] = mm3(feat_ref[...], pre_one, NT)

    sect = time_rows(sect_ref, span)
    tw = mm3(sect, sg_ref[...], NT) * same_ref[...]
    tw = mm(pick_ref[...], tw, NN, HIGHEST)
    cg = cg_ref[...].astype(F32)
    signal = signal_ref[...].astype(F32)
    ones = jnp.ones((8, cg.shape[1]), F32)
    row = row_of(tw.shape)
    for m in range(3):
        moved = signal if m == 0 else earlier_lanes(signal, m, length)
        tw = jnp.where(row == BLOCKS + m, mm3(ones, moved * cg, NT), tw)
    q_ref[:span, :] = readout_grad
    q_ref[span:, :] = jnp.concatenate([tw, jnp.zeros((8, q_ref.shape[1] - span), F32)], 1)


def last_body(
    fast, fg_ref, perm_ref, inner_ref, norm_ref, n1_ref, res_ref, tok_ref, gains_ref, out_ref, *pay
):
    width = inner_ref.shape[1]
    first = [v.astype(BF16) for v in receive_pieces(fg_ref, perm_ref)]
    norm = parts_of(norm_ref[...])
    normed, factor = normalize_rows(tok_ref[...].astype(F32))
    normed = parts_of(normed)
    gain = parts_of(gains_ref[0:1, :])
    grads = [
        mm(first[a], inner_ref[a * width : (a + 1) * width, :], NT) + n1_ref[a]
        for a in range(BLOCKS)
    ]
    scaled = [grads[a] * gain[a] for a in range(BLOCKS)]
    total = width * BLOCKS
    plain = sum(jnp.sum(v, -1, keepdims=True) for v in scaled) / total
    joint = sum(jnp.sum(scaled[a] * normed[a], -1, keepdims=True) for a in range(BLOCKS)) / total
    out_ref[...] = jnp.concatenate(
        [res_ref[a] + factor * (scaled[a] - plain - normed[a] * joint) for a in range(BLOCKS)], 1
    )
    gain_grad = [jnp.sum(grads[a] * normed[a], 0, keepdims=True) for a in range(BLOCKS)]
    weight = [mm(norm[a], first[a], TN) for a in range(BLOCKS)]
    if not fast:
        for a in range(BLOCKS):
            pay[0][a * width : (a + 1) * width, :] = weight[a]
            pay[1][a : a + 1, :] = gain_grad[a]
        return
    count, rows, _ = pay[0].shape
    share = count // BLOCKS
    held = (rows - 8) * 3 // 5
    flat = jnp.concatenate(gain_grad, 1)
    tail = [flat[:, k : k + 128] for k in range(0, total, 128)]
    tail = jnp.concatenate(tail + [jnp.zeros((8 - len(tail), 128), F32)], 0)
    for a in range(BLOCKS):
        for k in range(share):
            block = pack_rows(weight[a][k * held : (k + 1) * held])
            pay[0][a * share + k] = jnp.concatenate([block, tail], 0).astype(BF16)


def first_sum_body(
    keep_ref, got_ref, side_ref, side_got, small_ref, small_got, left_keep, left_send, right_keep, right_send
):
    n, _, cut = left_keep.shape
    n -= 1
    for k in range(2 * n):
        main = keep_ref[k].astype(F32) + got_ref[k].astype(F32)
        side = side_ref[k].astype(F32) + side_got[k].astype(F32)
        right = jnp.concatenate([main[:, cut:], side], 1).astype(BF16)
        left_out, right_out = (left_keep, right_keep) if k < n else (left_send, right_send)
        left_out[k % n] = main[:, :cut].astype(BF16)
        right_out[k % n] = right
    small = (small_ref[...].astype(F32) + small_got[...].astype(F32)).astype(BF16)
    left_keep[n] = small
    left_send[n] = small


def second_sum_body(
    left_ref, left_got, right_ref, right_got, left_keep, left_send, right_keep, right_send
):
    n = right_keep.shape[0]
    for k in range(2 * n):
        left = (left_ref[k].astype(F32) + left_got[k].astype(F32)).astype(BF16)
        right = (right_ref[k].astype(F32) + right_got[k].astype(F32)).astype(BF16)
        left_out, right_out = (left_keep, right_keep) if k < n else (left_send, right_send)
        left_out[k % n] = left
        right_out[k % n] = right
    small = (left_ref[2 * n].astype(F32) + left_got[2 * n].astype(F32)).astype(BF16)
    left_keep[n] = small
    left_send[n] = small


def third_sum_body(left_ref, left_got, right_ref, right_got, *outs):
    left = [(left_ref[k].astype(F32) + left_got[k].astype(F32)).astype(BF16) for k in range(5)]
    right = [(right_ref[k].astype(F32) + right_got[k].astype(F32)).astype(BF16) for k in range(4)]
    for k, out_ref in enumerate(outs):
        out_ref[...] = jnp.concatenate([left[k], right[k], left[4]], 1)


def natural_order(values, owned):
    octet = values.shape[1] // (BLOCKS * owned)
    return jnp.concatenate(
        [
            values[:, (g * octet + o) * owned : (g * octet + o + 1) * owned]
            for o in range(octet)
            for g in range(BLOCKS)
        ],
        1,
    )


def weights_out_body(
    own_ref, one_ref, two_ref, three_ref, expand_ref, spread_ref, shrink_ref, mix_ref, rest_ref
):
    parts = [ref[...].astype(F32) for ref in (own_ref, one_ref, two_ref, three_ref)]
    held = (parts[0] + parts[1]) + (parts[2] + parts[3])
    owned, wide = expand_ref.shape[1:]
    width = mix_ref.shape[2]
    for k in range(2):
        expand_ref[k] = natural_order(held[:, k * wide : (k + 1) * wide], owned)
        start = 2 * wide + BLOCKS * width + k * width
        mix_ref[1 - k] = held[:, start : start + width]
    for g in range(BLOCKS):
        start = 2 * wide + g * width
        shrink_ref[g * owned : (g + 1) * owned, :] = held[:, start : start + width]
    start = 3 * wide + 2 * width
    small = jnp.concatenate([held[:, start : start + wide], held[:, start + wide :]], 0)
    for k in range(2):
        spread_ref[k] = natural_order(small[16 * k : 16 * k + 16], owned)
    for k in range(BLOCKS):
        rest_ref[k] = small[32:, k * width : (k + 1) * width]


def small_out_body(
    place_ref, own_ref, one_ref, two_ref, three_ref, value_ref, mix_ref, rest_ref, perm_ref,
    gains_ref, mixing_ref, twiddle_ref, kernel_ref, lift_ref, phase_ref, map_ref, read_ref, q_ref,
):
    order = map_ref.shape[0]
    m_rows, q_rows = order + 8, q_ref.shape[1]
    chans = q_rows - 8
    pieces = q_ref.shape[0]
    width = perm_ref.shape[2]
    parts = [ref[...] for ref in (own_ref, one_ref, two_ref, three_ref)]
    sums = [part[:m_rows].astype(F32) for part in parts]
    m_sum = (sums[0] + sums[1]) + (sums[2] + sums[3])
    map_ref[...] = m_sum[:order]
    lift_ref[...] = m_sum[order : order + lift_ref.shape[0]]
    phase_ref[...] = m_sum[order + lift_ref.shape[0] : order + lift_ref.shape[0] + 1]
    for k, outer in enumerate((0, 2, 1, 3)):
        for n, inner in enumerate((0, 4, 8, 12)):
            start = m_rows + n * q_rows
            q_ref[jnp.bitwise_xor(place_ref[0], outer ^ inner)] = parts[k][
                start : start + q_rows
            ].astype(F32)
    tall = jnp.concatenate([q_ref[n, :chans] for n in range(pieces)], 0).astype(BF16)
    broad = jnp.concatenate([q_ref[n, chans:, :chans] for n in range(pieces)], 1).astype(BF16)
    rest = [mm(broad, perm_ref[b]) for b in range(BLOCKS)]
    read_ref[...] = jnp.concatenate([mm(tall, perm_ref[b], TN) for b in range(BLOCKS)], 1)
    for a in range(BLOCKS):
        for b in range(BLOCKS):
            twiddle_ref[0, 4 * a + b : 4 * a + b + 1, :] = rest[b][a : a + 1]
    twiddle_ref[1] = rest_ref[2]
    twiddle_ref[2] = rest_ref[1]
    last = rest_ref[3]
    taps = [rest[b][BLOCKS : BLOCKS + 3] for b in range(BLOCKS)]
    taps += [last[BLOCKS + 3 * b : BLOCKS + 3 * b + 3] for b in range(BLOCKS)]
    kernel_ref[...] = jnp.concatenate(taps, 1)
    total = value_ref[0].astype(F32)
    for n in range(1, value_ref.shape[0]):
        total = total + value_ref[n].astype(F32)
    owned = mix_ref.shape[1]
    held = owned * 5 // 3
    mixing_ref[0] = unpack_rows(total, owned)
    mixing_ref[1] = mix_ref[0]
    mixing_ref[2] = mix_ref[1]
    one = jnp.concatenate([total[held + k : held + k + 1] for k in range(6)], 1)
    two = jnp.concatenate([last[a : a + 1] for a in range(BLOCKS)], 1)
    gains_ref[...] = jnp.concatenate([one, two], 0)


def hop(values, distance):
    pieces = lax.axis_size("seq")
    return lax.ppermute(values, "seq", [(n, n ^ distance) for n in range(pieces)])


def hop_y(values, distance=0):
    if not distance:
        return lax.ppermute(values, "batch", [(0, 1), (1, 0)])
    apart = 2 * distance + 1
    return lax.ppermute(values, BOTH, [(n, n ^ apart) for n in range(2 * lax.axis_size("seq"))])


def pair_sum(parts, kind):
    wide = [v.astype(F32) for v in parts]
    return ((wide[0] + wide[1]) + (wide[2] + wide[3])).astype(kind)


def held_until(values, *others):
    return lax.optimization_barrier((values, *others))[0]


def added(kept, came, at, kind):
    return (kept[at].astype(F32) + came[at].astype(F32)).astype(kind)


def per_device(
    tokens,
    cotangent,
    gains,
    mixing,
    twiddle,
    expand,
    spread,
    shrink,
    squeeze,
    kernel,
    lifting,
    phases,
    mapping,
    readout,
    damping,
):
    seqs, share, total = tokens.shape
    pieces, groups = lax.axis_size("seq"), lax.axis_size("batch")
    devices = pieces * groups
    place = lax.axis_index("seq")
    me = (place * groups + lax.axis_index("batch")).astype(jnp.int32).reshape(1)
    rows = seqs * share
    length = pieces * share
    width = total // BLOCKS
    wide = expand.shape[2]
    owned = mixing.shape[1]
    octet = devices // BLOCKS
    order = mapping.shape[0]
    fast = pieces == 16 and groups == 2 and owned % 8 == 0 and seqs == 2
    span = width // pieces
    chans = BLOCKS * span
    def exchange(values):
        return lax.all_to_all(values, "seq", 0, 0, tiled=True)

    table, table_back = packed_tables(share)
    high, low = split_table(table[:share])
    perm = spread_matrix(pieces, span)
    feats = feature_rows(length)
    same = np.tile(np.eye(span, dtype=np.float32), (BLOCKS, BLOCKS))
    pick = np.zeros((8, chans), np.float32)
    for a in range(BLOCKS):
        pick[a, a * span : (a + 1) * span] = 1.0

    if fast:
        own = pack_rows(mixing[0])
        own = jnp.broadcast_to(own[None], (devices,) + own.shape)
        inner_part = lax.all_to_all(own, BOTH, 0, 0, tiled=True)
    else:
        inner_part = lax.all_gather(mixing[0], BOTH, axis=0, tiled=True)
    expand_own = expand.reshape(2, owned, octet, BLOCKS, owned).swapaxes(2, 3)
    expand_own = expand_own.reshape(2, owned, wide)
    shrink_own = shrink.reshape(BLOCKS, owned, width).swapaxes(0, 1).reshape(owned, BLOCKS * width)
    packed = jnp.concatenate(
        [expand_own[0], expand_own[1], shrink_own, mixing[1], mixing[2]], 1
    )
    if fast:
        packed = held_until(packed, own)
        z_got = [hop(packed, d) for d in (4, 8, 12)]
    else:
        full = lax.all_gather(packed, BOTH, axis=0, tiled=True)
        pair = full[:, 3 * wide :]

    tok = tokens.reshape(rows, total)
    cot = cotangent.reshape(rows, total)
    ahead = [(n, n + 1) for n in range(pieces - 1)]
    halo = lax.ppermute(tokens[:, share - 2 :], "seq", ahead)
    halo = jnp.pad(halo.reshape(2 * seqs, total), ((0, 16 - 2 * seqs), (0, 0)))
    (norm,) = call(norm_body, [((rows, total), BF16)], [tok, gains], 1)

    lift = jnp.concatenate([lifting, phases[None], jnp.zeros((2, order), F32)], 0)
    own_cols = jnp.concatenate([readout, damping[None], kernel[:, :total]], 0)
    own_cols = own_cols.reshape(order + 4, BLOCKS, pieces, span)
    own_cols = lax.dynamic_index_in_dim(own_cols, place, 2, False).reshape(order + 4, chans)
    read_own = own_cols[:order]
    turned = own_cols[order:].T
    damp_own, taps_own = turned[:, :1], turned[:, 1:]
    tw_rows = twiddle.astype(F32).transpose(0, 2, 3, 1).reshape(3, 16, width)
    sq_rows = squeeze.astype(F32).transpose(1, 2, 0).reshape(16, width)
    sp_rows = spread.astype(F32).reshape(2, octet, BLOCKS, owned, 16)
    sp_rows = sp_rows.transpose(0, 4, 2, 1, 3).reshape(2, 16, wide)
    tw_own = lax.dynamic_slice_in_dim(twiddle[0], place * span, span, 0)
    mix_own = jnp.einsum("jab,jk->bjak", tw_own, jnp.eye(span, dtype=BF16)).reshape(chans, chans)
    taps_sw = kernel[:, total:].reshape(3, BLOCKS, width).swapaxes(0, 1)

    if fast:
        inner_part, (tw_rows, sq_rows, sp_rows, mix_own, taps_sw, taps_own, read_own, lift) = (
            lax.optimization_barrier(
                (inner_part, (tw_rows, sq_rows, sp_rows, mix_own, taps_sw, taps_own, read_own, lift))
            )
        )

    blocks = (pieces, seqs * chans, share)
    inner, sect_out = call(
        functools.partial(value_body, fast),
        [((total, width), BF16), (blocks, BF16)],
        [inner_part, norm, perm],
        2,
    )
    sect_in = exchange(sect_out)
    if fast:
        held = jnp.stack([packed] + held_until(z_got, sect_out))
        left, right = held[:, :, :1408], held[:, :, 1408:]
        lift = held_until(lift, left, right)
    s1, c1, s2, c2, spec = call(
        filter_body,
        [((order, length), F32)] * 4 + [((pieces, chans, 2 * share), F32)],
        [lift, mapping, read_own, damp_own, feats, table],
        5,
    )
    if fast:
        got = held_until((hop(left, 2), hop_y(right)), spec)
        left, right = jnp.concatenate([left, got[0]], 0), jnp.concatenate([right, got[1]], 0)
        sect_in = held_until(sect_in, left, right)
    spectra = (pieces, seqs * chans, 2 * share)
    conv_scratch = [
        pltpu.VMEM(spectra, F32),
        pltpu.VMEM(spectra, F32),
        pltpu.VMEM((pieces, chans, share), F32),
        pltpu.VMEM((pieces, chans, share), F32),
    ]
    long_out, conv_in, signal = call(
        functools.partial(conv_body, length),
        [(blocks, BF16), (blocks, BF16), ((chans, seqs * length), BF16)],
        [sect_in, mix_own, taps_own, spec, high, low, table_back[:, :share]],
        7,
        scratch=conv_scratch,
    )
    long_in = exchange(long_out)
    if fast:
        got = held_until((hop_y(left), hop(right, 2)), long_out)
        left, right = jnp.concatenate([left, got[0]], 0), jnp.concatenate([right, got[1]], 0)
        full, pair = call(
            gather_body,
            [((total, 3 * wide + 2 * width), BF16), ((total, 2 * width), BF16)],
            [me, left, hop(left, 1), right, hop(right, 1)],
            5,
            scalars=1,
        )

    quad = (BLOCKS, rows, width)
    sect_sw, switch, switch_edge, gate_seq = call(
        functools.partial(switch_body, seqs),
        [(quad, F32), (quad, BF16), ((BLOCKS, 16, width), BF16), (quad, F32)],
        [norm, halo, gains, pair, tw_rows[1], taps_sw],
        1,
    )

    broad = (BLOCKS, rows, wide)
    if fast:
        half_devices = devices // 2
        weight_shapes = [((half_devices, owned, 3 * wide + width), BF16)] * 2
        side_shapes = [((half_devices, owned, width), BF16)] * 2
    else:
        weight_shapes = [((total, 3 * wide + width), F32)]
        side_shapes = [((total, width), F32)]
    (
        layer, lg_out, switch_grad, res_grad, spread_part, squeeze_part, merge_part, gain_part, *main
    ) = call(
        functools.partial(middle_body, fast, seqs),
        [
            ((rows, total), BF16), (blocks, BF16), (quad, BF16), (quad, F32),
            ((2, 16, wide), F32), ((16, width), F32), ((16, width), F32), ((BLOCKS, width), F32),
        ] + weight_shapes,
        [me, long_in, gate_seq, tok, cot, gains, full, tw_rows[2], sp_rows, sq_rows, perm],
        27,
        scratch=[pltpu.VMEM(broad, F32)] * 5 + [pltpu.VMEM(broad, BF16)] * 3,
        scalars=1,
    )
    lg_in = exchange(lg_out)

    first_rows = switch_grad.reshape(BLOCKS, seqs, share, width)[:, :, :2]
    after = lax.ppermute(first_rows, "seq", [(to, at) for at, to in ahead])
    after = after.reshape(BLOCKS, 2 * seqs, width)
    n1_sw, small, *side = call(
        functools.partial(switch_back_body, fast, seqs),
        [(quad, F32), ((24, 2 * wide), BF16)] + side_shapes,
        [me, switch_grad, after, switch, switch_edge, sect_sw, pair, tw_rows[1], taps_sw, norm,
         spread_part, squeeze_part, merge_part, gain_part],
        5,
        scalars=1,
    )
    if fast:
        got, side_got, small_got = hop(main[1], 1), hop(side[1], 1), hop(small, 1)
        def sum_shapes(n):
            left, right = ((n + 1, owned, 2 * wide), BF16), ((n, owned, wide + 2 * width), BF16)
            return [left, left, right, right]

        left, left_send, right, right_send = call(
            first_sum_body,
            sum_shapes(half_devices // 2),
            [main[0], got, side[0], side_got, small, small_got],
            4,
        )
        lg_in = held_until(lg_in, left, left_send, right, right_send)

    fg_out, conv_grad, signal_grad = call(
        functools.partial(conv_back_body, length),
        [(blocks, BF16), ((chans, seqs * length), BF16), ((chans, seqs * length), F32)],
        [lg_in, mix_own, taps_own, spec, high, low, table_back[:, :share]],
        8,
        scratch=conv_scratch,
    )
    fg_in = exchange(fg_out)

    if fast:
        got = held_until((hop_y(left_send), hop(right_send, 2)), fg_out)
        left, left_send, right, right_send = call(
            second_sum_body, sum_shapes(half_devices // 4), [left, got[0], right, got[1]], 3
        )
        lg_in = held_until(lg_in, left, left_send, right, right_send)

    q_rows = chans + 8
    m_part, q_part = call(
        functools.partial(filter_back_body, length),
        [((order + 8, order), F32), ((q_rows, order), F32)],
        [
            lg_in, conv_in, sect_in, signal, conv_grad, signal_grad, s1, c1, s2, c2, read_own,
            mapping, damp_own, feats, high, low, table_back, same, pick,
        ],
        14,
        scratch=[
            pltpu.VMEM(spectra, F32),
            pltpu.VMEM(blocks, F32),
            pltpu.VMEM(blocks, F32),
            pltpu.VMEM(spectra, F32),
            pltpu.VMEM((pieces, chans, 2 * share), F32),
        ],
    )

    if fast:
        got = held_until((hop(left_send, 2), hop_y(right_send)), m_part)
        shape = ((owned, 5 * wide + 2 * width), BF16)
        own, *sends = call(third_sum_body, [shape] * 4, [left, got[0], right, got[1]], 2)
        z_got = [hop(sent, d) for sent, d in zip(sends, (8, 4, 12))]
        fg_in = held_until(fg_in, own, sends)

    if fast:
        last_shapes = [((devices, owned * 5 // 3 + 8, 128), BF16)]
    else:
        last_shapes = [((total, width), F32), ((BLOCKS, width), F32)]
    tokens_grad, *pay = call(
        functools.partial(last_body, fast),
        [((rows, total), F32)] + last_shapes,
        [fg_in, perm, inner, norm, n1_sw, res_grad, tok, gains],
        3,
    )
    if fast:
        value_parts = lax.all_to_all(pay[0], BOTH, 0, 0, tiled=True)
    else:
        value_grad = lax.psum_scatter(pay[0], BOTH, scatter_dimension=0, tiled=True)
        gain_one = lax.psum(pay[1], BOTH)

    if fast:
        m_rows = order + 8
        both = jnp.concatenate([m_part, q_part], 0).astype(BF16)
        both = held_until(both, fg_in)
        both = added(both, held_until(hop_y(both), tokens_grad), slice(0, None), BF16)
        got = [both] + held_until([hop(both, d) for d in (4, 8, 12)], z_got)
        m_sum = pair_sum([g[:m_rows] for g in got], BF16)
        both = jnp.concatenate([m_sum] + [g[m_rows:] for g in got], 0)
        z_shapes = [((2, owned, wide), F32), ((2, 16, wide), F32), ((BLOCKS * owned, width), F32)]
        z_shapes += [((2, owned, width), F32), ((BLOCKS, 16, width), F32)]
        expand_grad, spread_sum, shrink_grad, mix_sum, rest_sum = call(
            weights_out_body, z_shapes, [own, *z_got], 4
        )
        got = [both] + held_until([hop(both, d) for d in (2, 1, 3)], rest_sum)
        out_shapes = [(2, total), (3, owned, width), (3, 16, width), (3, 2 * total)]
        out_shapes += [lifting.shape, (1, order), mapping.shape, readout.shape]
        (
            gains_grad, mixing_grad, twiddle_sum, kernel_grad, lifting_grad, phases_grad,
            mapping_grad, readout_grad,
        ) = call(
            small_out_body,
            [(shape, F32) for shape in out_shapes],
            [place.astype(jnp.int32).reshape(1), *got, value_parts, mix_sum, rest_sum, perm],
            4,
            scratch=[pltpu.VMEM((pieces, q_rows, order), F32)],
            scalars=1,
        )
        squeeze_sum = rest_sum[0]
    else:
        m_sum = lax.psum(m_part, BOTH)
        q_all = lax.all_gather(lax.psum(q_part, "batch"), "seq", axis=0, tiled=False)
        main_sum = lax.psum_scatter(main[0], BOTH, scatter_dimension=0, tiled=True)
        switch_own = lax.psum_scatter(side[0], BOTH, scatter_dimension=0, tiled=True)
        small = lax.psum(small.astype(F32), BOTH)
        small = jnp.concatenate([small[:, :wide], small[:, wide : 2 * wide]], 0)

        def natural(grad):
            shape = grad.shape
            grad = grad.reshape(shape[0], BLOCKS, octet, owned).swapaxes(1, 2)
            return grad.reshape(shape)

        expand_grad = jnp.stack([natural(main_sum[:, k * wide : (k + 1) * wide]) for k in range(2)])
        shrink_grad = main_sum[:, 2 * wide : 3 * wide].reshape(owned, BLOCKS, width)
        shrink_grad = shrink_grad.swapaxes(0, 1).reshape(BLOCKS * owned, width)
        mixing_grad = jnp.stack([value_grad, switch_own, main_sum[:, 3 * wide :]])
        spread_sum = jnp.stack([natural(small[:16]), natural(small[16:32])])
        squeeze_sum, merge_sum, switch_sum, tail_sum = small[32:].reshape(16, BLOCKS, width).swapaxes(0, 1)
        value_sum = q_all[:, chans : chans + BLOCKS, :chans].reshape(pieces, BLOCKS, BLOCKS, span)
        value_sum = value_sum.transpose(1, 2, 0, 3).reshape(16, width)
        twiddle_sum = jnp.stack([value_sum, switch_sum, merge_sum])
        taps_value = q_all[:, chans + BLOCKS : chans + BLOCKS + 3, :chans]
        taps_value = taps_value.reshape(pieces, 3, BLOCKS, span).transpose(1, 2, 0, 3)
        taps_sum = tail_sum[BLOCKS:].reshape(BLOCKS, 3, width).swapaxes(0, 1)
        kernel_grad = jnp.concatenate(
            [taps_value.reshape(3, total), taps_sum.reshape(3, total)], 1
        )
        readout_grad = q_all[:, :chans].reshape(pieces, BLOCKS, span, order)
        readout_grad = readout_grad.transpose(3, 1, 0, 2).reshape(order, total)
        gains_grad = jnp.stack([gain_one.reshape(total), tail_sum[:BLOCKS].reshape(total)])
        lifting_grad = m_sum[order : order + lifting.shape[0]]
        phases_grad = m_sum[order + lifting.shape[0]]
        mapping_grad = m_sum[:order]

    def of_units(rows_now):
        lead = rows_now.shape[:-2]
        shaped = rows_now.reshape(*lead, BLOCKS, BLOCKS, rows_now.shape[-1])
        return jnp.moveaxis(shaped, -1, -3)

    return (
        layer.reshape(seqs, share, total),
        tokens_grad.reshape(seqs, share, total),
        gains_grad,
        mixing_grad,
        of_units(twiddle_sum),
        expand_grad,
        of_units(spread_sum),
        shrink_grad,
        of_units(squeeze_sum),
        kernel_grad,
        lifting_grad,
        phases_grad.reshape(order),
        mapping_grad,
        readout_grad,
    )


def solution(mesh):
    return jax.shard_map(
        per_device,
        mesh=mesh,
        in_specs=(
            P("batch", "seq", None),
            P("batch", "seq", None),
            P(),
            P(None, ("seq", "batch"), None),
            P(),
            P(None, ("seq", "batch"), None),
            P(),
            P(("seq", "batch"), None),
            P(),
            P(),
            P(),
            P(),
            P(),
            P(),
            P(),
        ),
        out_specs=(
            P("batch", "seq", None),
            P("batch", "seq", None),
            P(),
            P(None, ("seq", "batch"), None),
            P(),
            P(None, ("seq", "batch"), None),
            P(),
            P(("seq", "batch"), None),
            P(),
            P(),
            P(),
            P(),
            P(),
            P(),
        ),
        check_vma=False,
    )
```

```python
import functools
import math

import jax
import jax.numpy as jnp
import numpy as np
from jax import lax
from jax.experimental import pallas as pl
from jax.experimental.pallas import tpu as pltpu
from jax.sharding import PartitionSpec as P

BLOCKS = 4
BOTH = ("seq", "batch")
F32 = jnp.float32
BF16 = jnp.bfloat16
HIGHEST = lax.Precision.HIGHEST
LIMIT = 52
FILLERS = dict.fromkeys(
    (
        "gather_body", "switch_body", "switch_back_body", "first_sum_body", "second_sum_body",
        "third_sum_body", "weights_out_body",
    ),
    0.05,
)
NN = ((1,), (0,))
NT = ((1,), (1,))
TN = ((0,), (0,))


def mm(left, right, dims=NN, precision=None):
    return lax.dot_general(
        left, right, (dims, ((), ())), preferred_element_type=F32, precision=precision
    )


class Late:
    def __init__(self, source, held, done):
        self.held, self.waiting = held, pltpu.make_async_copy(source, held, done)
        self.waiting.start()

    def ready(self):
        if self.waiting is not None:
            self.waiting.wait()
            self.waiting = None
        return self.held


class Early:
    def __init__(self, target, held, done):
        self.ref, self.copy, self.left = held, pltpu.make_async_copy(held, target, done), False

    def leave(self):
        if not self.left:
            self.copy.start()
            self.left = True


def call(body, outs, operands, micros, scratch=(), scalars=0, limit=LIMIT, late=(), early=()):
    name = (body.func if isinstance(body, functools.partial) else body).__name__
    specs = [
        pl.BlockSpec(
            memory_space=pl.ANY if k in late else pltpu.SMEM if k < scalars else pltpu.VMEM
        )
        for k in range(len(operands))
    ]
    out_specs = [
        pl.BlockSpec(memory_space=pl.ANY if k in early else pltpu.VMEM) for k in range(len(outs))
    ]
    staging = [pltpu.VMEM(operands[k].shape, operands[k].dtype) for k in late]
    staging += [pltpu.VMEM(*outs[k]) for k in early]
    count = len(staging)

    def whole(*refs):
        refs = list(refs)
        held = refs[len(operands) + len(outs) :][:count]
        rest = refs[len(operands) + len(outs) + count :]
        if not count:
            body(*refs)
            return
        done, rest = rest[0], rest[1:]
        for n, k in enumerate(late):
            refs[k] = Late(refs[k], held[n], done.at[n])
        for n, k in enumerate(early):
            at = len(operands) + k
            refs[at] = Early(refs[at], held[len(late) + n], done.at[len(late) + n])
        body(*refs[: len(operands) + len(outs)], *rest)
        for k in early:
            refs[len(operands) + k].leave()
        for k in early:
            refs[len(operands) + k].copy.wait()
        for k in late:
            refs[k].ready()

    if count:
        staging.append(pltpu.SemaphoreType.DMA((count,)))
    return pl.pallas_call(
        whole,
        out_shape=[jax.ShapeDtypeStruct(shape, kind) for shape, kind in outs],
        in_specs=specs,
        out_specs=out_specs,
        scratch_shapes=staging + list(scratch),
        compiler_params=pltpu.CompilerParams(vmem_limit_bytes=limit << 20),
        cost_estimate=pl.CostEstimate(
            flops=int(FILLERS.get(name, micros) * 1.15e9), bytes_accessed=1 << 16, transcendentals=0
        ),
    )(*operands)


def packed_tables(points):
    size = 2 * points
    place = np.arange(size)[:, None].astype(np.int64)
    bins = np.arange(points)[None, :]
    angle = 2.0 * np.pi / size * ((place * bins) % size)
    forward = np.concatenate([np.cos(angle), -np.sin(angle)], 1)
    forward[:, points] = np.where(np.arange(size) % 2 == 0, 1.0, -1.0)
    weight = np.where(np.arange(size) % points == 0, 1.0, 2.0) / size
    backward = (forward * weight[None, :]).T
    return forward.astype(np.float32), np.ascontiguousarray(backward).astype(np.float32)


def split_table(table):
    high = table.astype(jnp.bfloat16)
    low = (table - high.astype(np.float32)).astype(jnp.bfloat16)
    return high, low


def feature_rows(length):
    place = np.arange(length)
    rows = [place / length]
    for harmonic in (1, 2):
        angle = 2.0 * np.pi / length * ((harmonic * place) % length)
        rows += [np.cos(angle), np.sin(angle)]
    rows += [np.ones(length), np.zeros(length), np.zeros(length)]
    return np.stack(rows).astype(np.float32)


def spread_matrix(pieces, span):
    width = pieces * span
    out = np.zeros((BLOCKS, pieces, BLOCKS, span, width), np.float32)
    for b in range(BLOCKS):
        for piece in range(pieces):
            for k in range(span):
                out[b, piece, b, k, piece * span + k] = 1.0
    return out.reshape(BLOCKS, pieces * BLOCKS * span, width).astype(jnp.bfloat16)


def normalize_rows(values):
    centred = values - jnp.mean(values, -1, keepdims=True)
    factor = lax.rsqrt(jnp.mean(centred * centred, -1, keepdims=True) + 1e-05)
    return centred * factor, factor


def sincos(angle):
    turns = (angle * (2.0 / math.pi) + 12582912.0) - 12582912.0
    rest = (angle - turns * 1.5703125) - turns * 4.83826794896619e-4
    square = rest * rest
    sine = rest + rest * square * (
        -1.6666654611e-1 + square * (8.3321608736e-3 + square * -1.9515295891e-4)
    )
    cosine = (
        1.0
        - 0.5 * square
        + square
        * square
        * (4.166664568298827e-2 + square * (-1.388731625493765e-3 + square * 2.443315711809948e-5))
    )
    quarter = turns.astype(jnp.int32)
    odd = jnp.bitwise_and(quarter, 1) == 1
    sine_sign = (1 - jnp.bitwise_and(quarter, 2)).astype(F32)
    cosine_sign = (1 - jnp.bitwise_and(quarter + 1, 2)).astype(F32)
    return (
        jnp.where(odd, cosine, sine) * sine_sign,
        jnp.where(odd, sine, cosine) * cosine_sign,
    )


def parts_of(values):
    width = values.shape[1] // BLOCKS
    return [values[:, k * width : (k + 1) * width] for k in range(BLOCKS)]


def mix(sectioned, rows):
    return [
        sum(sectioned[a] * rows[4 * a + b : 4 * a + b + 1, :] for a in range(BLOCKS))
        for b in range(BLOCKS)
    ]


def unmix(upstream, rows):
    return [
        sum(upstream[b] * rows[4 * a + b : 4 * a + b + 1, :] for b in range(BLOCKS))
        for a in range(BLOCKS)
    ]


def mix_grad(sectioned, upstream):
    return jnp.concatenate(
        [
            jnp.sum(sectioned[a] * upstream[b], 0, keepdims=True)
            for a in range(BLOCKS)
            for b in range(BLOCKS)
        ],
        0,
    )


def lane_of(shape):
    return lax.broadcasted_iota(jnp.int32, shape, len(shape) - 1)


def row_of(shape):
    return lax.broadcasted_iota(jnp.int32, shape, 0)


def time_rows(block_ref, span):
    pieces, rows, _ = block_ref.shape
    return jnp.concatenate(
        [
            block_ref[n].astype(F32)[s * span : (s + 1) * span]
            for s in range(rows // span)
            for n in range(pieces)
        ],
        1,
    )


def later_lanes(values, steps, length):
    total = values.shape[1]
    moved = pltpu.roll(values, total - steps, 1)
    return jnp.where(lane_of(values.shape) % length < length - steps, moved, 0.0)


def earlier_lanes(values, steps, length):
    moved = pltpu.roll(values, steps, 1)
    return jnp.where(lane_of(values.shape) % length >= steps, moved, 0.0)


def to_pieces(lanes_now, out_ref, length):
    pieces, _, width = out_ref.shape
    seqs = lanes_now.shape[1] // length
    for n in range(pieces):
        out_ref[n] = jnp.concatenate(
            [
                lanes_now[:, s * length + n * width : s * length + (n + 1) * width]
                for s in range(seqs)
            ],
            0,
        ).astype(BF16)


def spectrum(flat, high_ref, low_ref, out_ref):
    out = mm(flat, high_ref[...]) + mm(flat, low_ref[...])
    out_ref[...] = out.reshape(out_ref.shape)


def mm2(left, right, dims=NN):
    left_high = left.astype(BF16)
    left_low = (left - left_high.astype(F32)).astype(BF16)
    return mm(left_low, right, dims) + mm(left_high, right, dims)


def mm3(left, right, dims=NN):
    left_high, right_high = left.astype(BF16), right.astype(BF16)
    left_low = (left - left_high.astype(F32)).astype(BF16)
    right_low = (right - right_high.astype(F32)).astype(BF16)
    return (
        mm(left_high, right_low, dims) + mm(left_low, right_high, dims)
    ) + mm(left_high, right_high, dims)


def nyquist_split(spec):
    half = spec.shape[-1] // 2
    real, imaginary = spec[..., :half], spec[..., half:]
    first = lane_of(real.shape) == 0
    return jnp.where(first, 0.0, imaginary), jnp.where(first, imaginary, real)


def norm_body(tok_ref, gains_ref, norm_ref):
    norm = normalize_rows(tok_ref[...].astype(F32))[0] * gains_ref[0:1, :]
    norm_ref[...] = norm.astype(BF16)


def unit_rows(ref):
    return jnp.concatenate([ref[a].astype(F32) for a in range(BLOCKS)], 0)


def filter_body(
    place_ref, lift_ref, phase_ref, map_ref, read_all, damp_all, taps_all, tw_ref, perm_ref, feat_ref,
    table_ref, s1, c1, s2, c2, spec_ref, read_ref, columns_ref, mix_ref,
):
    span = read_ref.shape[1]
    at = pl.ds(pl.multiple_of(place_ref[0] * span, span), span)
    chosen = [perm_ref[b, at, :] for b in range(BLOCKS)]
    width = perm_ref.shape[2]
    read_ref[...] = sum(
        mm(read_all[:, b * width : (b + 1) * width], chosen[b].astype(F32), NT, HIGHEST)
        for b in range(BLOCKS)
    )
    rows = jnp.concatenate([damp_all[...], taps_all[...], jnp.zeros((4, BLOCKS * width), F32)], 0)
    columns = sum(
        mm(chosen[b].astype(F32), rows[:, b * width : (b + 1) * width], NT, HIGHEST)
        for b in range(BLOCKS)
    )
    columns_ref[...] = columns
    factors = unit_rows(tw_ref)
    mix_ref[...] = sum(
        mm((chosen[b] * factors[4 * a + b : 4 * a + b + 1].astype(BF16)), chosen[a], NT)
        for a in range(BLOCKS)
        for b in range(BLOCKS)
    ).astype(BF16)
    lift = jnp.concatenate(
        [lift_ref[...], phase_ref[...], jnp.zeros((7 - lift_ref.shape[0], map_ref.shape[0]), F32)], 0
    )
    sine_one, cosine_one = sincos(mm(lift, feat_ref[...], TN, HIGHEST))
    s1[...] = sine_one.astype(BF16)
    c1[...] = cosine_one.astype(BF16)
    sine_two, cosine_two = sincos(mm(map_ref[...], sine_one, TN, HIGHEST))
    s2[...] = sine_two.astype(BF16)
    c2[...] = cosine_two.astype(BF16)
    shape = (read_ref.shape[1], sine_two.shape[1])
    place = lane_of(shape).astype(F32)
    response = mm(read_ref[...], sine_two, TN, HIGHEST) * jnp.exp(-place * columns[:, 0:1])
    pieces, span, doubled = spec_ref.shape
    width = doubled // 2
    zero = jnp.zeros((span, width), F32)
    rows = []
    for k in range(pieces):
        now = response[:, k * width : (k + 1) * width]
        before = response[:, (k - 1) * width : k * width] if k else zero
        rows.append(
            jnp.concatenate([now, jnp.where(lane_of(before.shape) == 0, 0.0, before)], 1)
        )
    spec = mm3(jnp.concatenate(rows, 0), table_ref[...])
    spec_ref[...] = spec.reshape(pieces, span, doubled)


def value_body(packed, *refs):
    if packed:
        held_ref, norm_ref, perm_ref, full_ref, out_ref = refs
        rows = held_ref.shape[1] * 3 // 5
        share = held_ref.shape[0] // BLOCKS
        inner = []
        for a in range(BLOCKS):
            blocks = []
            for k in range(a * share, (a + 1) * share):
                held = held_ref[k].astype(F32)
                blocks.append(unpack_rows(held, rows))
            inner.append(jnp.concatenate(blocks, 0).astype(BF16))
            full_ref[a * rows * share : (a + 1) * rows * share, :] = inner[a]
    else:
        inner_ref, norm_ref, perm_ref, full_ref, out_ref = refs
        full_ref[...] = inner_ref[...]
        width = full_ref.shape[1]
        inner = [full_ref[a * width : (a + 1) * width, :] for a in range(BLOCKS)]
    norm = parts_of(norm_ref[...])
    first = [mm(norm[a], inner[a]).astype(BF16) for a in range(BLOCKS)]
    send_pieces(first, perm_ref, out_ref)


def pack_rows(values):
    rows = values.shape[0]
    rest = [values[k : k + 8, 128:] for k in range(0, rows, 8)] + [jnp.zeros_like(values[:8, 128:])]
    pairs = [jnp.concatenate(rest[k : k + 2], 1) for k in range(0, rows // 8, 2)]
    return jnp.concatenate([values[:, :128]] + pairs, 0)


def unpack_rows(held, rows):
    rest = []
    for k in range(rows // 8):
        start = rows + 8 * (k // 2)
        rest.append(held[start : start + 8, 64 * (k % 2) : 64 * (k % 2) + 64])
    return jnp.concatenate([held[:rows], jnp.concatenate(rest, 0)], 1)


def gather_body(
    me_ref, left_own, left_other, right_own, right_other, spread_ref, full_ref, pair_ref, rows_ref
):
    rows, cut = left_own.shape[1:]
    octet = spread_ref.shape[3] // (BLOCKS * rows)
    for k in range(2):
        natural = unit_rows(spread_ref.at[k])
        rows_ref[k] = jnp.concatenate(
            [
                natural[:, (o * BLOCKS + g) * rows : (o * BLOCKS + g + 1) * rows]
                for g in range(BLOCKS)
                for o in range(octet)
            ],
            1,
        )
    start = full_ref.shape[1] - pair_ref.shape[1]
    count = 2 * left_own.shape[0]
    per = 2 if rows % 16 else 1
    for k in range(0, count, per):
        blocks = []
        for owner in range(k, k + per):
            bits = apart_bits(me_ref, owner)
            deep = bits[3] + 2 * bits[4]
            left = bits[0] * 8 + bits[2] * 4 + deep
            right = bits[2] * 8 + bits[0] * 4 + deep
            near = bits[1] == 0
            blocks.append(
                jnp.concatenate(
                    [
                        jnp.where(near, left_own[left].astype(F32), left_other[left].astype(F32)),
                        jnp.where(
                            near, right_own[right].astype(F32), right_other[right].astype(F32)
                        ),
                    ],
                    1,
                )
            )
        block = jnp.concatenate(blocks, 0).astype(BF16)
        full_ref[k * rows : (k + per) * rows, :] = block
        pair_ref[k * rows : (k + per) * rows, :] = block[:, start:]


def send_pieces(parts, perm_ref, out_ref):
    pieces, rows, width = out_ref.shape
    seqs = parts[0].shape[0] // width
    span = rows // seqs
    turned = [
        sum(
            mm(perm_ref[k], parts[k][s * width : (s + 1) * width], NT) for k in range(BLOCKS)
        )
        for s in range(seqs)
    ]
    for n in range(pieces):
        out_ref[n] = jnp.concatenate(
            [turned[s][n * span : (n + 1) * span] for s in range(seqs)], 0
        ).astype(BF16)


def receive_pieces(in_ref, perm_ref):
    pieces, rows, width = in_ref.shape
    seqs = rows * pieces // (BLOCKS * perm_ref.shape[2])
    span = rows // seqs
    held = [in_ref[n].astype(F32) for n in range(pieces)]
    turned = [
        jnp.concatenate([h[s * span : (s + 1) * span] for h in held], 0).T.astype(BF16)
        for s in range(seqs)
    ]
    return [
        jnp.concatenate([mm(turned[s], perm_ref[k]) for s in range(seqs)], 0)
        for k in range(BLOCKS)
    ]


def earlier_rows(values, halo, steps):
    moved = pltpu.roll(values, steps, 0)
    row = row_of(values.shape)
    for k in range(steps):
        moved = jnp.where(row == k, halo[2 - steps + k : 3 - steps + k], moved)
    return moved


def later_rows(values, halo, steps):
    count = values.shape[0]
    moved = pltpu.roll(values, count - steps, 0)
    row = row_of(values.shape)
    for k in range(steps):
        moved = jnp.where(row == count - steps + k, halo[k : k + 1], moved)
    return moved


def per_sequence(function, values, halo, seqs, steps):
    count = values.shape[0] // seqs
    return jnp.concatenate(
        [
            function(values[s * count : (s + 1) * count], halo[2 * s : 2 * s + 2], steps)
            for s in range(seqs)
        ],
        0,
    )


def switch_body(
    seqs, norm_ref, halo_ref, gains_ref, full_ref, tw_ref, taps_ref, sect_ref, sw_ref, sh_ref, gate_ref
):
    width = norm_ref.shape[1] // BLOCKS
    edge = jnp.concatenate([halo_ref[s].astype(F32) for s in range(seqs)], 0)
    edge = jnp.concatenate([edge, jnp.zeros((16 - 2 * seqs, edge.shape[1]), F32)], 0)
    edge_norm = normalize_rows(edge)[0] * gains_ref[0:1, :]
    norm, halo = parts_of(norm_ref[...]), parts_of(edge_norm.astype(BF16))
    inner = [full_ref[a * width : (a + 1) * width, :][:, :width] for a in range(BLOCKS)]
    first = [mm(norm[a], inner[a]) for a in range(BLOCKS)]
    for a in range(BLOCKS):
        sect_ref[a] = first[a]
    rows = unit_rows(tw_ref)
    all_taps = parts_of(taps_ref[...][:, BLOCKS * width :])
    switch = mix(first, rows)
    edge = mix([mm(halo[a], inner[a]) for a in range(BLOCKS)], rows)
    for b in range(BLOCKS):
        sw_ref[b] = switch[b].astype(BF16)
        sh_ref[b] = edge[b].astype(BF16)
        now = switch[b].astype(BF16).astype(F32)
        before = edge[b].astype(BF16).astype(F32)
        taps = all_taps[b]
        gate_ref[b] = (
            taps[0:1] * now
            + taps[1:2] * per_sequence(earlier_rows, now, before, seqs, 1)
            + taps[2:3] * per_sequence(earlier_rows, now, before, seqs, 2)
        )


def loop(start, stop, body, carry, unrolled):
    if not unrolled:
        return lax.fori_loop(start, stop, body, carry)
    for step in range(start, stop):
        carry = body(step, carry)
    return carry


def bins_of(half):
    return [(slice(k, k + 128), slice(half + k, half + k + 128)) for k in range(0, half, 128)]


def convolve(spec_ref, b_ref, c_ref, x_ref, y_ref):
    pieces, rows, doubled = x_ref.shape
    span = spec_ref.shape[1]
    zero = jnp.zeros((span, 128), F32)
    parts = [slice(k, k + span) for k in range(0, rows, span)]
    for low, up in bins_of(doubled // 2):

        def outer(i, carry, low=low, up=up):
            def inner(j, totals):
                k = i - j
                a_now, b_now, c_now = spec_ref[k, :, low], b_ref[k, :, low], c_ref[k, :, low]
                out = []
                for s, at in enumerate(parts):
                    real, imag = x_ref[j, at, low], x_ref[j, at, up]
                    out.append(totals[2 * s] + a_now * real - b_now * imag)
                    out.append(totals[2 * s + 1] + b_now * real + c_now * imag)
                return tuple(out)

            totals = loop(0, i + 1, inner, (zero,) * (2 * len(parts)), pieces <= 8)
            for s, at in enumerate(parts):
                y_ref[i, at, low] = totals[2 * s]
                y_ref[i, at, up] = totals[2 * s + 1]
            return carry

        loop(0, pieces, outer, 0, pieces <= 8)


def correlate(spec_ref, b_ref, c_ref, g_ref, y_ref):
    pieces, rows, doubled = g_ref.shape
    span = spec_ref.shape[1]
    zero = jnp.zeros((span, 128), F32)
    parts = [slice(k, k + span) for k in range(0, rows, span)]
    for low, up in bins_of(doubled // 2):

        def outer(j, carry, low=low, up=up):
            def inner(i, totals):
                k = i - j
                a_now, b_now, c_now = spec_ref[k, :, low], b_ref[k, :, low], c_ref[k, :, low]
                out = []
                for s, at in enumerate(parts):
                    real, imag = g_ref[i, at, low], g_ref[i, at, up]
                    out.append(totals[2 * s] + a_now * real + b_now * imag)
                    out.append(totals[2 * s + 1] + c_now * imag - b_now * real)
                return tuple(out)

            totals = loop(j, pieces, inner, (zero,) * (2 * len(parts)), pieces <= 8)
            for s, at in enumerate(parts):
                y_ref[j, at, low] = totals[2 * s]
                y_ref[j, at, up] = totals[2 * s + 1]
            return carry

        loop(0, pieces, outer, 0, pieces <= 8)


def block_rows(piece_ref, block):
    pieces, _, width = piece_ref.shape
    each = block // width
    return jnp.concatenate(
        [
            jnp.concatenate([piece_ref[n + k] for k in range(each)], 1)
            for n in range(0, pieces, each)
        ],
        0,
    )


def conv_body(
    length, sect_ref, mix_ref, taps_ref, spec_ref, high_ref, low_ref, back_ref,
    out_ref, cin_ref, signal_ref, x_ref, y_ref, b_ref, c_ref,
):
    span = spec_ref.shape[1]
    lanes_now = time_rows(sect_ref, span).astype(BF16)
    signal = mm(mix_ref[...], lanes_now).astype(BF16)
    signal_ref[...] = signal
    signal = signal.astype(F32)
    conv_in = (
        taps_ref[:, 1:2] * signal
        + taps_ref[:, 2:3] * earlier_lanes(signal, 1, length)
        + taps_ref[:, 3:4] * earlier_lanes(signal, 2, length)
    )
    to_pieces(conv_in, cin_ref, length)
    spectrum(cin_ref[...].reshape(-1, cin_ref.shape[2]), high_ref, low_ref, x_ref)
    b_ref[...], c_ref[...] = nyquist_split(spec_ref[...])
    convolve(spec_ref, b_ref, c_ref, x_ref, y_ref)
    pieces, rows, doubled = y_ref.shape
    out = mm3(y_ref[...].reshape(pieces * rows, doubled), back_ref[...]).astype(BF16)
    width = out_ref.shape[2]
    each = doubled // 2 // width
    for n in range(pieces):
        for k in range(each):
            out_ref[n * each + k] = out[n * rows : (n + 1) * rows, k * width : (k + 1) * width]


def middle_body(
    fast, seqs, me_ref, long_ref, gate_ref, tok_ref, cot_ref, gains_ref, full_ref, pair_ref, tw_ref,
    sp_ref, sq_ref, perm_ref, layer_ref, lg_ref, swg_ref, res_ref, spg_ref, sqg_ref, twg_ref, gain_ref, edge_ref, *refs,
):
    *weight_outs, fg, fu, act, ug, hg, hid_ref, fgate_ref, fup_ref = refs
    rows, total = tok_ref.shape
    width = total // BLOCKS
    wide = fg.shape[2]
    base = 2 * wide
    tw_rows, sq_rows = unit_rows(tw_ref), unit_rows(sq_ref)
    gate = [gate_ref[b] for b in range(BLOCKS)]
    long_out = receive_pieces(long_ref, perm_ref)
    gated = [(gate[b] * long_out[b]).astype(BF16) for b in range(BLOCKS)]
    at = [slice(a * width, (a + 1) * width) for a in range(BLOCKS)]
    merge = [pair_ref[at[a], :][:, width:] for a in range(BLOCKS)]
    sect_merge = [mm(gated[a], merge[a]) for a in range(BLOCKS)]
    merged = mix(sect_merge, tw_rows)
    tokens = parts_of(tok_ref[...].astype(F32))
    residual = [tokens[b] + merged[b] for b in range(BLOCKS)]
    mean = sum(jnp.sum(r, -1, keepdims=True) for r in residual) / total
    centred = [r - mean for r in residual]
    variance = sum(jnp.sum(c * c, -1, keepdims=True) for c in centred) / total
    factor = lax.rsqrt(variance + 1e-05)
    normed = [c * factor for c in centred]
    gain = parts_of(gains_ref[1:2, :])
    norm_two = [(normed[a] * gain[a]).astype(BF16) for a in range(BLOCKS)]
    full_ref, sp_ref = full_ref.ready(), sp_ref.ready()
    for a in range(BLOCKS):
        fg[a] = mm(norm_two[a], full_ref[at[a], :wide])
        fu[a] = mm(norm_two[a], full_ref[at[a], wide : 2 * wide])

    step = 32
    lanes = 128

    def forward_lane(l, carry):
        here = pl.ds(pl.multiple_of(l * lanes, lanes), lanes)

        def forward_row(r, inner_carry):
            down = pl.ds(pl.multiple_of(r * step, step), step)
            gate_pre = mix([fg[a, down, here] for a in range(BLOCKS)], sp_ref[0, :, here])
            held = []
            for v in gate_pre:
                square = v * v
                half = 0.5 + 0.5 * jnp.tanh(v * (0.7978845608 + 0.0356774081 * square))
                active = v * half
                steep = 1.5957691216 + 0.2140644488 * square
                held.append((active, half + active * (1.0 - half) * steep))
            up_pre = mix([fu[a, down, here] for a in range(BLOCKS)], sp_ref[1, :, here])
            for b in range(BLOCKS):
                active, slope = held[b]
                hid_ref[b, down, here] = (active * up_pre[b]).astype(BF16)
                act[b, down, here] = active
                ug[b, down, here] = up_pre[b] * slope
            return inner_carry

        return lax.fori_loop(0, rows // step, forward_row, carry)

    lax.fori_loop(0, wide // lanes, forward_lane, 0)

    shrink = []
    for a in range(BLOCKS):
        held = full_ref[at[a], base : base + wide]
        shrink.append(jnp.concatenate(parts_of(held), 0))
    sect_down = [mm(hid_ref[a], shrink[a]) for a in range(BLOCKS)]
    lowered = mix(sect_down, sq_rows)
    layer_ref.ref[...] = jnp.concatenate(
        [(residual[b] + lowered[b]).astype(BF16) for b in range(BLOCKS)], 1
    )
    layer_ref.leave()
    upstream = parts_of(cot_ref.ready()[...].astype(F32))
    sqg_ref[...] = mix_grad(sect_down, upstream)
    back_down = unmix(upstream, sq_rows)
    back_down = [v.astype(BF16) for v in back_down]
    for a in range(BLOCKS):
        hg[a] = mm(back_down[a], shrink[a], NT)

    def backward_lane(l, carry):
        here = pl.ds(pl.multiple_of(l * lanes, lanes), lanes)
        zero = jnp.zeros((8, lanes), F32)
        for k, (held, slopes, out_ref) in enumerate(((fg, ug, fgate_ref), (fu, act, fup_ref))):

            def backward_row(r, sums, k=k, held=held, slopes=slopes, out_ref=out_ref):
                down = pl.ds(pl.multiple_of(r * step, step), step)
                grads = [hg[b, down, here] * slopes[b, down, here] for b in range(BLOCKS)]
                for a, value in enumerate(unmix(grads, sp_ref[k, :, here])):
                    out_ref[a, down, here] = value.astype(BF16)
                out = []
                for a in range(BLOCKS):
                    value = held[a, down, here]
                    for b in range(BLOCKS):
                        product = value * grads[b]
                        for n in range(0, step, 16):
                            pair = product[n : n + 8] + product[n + 8 : n + 16]
                            part = pair if n == 0 else part + pair
                        out.append(sums[4 * a + b] + part)
                return tuple(out)

            sums = lax.fori_loop(0, rows // step, backward_row, (zero,) * 16)
            for n in range(16):
                spg_ref[k, pl.ds(n, 1), here] = jnp.sum(sums[n], 0, keepdims=True)
        return carry

    lax.fori_loop(0, wide // lanes, backward_lane, 0)

    n2_grad = [
        mm(fgate_ref[a], full_ref[at[a], :wide], NT)
        + mm(fup_ref[a], full_ref[at[a], wide : 2 * wide], NT)
        for a in range(BLOCKS)
    ]
    scaled = [n2_grad[a] * gain[a] for a in range(BLOCKS)]
    plain = sum(jnp.sum(v, -1, keepdims=True) for v in scaled) / total
    joint = sum(jnp.sum(scaled[a] * normed[a], -1, keepdims=True) for a in range(BLOCKS)) / total
    res_grad = [
        upstream[a] + factor * (scaled[a] - plain - normed[a] * joint) for a in range(BLOCKS)
    ]
    gain_ref[...] = jnp.concatenate(
        [jnp.sum(n2_grad[a] * normed[a], 0, keepdims=True) for a in range(BLOCKS)], 0
    )
    for a in range(BLOCKS):
        res_ref.ref[a] = res_grad[a]
    res_ref.leave()
    twg_ref[...] = mix_grad(sect_merge, res_grad)
    back_merge = [v.astype(BF16) for v in unmix(res_grad, tw_rows)]
    long_grad = []
    for a in range(BLOCKS):
        gated_grad = mm(back_merge[a], merge[a], NT)
        long_grad.append((gated_grad * gate[a]).astype(BF16))
        now = (gated_grad * long_out[a]).astype(BF16)
        swg_ref.ref[a] = now
        share = rows // seqs
        edge_ref[a] = jnp.concatenate([now[s * share : s * share + 2] for s in range(seqs)], 0)
    swg_ref.leave()
    send_pieces(long_grad, perm_ref, lg_ref.ref)
    lg_ref.leave()

    for a in range(BLOCKS):
        from_hidden = mm(hid_ref[a], back_down[a], TN)
        held = jnp.concatenate(
            [mm(norm_two[a], fgate_ref[a], TN), mm(norm_two[a], fup_ref[a], TN)]
            + [from_hidden[g * width : (g + 1) * width] for g in range(BLOCKS)]
            + [mm(gated[a], back_merge[a], TN)],
            1,
        )
        put_blocks(fast, me_ref, weight_outs, a, held, 2 * wide)


def switch_back_body(
    fast, seqs, me_ref, swg_ref, next_ref, sw_ref, sh_ref, sect_ref, full_ref, tw_ref, taps_ref,
    norm_ref, spg_ref, sqg_ref, mg_ref, gain_ref, n1_ref, small_ref, *outs,
):
    width = swg_ref.shape[2]
    all_taps = parts_of(taps_ref[...][:, BLOCKS * width :])
    back, taps_grad = [], []
    for b in range(BLOCKS):
        grad = swg_ref[b].astype(F32)
        after = next_ref[b].astype(F32)
        taps = all_taps[b]
        back.append(
            taps[0:1] * grad
            + taps[1:2] * per_sequence(later_rows, grad, after, seqs, 1)
            + taps[2:3] * per_sequence(later_rows, grad, after, seqs, 2)
        )
        now, before = sw_ref[b].astype(F32), sh_ref[b].astype(F32)
        shifted = [now] + [per_sequence(earlier_rows, now, before, seqs, m) for m in (1, 2)]
        taps_grad += [jnp.sum(value * grad, 0, keepdims=True) for value in shifted]
    tw_grad = mix_grad([sect_ref[a] for a in range(BLOCKS)], back)
    rest = [sqg_ref[...], mg_ref[...], tw_grad, jnp.concatenate([gain_ref[...]] + taps_grad, 0)]
    small = jnp.concatenate([spg_ref[0], spg_ref[1], jnp.concatenate(rest, 1)], 0)
    count = small_ref.shape[0]
    small_ref[...] = jnp.concatenate([small[:count], small[count:]], 1).astype(BF16)
    first = unmix(back, unit_rows(tw_ref))
    norm = parts_of(norm_ref[...])
    for a in range(BLOCKS):
        now = first[a].astype(BF16)
        n1_ref[a] = mm(now, full_ref[a * width : (a + 1) * width, :][:, :width], NT)
        put_blocks(fast, me_ref, outs, a, mm(norm[a], now, TN), 0)


def apart_bits(me_ref, owner):
    apart = jnp.bitwise_xor(me_ref[0], owner)
    return [jnp.bitwise_and(lax.shift_right_logical(apart, n), 1) for n in range(5)]


def put_blocks(fast, me_ref, outs, a, held, start):
    width = held.shape[0]
    if not fast:
        outs[0][a * width : (a + 1) * width, :] = held
        return
    keep_ref, send_ref = outs
    rows = keep_ref.shape[1]
    for k in range(width // rows):
        block = held[k * rows : (k + 1) * rows].astype(BF16)
        bits = apart_bits(me_ref, a * (width // rows) + k)
        deep = bits[3] * 2 + bits[4]
        for ref, core in ((keep_ref, 0), (send_ref, 1)):

            @pl.when(bits[1] == core)
            def _(ref=ref, block=block, bits=bits, deep=deep):
                if start:
                    ref[bits[0] * 8 + bits[2] * 4 + deep, :, :start] = block[:, :start]
                ref[bits[2] * 8 + bits[0] * 4 + deep, :, start:] = block[:, start:]


def conv_back_body(
    length, g_ref, mix_ref, taps_ref, spec_ref, high_ref, low_ref, back_ref,
    out_ref, cg_ref, sg_ref, x_ref, y_ref, b_ref, c_ref,
):
    span = spec_ref.shape[1]
    spectrum(block_rows(g_ref, x_ref.shape[2] // 2), high_ref, low_ref, x_ref)
    b_ref[...], c_ref[...] = nyquist_split(spec_ref[...])
    correlate(spec_ref, b_ref, c_ref, x_ref, y_ref)
    pieces, rows, doubled = y_ref.shape
    flat = mm3(y_ref[...].reshape(pieces * rows, doubled), back_ref[...])
    flat = flat.astype(BF16).astype(F32)
    grad = jnp.concatenate(
        [
            flat[n * rows + s * span : n * rows + (s + 1) * span]
            for s in range(rows // span)
            for n in range(pieces)
        ],
        1,
    )
    cg_ref[...] = grad.astype(BF16)
    signal_grad = (
        taps_ref[:, 1:2] * grad
        + taps_ref[:, 2:3] * later_lanes(grad, 1, length)
        + taps_ref[:, 3:4] * later_lanes(grad, 2, length)
    )
    sg_ref[...] = signal_grad
    to_pieces(mm(mix_ref[...].astype(F32), signal_grad, TN, HIGHEST), out_ref, length)


def filter_back_body(
    length, g_ref, cin_ref, sect_ref, signal_ref, cg_ref, sg_ref, s1, c1, s2, c2, read_ref, map_ref,
    damp_ref, feat_ref, high_ref, low_ref, back_ref, same_ref, pick_ref,
    out_ref, x_ref, b_ref, c_ref, gs_ref, p_ref,
):
    pieces, span, doubled = p_ref.shape
    half = doubled // 2
    spectrum(cin_ref[...].reshape(-1, half), high_ref, low_ref, x_ref)
    b_ref[...], c_ref[...] = nyquist_split(x_ref[...])
    spectrum(block_rows(g_ref, half), high_ref, low_ref, gs_ref)
    seqs = x_ref.shape[1] // span
    zero = jnp.zeros((span, 128), F32)
    parts = [slice(k, k + span) for k in range(0, seqs * span, span)]
    for low, up in bins_of(half):

        def outer(k, carry, low=low, up=up):
            def inner(j, totals):
                real, imag = totals
                for at in parts:
                    a_now, b_now, c_now = x_ref[j, at, low], b_ref[j, at, low], c_ref[j, at, low]
                    g_real, g_imag = gs_ref[j + k, at, low], gs_ref[j + k, at, up]
                    real = real + a_now * g_real + b_now * g_imag
                    imag = imag + c_now * g_imag - b_now * g_real
                return real, imag

            real, imag = loop(0, pieces - k, inner, (zero, zero), pieces <= 8)
            p_ref[k, :, low] = real
            p_ref[k, :, up] = imag
            return carry

        loop(0, pieces, outer, 0, pieces <= 8)
    flat = mm3(p_ref[...].reshape(pieces * span, doubled), back_ref[...])
    chunks = []
    for k in range(pieces):
        now = flat[k * span : (k + 1) * span, :half]
        if k + 1 < pieces:
            after = flat[(k + 1) * span : (k + 2) * span, half:]
            now = now + jnp.where(lane_of(after.shape) == 0, 0.0, after)
        chunks.append(now)
    response_grad = jnp.concatenate(chunks, 1)
    place = lane_of(response_grad.shape).astype(F32)
    response_grad = response_grad * jnp.exp(-place * damp_ref[:, 0:1])
    readout_grad = mm2(response_grad, s2[...], NT)
    pre_two = mm3(read_ref[...], response_grad) * c2[...].astype(F32)
    order = s1.shape[0]
    high = pre_two.astype(BF16)
    low = (pre_two - high.astype(F32)).astype(BF16)
    mapping_grad = mm(s1[...], low, NT) + mm(s1[...], high, NT)
    pre_one = mm3(map_ref[...], pre_two) * c1[...].astype(F32)
    lift_grad = mm3(feat_ref[...], pre_one, NT)

    sect = time_rows(sect_ref, span).astype(BF16)
    high = sg_ref[...].astype(BF16)
    low = (sg_ref[...] - high.astype(F32)).astype(BF16)
    tw = (mm(sect, low, NT) + mm(sect, high, NT)) * same_ref[...]
    tw = mm(pick_ref[...], tw, NN, HIGHEST)
    cg = cg_ref[...].astype(F32)
    signal = signal_ref[...].astype(F32)
    taps = []
    for m in range(3):
        moved = signal if m == 0 else earlier_lanes(signal, m, length)
        taps.append(jnp.sum(moved * cg, 1, keepdims=True))
    column = lane_of((span, 128))
    columns = sum(jnp.where(column == BLOCKS + m, taps[m], 0.0) for m in range(3))
    tw = tw + columns.T[: tw.shape[0], :span]
    tw = jnp.concatenate([tw, jnp.zeros((8, order - span), F32)], 1)
    out = jnp.concatenate([mapping_grad, lift_grad, readout_grad, tw], 0)
    out_ref[...] = out.astype(out_ref.dtype)


def last_body(
    fast, fg_ref, perm_ref, inner_ref, norm_ref, n1_ref, res_ref, tok_ref, gains_ref, out_ref, *pay
):
    width = inner_ref.shape[1]
    first = [v.astype(BF16) for v in receive_pieces(fg_ref, perm_ref)]
    norm = parts_of(norm_ref[...])
    normed, factor = normalize_rows(tok_ref[...].astype(F32))
    normed = parts_of(normed)
    gain = parts_of(gains_ref[0:1, :])
    grads = [
        mm(first[a], inner_ref[a * width : (a + 1) * width, :], NT) + n1_ref[a]
        for a in range(BLOCKS)
    ]
    scaled = [grads[a] * gain[a] for a in range(BLOCKS)]
    total = width * BLOCKS
    plain = sum(jnp.sum(v, -1, keepdims=True) for v in scaled) / total
    joint = sum(jnp.sum(scaled[a] * normed[a], -1, keepdims=True) for a in range(BLOCKS)) / total
    out_ref[...] = jnp.concatenate(
        [res_ref[a] + factor * (scaled[a] - plain - normed[a] * joint) for a in range(BLOCKS)], 1
    )
    gain_grad = [jnp.sum(grads[a] * normed[a], 0, keepdims=True) for a in range(BLOCKS)]
    weight = [mm(norm[a], first[a], TN) for a in range(BLOCKS)]
    if not fast:
        for a in range(BLOCKS):
            pay[0][a * width : (a + 1) * width, :] = weight[a]
            pay[1][a : a + 1, :] = gain_grad[a]
        return
    count, rows, _ = pay[0].shape
    share = count // BLOCKS
    held = (rows - 8) * 3 // 5
    flat = jnp.concatenate(gain_grad, 1)
    tail = [flat[:, k : k + 128] for k in range(0, total, 128)]
    tail = jnp.concatenate(tail + [jnp.zeros((8 - len(tail), 128), F32)], 0)
    for a in range(BLOCKS):
        for k in range(share):
            block = pack_rows(weight[a][k * held : (k + 1) * held])
            pay[0][a * share + k] = jnp.concatenate([block, tail], 0).astype(BF16)


def first_sum_body(
    keep_ref, got_ref, side_ref, side_got, small_ref, small_got, left_keep, left_send, right_keep, right_send
):
    n, _, cut = left_keep.shape
    n -= 1
    for k in range(2 * n):
        main = keep_ref[k].astype(F32) + got_ref[k].astype(F32)
        side = side_ref[k].astype(F32) + side_got[k].astype(F32)
        right = jnp.concatenate([main[:, cut:], side], 1).astype(BF16)
        left_out, right_out = (left_keep, right_keep) if k < n else (left_send, right_send)
        left_out[k % n] = main[:, :cut].astype(BF16)
        right_out[k % n] = right
    small = (small_ref[...].astype(F32) + small_got[...].astype(F32)).astype(BF16)
    left_keep[n] = small
    left_send[n] = small


def second_sum_body(
    left_ref, left_got, right_ref, right_got, left_keep, left_send, right_keep, right_send
):
    n = right_keep.shape[0]
    for k in range(2 * n):
        left = (left_ref[k].astype(F32) + left_got[k].astype(F32)).astype(BF16)
        right = (right_ref[k].astype(F32) + right_got[k].astype(F32)).astype(BF16)
        left_out, right_out = (left_keep, right_keep) if k < n else (left_send, right_send)
        left_out[k % n] = left
        right_out[k % n] = right
    small = (left_ref[2 * n].astype(F32) + left_got[2 * n].astype(F32)).astype(BF16)
    left_keep[n] = small
    left_send[n] = small


def third_sum_body(left_ref, left_got, right_ref, right_got, *outs):
    left = [(left_ref[k].astype(F32) + left_got[k].astype(F32)).astype(BF16) for k in range(5)]
    right = [(right_ref[k].astype(F32) + right_got[k].astype(F32)).astype(BF16) for k in range(4)]
    for k, out_ref in enumerate(outs):
        out_ref[...] = jnp.concatenate([left[k], right[k], left[4]], 1)


def natural_order(values, owned):
    octet = values.shape[1] // (BLOCKS * owned)
    return jnp.concatenate(
        [
            values[:, (g * octet + o) * owned : (g * octet + o + 1) * owned]
            for o in range(octet)
            for g in range(BLOCKS)
        ],
        1,
    )


def weights_out_body(
    own_ref, one_ref, two_ref, three_ref, expand_ref, spread_ref, shrink_ref, mix_ref, rest_ref
):
    parts = [ref[...].astype(F32) for ref in (own_ref, one_ref, two_ref, three_ref)]
    held = (parts[0] + parts[1]) + (parts[2] + parts[3])
    owned, wide = expand_ref.shape[1:]
    width = mix_ref.shape[2]
    for k in range(2):
        expand_ref[k] = natural_order(held[:, k * wide : (k + 1) * wide], owned)
        start = 2 * wide + BLOCKS * width + k * width
        mix_ref[1 - k] = held[:, start : start + width]
    for g in range(BLOCKS):
        start = 2 * wide + g * width
        shrink_ref[g * owned : (g + 1) * owned, :] = held[:, start : start + width]
    start = 3 * wide + 2 * width
    small = jnp.concatenate([held[:, start : start + wide], held[:, start + wide :]], 0)
    for k in range(2):
        spread_ref[k] = natural_order(small[16 * k : 16 * k + 16], owned)
    for k in range(BLOCKS):
        rest_ref[k] = small[32:, k * width : (k + 1) * width]


def small_out_body(
    place_ref, own_ref, one_ref, two_ref, three_ref, rest_ref, perm_ref, twiddle_ref, kernel_ref, lift_ref, phase_ref, map_ref, read_ref, q_ref,
):
    order = map_ref.shape[0]
    m_rows, q_rows = order + 8, q_ref.shape[1]
    chans = q_rows - 8
    pieces = q_ref.shape[0]
    width = perm_ref.shape[2]
    parts = [ref[...] for ref in (own_ref, one_ref, two_ref, three_ref)]
    sums = [part[:m_rows].astype(F32) for part in parts]
    m_sum = (sums[0] + sums[1]) + (sums[2] + sums[3])
    map_ref[...] = m_sum[:order]
    lift_ref[...] = m_sum[order : order + lift_ref.shape[0]]
    phase_ref[...] = m_sum[order + lift_ref.shape[0] : order + lift_ref.shape[0] + 1]
    for k, outer in enumerate((0, 2, 1, 3)):
        for n, inner in enumerate((0, 4, 8, 12)):
            start = m_rows + n * q_rows
            q_ref[jnp.bitwise_xor(place_ref[0], outer ^ inner)] = parts[k][
                start : start + q_rows
            ].astype(F32)
    tall = jnp.concatenate([q_ref[n, :chans] for n in range(pieces)], 0).astype(BF16)
    broad = jnp.concatenate([q_ref[n, chans:, :chans] for n in range(pieces)], 1).astype(BF16)
    rest = [mm(broad, perm_ref[b]) for b in range(BLOCKS)]
    read_ref[...] = jnp.concatenate([mm(tall, perm_ref[b], TN) for b in range(BLOCKS)], 1)
    for a in range(BLOCKS):
        for b in range(BLOCKS):
            twiddle_ref[0, 4 * a + b : 4 * a + b + 1, :] = rest[b][a : a + 1]
    twiddle_ref[1] = rest_ref[2]
    twiddle_ref[2] = rest_ref[1]
    last = rest_ref[3]
    taps = [rest[b][BLOCKS : BLOCKS + 3] for b in range(BLOCKS)]
    taps += [last[BLOCKS + 3 * b : BLOCKS + 3 * b + 3] for b in range(BLOCKS)]
    kernel_ref[...] = jnp.concatenate(taps, 1)


def value_out_body(value_ref, mix_ref, rest_ref, gains_ref, mixing_ref):
    last = rest_ref[3]
    total = value_ref[0].astype(F32)
    for n in range(1, value_ref.shape[0]):
        total = total + value_ref[n].astype(F32)
    owned = mix_ref.shape[1]
    held = owned * 5 // 3
    mixing_ref[0] = unpack_rows(total, owned)
    mixing_ref[1] = mix_ref[0]
    mixing_ref[2] = mix_ref[1]
    one = jnp.concatenate([total[held + k : held + k + 1] for k in range(6)], 1)
    two = jnp.concatenate([last[a : a + 1] for a in range(BLOCKS)], 1)
    gains_ref[...] = jnp.concatenate([one, two], 0)


def hop(values, distance):
    pieces = lax.axis_size("seq")
    return lax.ppermute(values, "seq", [(n, n ^ distance) for n in range(pieces)])


def hop_y(values, distance=0):
    if not distance:
        return lax.ppermute(values, "batch", [(0, 1), (1, 0)])
    apart = 2 * distance + 1
    return lax.ppermute(values, BOTH, [(n, n ^ apart) for n in range(2 * lax.axis_size("seq"))])


def pair_sum(parts, kind):
    wide = [v.astype(F32) for v in parts]
    return ((wide[0] + wide[1]) + (wide[2] + wide[3])).astype(kind)


def held_until(values, *others):
    return lax.optimization_barrier((values, *others))[0]


def added(kept, came, at, kind):
    return (kept[at].astype(F32) + came[at].astype(F32)).astype(kind)


def per_device(
    tokens,
    cotangent,
    gains,
    mixing,
    twiddle,
    expand,
    spread,
    shrink,
    squeeze,
    kernel,
    lifting,
    phases,
    mapping,
    readout,
    damping,
):
    seqs, share, total = tokens.shape
    pieces, groups = lax.axis_size("seq"), lax.axis_size("batch")
    devices = pieces * groups
    place = lax.axis_index("seq")
    me = (place * groups + lax.axis_index("batch")).astype(jnp.int32).reshape(1)
    rows = seqs * share
    length = pieces * share
    width = total // BLOCKS
    wide = expand.shape[2]
    owned = mixing.shape[1]
    octet = devices // BLOCKS
    order = mapping.shape[0]
    fast = pieces == 16 and groups == 2 and owned % 8 == 0 and seqs == 2
    span = width // pieces
    chans = BLOCKS * span
    def exchange(values):
        return lax.all_to_all(values, "seq", 0, 0, tiled=True)

    block = 2 * share
    count = length // block
    table, table_back = packed_tables(block)
    high, low = split_table(table[:block])
    perm = spread_matrix(pieces, span)
    feats = feature_rows(length)
    same = np.tile(np.eye(span, dtype=np.float32), (BLOCKS, BLOCKS))
    pick = np.zeros((8, chans), np.float32)
    for a in range(BLOCKS):
        pick[a, a * span : (a + 1) * span] = 1.0

    expand_own = expand.reshape(2, owned, octet, BLOCKS, owned).swapaxes(2, 3)
    expand_own = expand_own.reshape(2, owned, wide)
    shrink_own = shrink.reshape(BLOCKS, owned, width).swapaxes(0, 1).reshape(owned, BLOCKS * width)
    packed = jnp.concatenate(
        [expand_own[0], expand_own[1], shrink_own, mixing[1], mixing[2]], 1
    )
    if fast:
        z_got = [hop(packed, d) for d in (4, 8, 12)]
        own = pack_rows(held_until(mixing[0], packed))
        own = jnp.broadcast_to(own[None], (devices,) + own.shape)
        inner_part = lax.all_to_all(own, BOTH, 0, 0, tiled=True)
    else:
        inner_part = lax.all_gather(mixing[0], BOTH, axis=0, tiled=True)
        full = lax.all_gather(packed, BOTH, axis=0, tiled=True)
        pair = full[:, 3 * wide :]
        sp_rows = spread.astype(F32).reshape(2, octet, BLOCKS, owned, 16)
        sp_rows = sp_rows.transpose(0, 4, 2, 1, 3).reshape(2, 16, wide)

    tok = tokens.reshape(rows, total)
    cot = cotangent.reshape(rows, total)
    (norm,) = call(norm_body, [((rows, total), BF16)], [tok, gains], 1)

    tw_units, sp_units = twiddle.transpose(0, 2, 3, 1), spread.transpose(0, 2, 3, 1)
    sq_units = squeeze.transpose(1, 2, 0)
    s1, c1, s2, c2, spec, read_own, columns, mix_own = call(
        filter_body,
        [((order, length), BF16)] * 4
        + [((count, chans, 2 * block), F32), ((order, chans), F32), ((chans, 8), F32)]
        + [((chans, chans), BF16)],
        [
            place.astype(jnp.int32).reshape(1), lifting, phases[None], mapping, readout, damping[None],
            kernel[:, :total], tw_units[0], perm, feats, table,
        ],
        7,
        scalars=1,
    )
    if fast:
        held = jnp.stack([packed] + z_got)
        left, right = held[:, :, :1408], held[:, :, 1408:]
        inner_part, left, right, _ = lax.optimization_barrier((inner_part, left, right, spec))

    blocks = (pieces, seqs * chans, share)
    inner, sect_out = call(
        functools.partial(value_body, fast),
        [((total, width), BF16), (blocks, BF16)],
        [inner_part, norm, perm],
        2,
    )
    sect_in = exchange(sect_out)
    tokens = held_until(tokens, sect_out)
    ahead = [(n, n + 1) for n in range(pieces - 1)]
    halo = lax.ppermute(tokens[:, share - 2 :], "seq", ahead)
    if fast:
        got = held_until((hop(left, 2), hop_y(right)), sect_out)
        left, right = jnp.concatenate([left, got[0]], 0), jnp.concatenate([right, got[1]], 0)
        got = (hop_y(left), hop(right, 2))
        left, right = jnp.concatenate([left, got[0]], 0), jnp.concatenate([right, got[1]], 0)
        sect_in, left, right, halo = lax.optimization_barrier((sect_in, left, right, halo))
    spectra = (count, seqs * chans, 2 * block)
    long_blocks = (count, seqs * chans, block)
    conv_scratch = [
        pltpu.VMEM(spectra, F32),
        pltpu.VMEM(spectra, F32),
        pltpu.VMEM((count, chans, block), F32),
        pltpu.VMEM((count, chans, block), F32),
    ]
    long_out, conv_in, signal = call(
        functools.partial(conv_body, length),
        [(blocks, BF16), (long_blocks, BF16), ((chans, seqs * length), BF16)],
        [sect_in, mix_own, columns, spec, high, low, table_back[:, :block]],
        7,
        scratch=conv_scratch,
    )
    long_in = exchange(long_out)
    if fast:
        got = held_until((hop(left, 1), hop(right, 1)), long_out)
        full, pair, sp_rows = call(
            gather_body,
            [
                ((total, 3 * wide + 2 * width), BF16), ((total, 2 * width), BF16),
                ((2, 16, wide), F32),
            ],
            [me, left, got[0], right, got[1], sp_units],
            5,
            scalars=1,
        )

    quad = (BLOCKS, rows, width)
    sect_sw, switch, switch_edge, gate_seq = call(
        functools.partial(switch_body, seqs),
        [(quad, F32), (quad, BF16), ((BLOCKS, 16, width), BF16), (quad, F32)],
        [norm, halo, gains, pair, tw_units[1], kernel],
        1,
    )

    broad = (BLOCKS, rows, wide)
    if fast:
        half_devices = devices // 2
        weight_shapes = [((half_devices, owned, 3 * wide + width), BF16)] * 2
        side_shapes = [((half_devices, owned, width), BF16)] * 2
    else:
        weight_shapes = [((total, 3 * wide + width), F32)]
        side_shapes = [((total, width), F32)]
    (
        layer, lg_out, switch_grad, res_grad, spread_part, squeeze_part, merge_part, gain_part,
        first_rows, *main,
    ) = call(
        functools.partial(middle_body, fast, seqs),
        [
            ((rows, total), BF16), (blocks, BF16), (quad, BF16), (quad, F32),
            ((2, 16, wide), F32), ((16, width), F32), ((16, width), F32), ((BLOCKS, width), F32),
            ((BLOCKS, 2 * seqs, width), BF16),
        ] + weight_shapes,
        [me, long_in, gate_seq, tok, cot, gains, full, pair, tw_units[2], sp_rows, sq_units, perm],
        27,
        scratch=[pltpu.VMEM(broad, F32)] * 5 + [pltpu.VMEM(broad, BF16)] * 3,
        late=(4, 6, 9),
        early=(0, 1, 2, 3),
        scalars=1,
    )
    lg_in = exchange(lg_out)

    after = lax.ppermute(first_rows, "seq", [(to, at) for at, to in ahead])
    n1_sw, small, *side = call(
        functools.partial(switch_back_body, fast, seqs),
        [(quad, F32), ((24, 2 * wide), BF16)] + side_shapes,
        [me, switch_grad, after, switch, switch_edge, sect_sw, pair, tw_units[1], kernel, norm,
         spread_part, squeeze_part, merge_part, gain_part],
        5,
        scalars=1,
    )
    if fast:
        got, side_got, small_got = hop(main[1], 1), hop(side[1], 1), hop(small, 1)
        def sum_shapes(n):
            left, right = ((n + 1, owned, 2 * wide), BF16), ((n, owned, wide + 2 * width), BF16)
            return [left, left, right, right]

        left, left_send, right, right_send = call(
            first_sum_body,
            sum_shapes(half_devices // 2),
            [main[0], got, side[0], side_got, small, small_got],
            4,
        )
        lg_in = held_until(lg_in, left, left_send, right, right_send)

    fg_out, conv_grad, signal_grad = call(
        functools.partial(conv_back_body, length),
        [(blocks, BF16), ((chans, seqs * length), BF16), ((chans, seqs * length), F32)],
        [lg_in, mix_own, columns, spec, high, low, table_back[:, :block]],
        8,
        scratch=conv_scratch,
    )
    fg_in = exchange(fg_out)

    if fast:
        got = held_until((hop_y(left_send), hop(right_send, 2)), fg_out)
        left, left_send, right, right_send = call(
            second_sum_body, sum_shapes(half_devices // 4), [left, got[0], right, got[1]], 3
        )
        lg_in = held_until(lg_in, left, left_send, right, right_send)

    q_rows = chans + 8
    m_rows = order + 8
    (both,) = call(
        functools.partial(filter_back_body, length),
        [((m_rows + q_rows, order), BF16 if fast else F32)],
        [
            lg_in, conv_in, sect_in, signal, conv_grad, signal_grad, s1, c1, s2, c2, read_own,
            mapping, columns, feats, high, low, table_back, same, pick,
        ],
        14,
        scratch=[
            pltpu.VMEM(spectra, F32),
            pltpu.VMEM(long_blocks, F32),
            pltpu.VMEM(long_blocks, F32),
            pltpu.VMEM(spectra, F32),
            pltpu.VMEM((count, chans, 2 * block), F32),
        ],
    )

    if fast:
        got = held_until((hop(left_send, 2), hop_y(right_send)), both)
        shape = ((owned, 5 * wide + 2 * width), BF16)
        own, *sends = call(third_sum_body, [shape] * 4, [left, got[0], right, got[1]], 2)
        z_got = [hop(sent, d) for sent, d in zip(sends, (8, 4, 12))]
        both = added(both, held_until(hop_y(both), own), slice(0, None), BF16)
        fg_in = held_until(fg_in, own, sends, both)

    if fast:
        last_shapes = [((devices, owned * 5 // 3 + 8, 128), BF16)]
    else:
        last_shapes = [((total, width), F32), ((BLOCKS, width), F32)]
    tokens_grad, *pay = call(
        functools.partial(last_body, fast),
        [((rows, total), F32)] + last_shapes,
        [fg_in, perm, inner, norm, n1_sw, res_grad, tok, gains],
        3,
    )
    if fast:
        value_parts = lax.all_to_all(pay[0], BOTH, 0, 0, tiled=True)
    else:
        value_grad = lax.psum_scatter(pay[0], BOTH, scatter_dimension=0, tiled=True)
        gain_one = lax.psum(pay[1], BOTH)

    if fast:
        got = [both] + held_until([hop(both, d) for d in (4, 8, 12)], tokens_grad, z_got)
        m_sum = pair_sum([g[:m_rows] for g in got], BF16)
        both = jnp.concatenate([m_sum] + [g[m_rows:] for g in got], 0)
        z_shapes = [((2, owned, wide), F32), ((2, 16, wide), F32), ((BLOCKS * owned, width), F32)]
        z_shapes += [((2, owned, width), F32), ((BLOCKS, 16, width), F32)]
        expand_grad, spread_sum, shrink_grad, mix_sum, rest_sum = call(
            weights_out_body, z_shapes, [own, *z_got], 4
        )
        got = [both] + held_until([hop(both, d) for d in (2, 1, 3)], rest_sum)
        out_shapes = [(3, 16, width), (3, 2 * total), lifting.shape, (1, order), mapping.shape]
        twiddle_sum, kernel_grad, lifting_grad, phases_grad, mapping_grad, readout_grad = call(
            small_out_body,
            [(shape, F32) for shape in (*out_shapes, readout.shape)],
            [place.astype(jnp.int32).reshape(1), *got, rest_sum, perm],
            3,
            scratch=[pltpu.VMEM((pieces, q_rows, order), F32)],
            scalars=1,
        )
        gains_grad, mixing_grad = call(
            value_out_body,
            [((2, total), F32), ((3, owned, width), F32)],
            [held_until(value_parts, twiddle_sum), mix_sum, rest_sum],
            1,
        )
        squeeze_sum = rest_sum[0]
    else:
        m_sum = lax.psum(both[:m_rows], BOTH)
        q_all = lax.all_gather(lax.psum(both[m_rows:], "batch"), "seq", axis=0, tiled=False)
        main_sum = lax.psum_scatter(main[0], BOTH, scatter_dimension=0, tiled=True)
        switch_own = lax.psum_scatter(side[0], BOTH, scatter_dimension=0, tiled=True)
        small = lax.psum(small.astype(F32), BOTH)
        small = jnp.concatenate([small[:, :wide], small[:, wide : 2 * wide]], 0)

        def natural(grad):
            shape = grad.shape
            grad = grad.reshape(shape[0], BLOCKS, octet, owned).swapaxes(1, 2)
            return grad.reshape(shape)

        expand_grad = jnp.stack([natural(main_sum[:, k * wide : (k + 1) * wide]) for k in range(2)])
        shrink_grad = main_sum[:, 2 * wide : 3 * wide].reshape(owned, BLOCKS, width)
        shrink_grad = shrink_grad.swapaxes(0, 1).reshape(BLOCKS * owned, width)
        mixing_grad = jnp.stack([value_grad, switch_own, main_sum[:, 3 * wide :]])
        spread_sum = jnp.stack([natural(small[:16]), natural(small[16:32])])
        squeeze_sum, merge_sum, switch_sum, tail_sum = small[32:].reshape(16, BLOCKS, width).swapaxes(0, 1)
        value_sum = q_all[:, chans : chans + BLOCKS, :chans].reshape(pieces, BLOCKS, BLOCKS, span)
        value_sum = value_sum.transpose(1, 2, 0, 3).reshape(16, width)
        twiddle_sum = jnp.stack([value_sum, switch_sum, merge_sum])
        taps_value = q_all[:, chans + BLOCKS : chans + BLOCKS + 3, :chans]
        taps_value = taps_value.reshape(pieces, 3, BLOCKS, span).transpose(1, 2, 0, 3)
        taps_sum = tail_sum[BLOCKS:].reshape(BLOCKS, 3, width).swapaxes(0, 1)
        kernel_grad = jnp.concatenate(
            [taps_value.reshape(3, total), taps_sum.reshape(3, total)], 1
        )
        readout_grad = q_all[:, :chans].reshape(pieces, BLOCKS, span, order)
        readout_grad = readout_grad.transpose(3, 1, 0, 2).reshape(order, total)
        gains_grad = jnp.stack([gain_one.reshape(total), tail_sum[:BLOCKS].reshape(total)])
        lifting_grad = m_sum[order : order + lifting.shape[0]]
        phases_grad = m_sum[order + lifting.shape[0]]
        mapping_grad = m_sum[:order]

    def of_units(rows_now):
        lead = rows_now.shape[:-2]
        shaped = rows_now.reshape(*lead, BLOCKS, BLOCKS, rows_now.shape[-1])
        return jnp.moveaxis(shaped, -1, -3)

    return (
        layer.reshape(seqs, share, total),
        tokens_grad.reshape(seqs, share, total),
        gains_grad,
        mixing_grad,
        of_units(twiddle_sum),
        expand_grad,
        of_units(spread_sum),
        shrink_grad,
        of_units(squeeze_sum),
        kernel_grad,
        lifting_grad,
        phases_grad.reshape(order),
        mapping_grad,
        readout_grad,
    )


def solution(mesh):
    return jax.shard_map(
        per_device,
        mesh=mesh,
        in_specs=(
            P("batch", "seq", None),
            P("batch", "seq", None),
            P(),
            P(None, ("seq", "batch"), None),
            P(),
            P(None, ("seq", "batch"), None),
            P(),
            P(("seq", "batch"), None),
            P(),
            P(),
            P(),
            P(),
            P(),
            P(),
            P(),
        ),
        out_specs=(
            P("batch", "seq", None),
            P("batch", "seq", None),
            P(),
            P(None, ("seq", "batch"), None),
            P(),
            P(None, ("seq", "batch"), None),
            P(),
            P(("seq", "batch"), None),
            P(),
            P(),
            P(),
            P(),
            P(),
            P(),
        ),
        check_vma=False,
    )
```

```python
import functools
import math

import jax
import jax.numpy as jnp
import numpy as np
from jax import lax
from jax.experimental import pallas as pl
from jax.experimental.pallas import tpu as pltpu
from jax.sharding import PartitionSpec as P

BLOCKS = 4
BOTH = ("seq", "batch")
F32 = jnp.float32
BF16 = jnp.bfloat16
HIGHEST = lax.Precision.HIGHEST
LIMIT = 52
NN = ((1,), (0,))
NT = ((1,), (1,))
TN = ((0,), (0,))


def mm(left, right, dims=NN, precision=None):
    return lax.dot_general(
        left, right, (dims, ((), ())), preferred_element_type=F32, precision=precision
    )


class Late:
    def __init__(self, source, held, done):
        self.held, self.waiting = held, pltpu.make_async_copy(source, held, done)
        self.waiting.start()

    def ready(self):
        if self.waiting is not None:
            self.waiting.wait()
            self.waiting = None
        return self.held


class Early:
    def __init__(self, target, held, done):
        self.ref, self.copy, self.left = held, pltpu.make_async_copy(held, target, done), False

    def leave(self):
        if not self.left:
            self.copy.start()
            self.left = True


def call(body, outs, operands, micros, scratch=(), scalars=0, limit=LIMIT, late=(), early=()):
    specs = [
        pl.BlockSpec(
            memory_space=pl.ANY if k in late else pltpu.SMEM if k < scalars else pltpu.VMEM
        )
        for k in range(len(operands))
    ]
    out_specs = [
        pl.BlockSpec(memory_space=pl.ANY if k in early else pltpu.VMEM) for k in range(len(outs))
    ]
    staging = [pltpu.VMEM(operands[k].shape, operands[k].dtype) for k in late]
    staging += [pltpu.VMEM(*outs[k]) for k in early]
    count = len(staging)

    def whole(*refs):
        refs = list(refs)
        held = refs[len(operands) + len(outs) :][:count]
        rest = refs[len(operands) + len(outs) + count :]
        if not count:
            body(*refs)
            return
        done, rest = rest[0], rest[1:]
        for n, k in enumerate(late):
            refs[k] = Late(refs[k], held[n], done.at[n])
        for n, k in enumerate(early):
            at = len(operands) + k
            refs[at] = Early(refs[at], held[len(late) + n], done.at[len(late) + n])
        body(*refs[: len(operands) + len(outs)], *rest)
        for k in early:
            refs[len(operands) + k].leave()
        for k in early:
            refs[len(operands) + k].copy.wait()
        for k in late:
            refs[k].ready()

    if count:
        staging.append(pltpu.SemaphoreType.DMA((count,)))
    return pl.pallas_call(
        whole,
        out_shape=[jax.ShapeDtypeStruct(shape, kind) for shape, kind in outs],
        in_specs=specs,
        out_specs=out_specs,
        scratch_shapes=staging + list(scratch),
        compiler_params=pltpu.CompilerParams(vmem_limit_bytes=limit << 20),
        cost_estimate=pl.CostEstimate(
            flops=int(micros * 1.15e9), bytes_accessed=1 << 16, transcendentals=0
        ),
    )(*operands)


def packed_tables(points):
    size = 2 * points
    place = np.arange(size)[:, None].astype(np.int64)
    bins = np.arange(points)[None, :]
    angle = 2.0 * np.pi / size * ((place * bins) % size)
    forward = np.concatenate([np.cos(angle), -np.sin(angle)], 1)
    forward[:, points] = np.where(np.arange(size) % 2 == 0, 1.0, -1.0)
    weight = np.where(np.arange(size) % points == 0, 1.0, 2.0) / size
    backward = (forward * weight[None, :]).T
    return forward.astype(np.float32), np.ascontiguousarray(backward).astype(np.float32)


def split_table(table):
    high = table.astype(jnp.bfloat16)
    low = (table - high.astype(np.float32)).astype(jnp.bfloat16)
    return high, low


def feature_rows(length):
    place = np.arange(length)
    rows = [place / length]
    for harmonic in (1, 2):
        angle = 2.0 * np.pi / length * ((harmonic * place) % length)
        rows += [np.cos(angle), np.sin(angle)]
    rows += [np.ones(length), np.zeros(length), np.zeros(length)]
    return np.stack(rows).astype(np.float32)


def spread_matrix(pieces, span):
    width = pieces * span
    out = np.zeros((BLOCKS, pieces, BLOCKS, span, width), np.float32)
    for b in range(BLOCKS):
        for piece in range(pieces):
            for k in range(span):
                out[b, piece, b, k, piece * span + k] = 1.0
    return out.reshape(BLOCKS, pieces * BLOCKS * span, width).astype(jnp.bfloat16)


def normalize_rows(values):
    centred = values - jnp.mean(values, -1, keepdims=True)
    factor = lax.rsqrt(jnp.mean(centred * centred, -1, keepdims=True) + 1e-05)
    return centred * factor, factor


def sincos(angle):
    turns = (angle * (2.0 / math.pi) + 12582912.0) - 12582912.0
    rest = (angle - turns * 1.5703125) - turns * 4.83826794896619e-4
    square = rest * rest
    sine = rest + rest * square * (
        -1.6666654611e-1 + square * (8.3321608736e-3 + square * -1.9515295891e-4)
    )
    cosine = (
        1.0
        - 0.5 * square
        + square
        * square
        * (4.166664568298827e-2 + square * (-1.388731625493765e-3 + square * 2.443315711809948e-5))
    )
    quarter = turns.astype(jnp.int32)
    odd = jnp.bitwise_and(quarter, 1) == 1
    sine_sign = (1 - jnp.bitwise_and(quarter, 2)).astype(F32)
    cosine_sign = (1 - jnp.bitwise_and(quarter + 1, 2)).astype(F32)
    return (
        jnp.where(odd, cosine, sine) * sine_sign,
        jnp.where(odd, sine, cosine) * cosine_sign,
    )


def parts_of(values):
    width = values.shape[1] // BLOCKS
    return [values[:, k * width : (k + 1) * width] for k in range(BLOCKS)]


def mix(sectioned, rows):
    return [
        sum(sectioned[a] * rows[4 * a + b : 4 * a + b + 1, :] for a in range(BLOCKS))
        for b in range(BLOCKS)
    ]


def unmix(upstream, rows):
    return [
        sum(upstream[b] * rows[4 * a + b : 4 * a + b + 1, :] for b in range(BLOCKS))
        for a in range(BLOCKS)
    ]


def mix_grad(sectioned, upstream):
    return jnp.concatenate(
        [
            jnp.sum(sectioned[a] * upstream[b], 0, keepdims=True)
            for a in range(BLOCKS)
            for b in range(BLOCKS)
        ],
        0,
    )


def lane_of(shape):
    return lax.broadcasted_iota(jnp.int32, shape, len(shape) - 1)


def row_of(shape):
    return lax.broadcasted_iota(jnp.int32, shape, 0)


def time_rows(block_ref, span):
    pieces, rows, _ = block_ref.shape
    return jnp.concatenate(
        [
            block_ref[n].astype(F32)[s * span : (s + 1) * span]
            for s in range(rows // span)
            for n in range(pieces)
        ],
        1,
    )


def later_lanes(values, steps, length):
    total = values.shape[1]
    moved = pltpu.roll(values, total - steps, 1)
    return jnp.where(lane_of(values.shape) % length < length - steps, moved, 0.0)


def earlier_lanes(values, steps, length):
    moved = pltpu.roll(values, steps, 1)
    return jnp.where(lane_of(values.shape) % length >= steps, moved, 0.0)


def to_pieces(lanes_now, out_ref, length):
    pieces, _, width = out_ref.shape
    seqs = lanes_now.shape[1] // length
    for n in range(pieces):
        out_ref[n] = jnp.concatenate(
            [
                lanes_now[:, s * length + n * width : s * length + (n + 1) * width]
                for s in range(seqs)
            ],
            0,
        ).astype(BF16)


def spectrum(flat, high_ref, low_ref, out_ref):
    out = mm(flat, high_ref[...]) + mm(flat, low_ref[...])
    out_ref[...] = out.reshape(out_ref.shape)


def mm2(left, right, dims=NN):
    left_high = left.astype(BF16)
    left_low = (left - left_high.astype(F32)).astype(BF16)
    return mm(left_low, right, dims) + mm(left_high, right, dims)


def mm3(left, right, dims=NN):
    left_high, right_high = left.astype(BF16), right.astype(BF16)
    left_low = (left - left_high.astype(F32)).astype(BF16)
    right_low = (right - right_high.astype(F32)).astype(BF16)
    return (
        mm(left_high, right_low, dims) + mm(left_low, right_high, dims)
    ) + mm(left_high, right_high, dims)


def nyquist_split(spec):
    half = spec.shape[-1] // 2
    real, imaginary = spec[..., :half], spec[..., half:]
    first = lane_of(real.shape) == 0
    return jnp.where(first, 0.0, imaginary), jnp.where(first, imaginary, real)


def norm_body(tok_ref, gains_ref, norm_ref):
    norm = normalize_rows(tok_ref[...].astype(F32))[0] * gains_ref[0:1, :]
    norm_ref[...] = norm.astype(BF16)


def unit_rows(ref):
    return jnp.concatenate([ref[a].astype(F32) for a in range(BLOCKS)], 0)


def filter_body(
    place_ref, lift_ref, phase_ref, map_ref, read_all, damp_all, taps_all, tw_ref, perm_ref, feat_ref,
    table_ref, s1, c1, s2, c2, spec_ref, read_ref, columns_ref, mix_ref,
):
    span = read_ref.shape[1]
    at = pl.ds(pl.multiple_of(place_ref[0] * span, span), span)
    chosen = [perm_ref[b, at, :] for b in range(BLOCKS)]
    width = perm_ref.shape[2]
    read_ref[...] = sum(
        mm(read_all[:, b * width : (b + 1) * width], chosen[b].astype(F32), NT, HIGHEST)
        for b in range(BLOCKS)
    )
    rows = jnp.concatenate([damp_all[...], taps_all[...], jnp.zeros((4, BLOCKS * width), F32)], 0)
    columns = sum(
        mm(chosen[b].astype(F32), rows[:, b * width : (b + 1) * width], NT, HIGHEST)
        for b in range(BLOCKS)
    )
    columns_ref[...] = columns
    factors = unit_rows(tw_ref)
    mix_ref[...] = sum(
        mm((chosen[b] * factors[4 * a + b : 4 * a + b + 1].astype(BF16)), chosen[a], NT)
        for a in range(BLOCKS)
        for b in range(BLOCKS)
    ).astype(BF16)
    lift = jnp.concatenate(
        [lift_ref[...], phase_ref[...], jnp.zeros((7 - lift_ref.shape[0], map_ref.shape[0]), F32)], 0
    )
    sine_one, cosine_one = sincos(mm(lift, feat_ref[...], TN, HIGHEST))
    s1[...] = sine_one.astype(BF16)
    c1[...] = cosine_one.astype(BF16)
    sine_two, cosine_two = sincos(mm(map_ref[...], sine_one, TN, HIGHEST))
    s2[...] = sine_two.astype(BF16)
    c2[...] = cosine_two.astype(BF16)
    shape = (read_ref.shape[1], sine_two.shape[1])
    place = lane_of(shape).astype(F32)
    response = mm(read_ref[...], sine_two, TN, HIGHEST) * jnp.exp(-place * columns[:, 0:1])
    pieces, span, doubled = spec_ref.shape
    width = doubled // 2
    zero = jnp.zeros((span, width), F32)
    rows = []
    for k in range(pieces):
        now = response[:, k * width : (k + 1) * width]
        before = response[:, (k - 1) * width : k * width] if k else zero
        rows.append(
            jnp.concatenate([now, jnp.where(lane_of(before.shape) == 0, 0.0, before)], 1)
        )
    spec = mm3(jnp.concatenate(rows, 0), table_ref[...])
    spec_ref[...] = spec.reshape(pieces, span, doubled)


def value_body(packed, *refs):
    if packed:
        held_ref, norm_ref, perm_ref, full_ref, out_ref = refs
        rows = held_ref.shape[1] * 3 // 5
        share = held_ref.shape[0] // BLOCKS
        inner = []
        for a in range(BLOCKS):
            blocks = []
            for k in range(a * share, (a + 1) * share):
                held = held_ref[k].astype(F32)
                blocks.append(unpack_rows(held, rows))
            inner.append(jnp.concatenate(blocks, 0).astype(BF16))
            full_ref[a * rows * share : (a + 1) * rows * share, :] = inner[a]
    else:
        inner_ref, norm_ref, perm_ref, full_ref, out_ref = refs
        full_ref[...] = inner_ref[...]
        width = full_ref.shape[1]
        inner = [full_ref[a * width : (a + 1) * width, :] for a in range(BLOCKS)]
    norm = parts_of(norm_ref[...])
    first = [mm(norm[a], inner[a]).astype(BF16) for a in range(BLOCKS)]
    send_pieces(first, perm_ref, out_ref)


def pack_rows(values):
    rows = values.shape[0]
    rest = [values[k : k + 8, 128:] for k in range(0, rows, 8)] + [jnp.zeros_like(values[:8, 128:])]
    pairs = [jnp.concatenate(rest[k : k + 2], 1) for k in range(0, rows // 8, 2)]
    return jnp.concatenate([values[:, :128]] + pairs, 0)


def unpack_rows(held, rows):
    rest = []
    for k in range(rows // 8):
        start = rows + 8 * (k // 2)
        rest.append(held[start : start + 8, 64 * (k % 2) : 64 * (k % 2) + 64])
    return jnp.concatenate([held[:rows], jnp.concatenate(rest, 0)], 1)


def gather_body(
    me_ref, left_own, left_other, right_own, right_other, wide_ref, shrink_ref, pair_ref
):
    rows, cut = left_own.shape[1:]
    width = shrink_ref.shape[2]
    first = wide_ref.shape[1]
    last = first + BLOCKS * width
    count = 2 * left_own.shape[0]
    per = 2 if rows % 16 else 1
    for k in range(0, count, per):
        blocks = []
        for owner in range(k, k + per):
            bits = apart_bits(me_ref, owner)
            deep = bits[3] + 2 * bits[4]
            left = bits[0] * 8 + bits[2] * 4 + deep
            right = bits[2] * 8 + bits[0] * 4 + deep
            near = bits[1] == 0
            blocks.append(
                jnp.concatenate(
                    [
                        jnp.where(near, left_own[left].astype(F32), left_other[left].astype(F32)),
                        jnp.where(
                            near, right_own[right].astype(F32), right_other[right].astype(F32)
                        ),
                    ],
                    1,
                )
            )
        block = jnp.concatenate(blocks, 0).astype(BF16)
        wide_ref[k * rows : (k + per) * rows, :] = block[:, :first]
        pair_ref[k * rows : (k + per) * rows, :] = block[:, last:]
        for n, block in enumerate(blocks):
            parts = [block[:, first + g * width : first + (g + 1) * width] for g in range(BLOCKS)]
            at = (k + n) * BLOCKS * rows
            here = slice(at % shrink_ref.shape[1], at % shrink_ref.shape[1] + BLOCKS * rows)
            shrink_ref[at // shrink_ref.shape[1], here, :] = jnp.concatenate(parts, 0).astype(BF16)


def send_pieces(parts, perm_ref, out_ref):
    pieces, rows, width = out_ref.shape
    seqs = parts[0].shape[0] // width
    span = rows // seqs
    turned = [
        sum(
            mm(perm_ref[k], parts[k][s * width : (s + 1) * width], NT) for k in range(BLOCKS)
        )
        for s in range(seqs)
    ]
    for n in range(pieces):
        out_ref[n] = jnp.concatenate(
            [turned[s][n * span : (n + 1) * span] for s in range(seqs)], 0
        ).astype(BF16)


def receive_pieces(in_ref, perm_ref):
    pieces, rows, width = in_ref.shape
    seqs = rows * pieces // (BLOCKS * perm_ref.shape[2])
    span = rows // seqs
    held = [in_ref[n].astype(F32) for n in range(pieces)]
    turned = [
        jnp.concatenate([h[s * span : (s + 1) * span] for h in held], 0).T.astype(BF16)
        for s in range(seqs)
    ]
    return [
        jnp.concatenate([mm(turned[s], perm_ref[k]) for s in range(seqs)], 0)
        for k in range(BLOCKS)
    ]


def earlier_rows(values, halo, steps):
    moved = pltpu.roll(values, steps, 0)
    row = row_of(values.shape)
    for k in range(steps):
        moved = jnp.where(row == k, halo[2 - steps + k : 3 - steps + k], moved)
    return moved


def later_rows(values, halo, steps):
    count = values.shape[0]
    moved = pltpu.roll(values, count - steps, 0)
    row = row_of(values.shape)
    for k in range(steps):
        moved = jnp.where(row == count - steps + k, halo[k : k + 1], moved)
    return moved


def per_sequence(function, values, halo, seqs, steps):
    count = values.shape[0] // seqs
    return jnp.concatenate(
        [
            function(values[s * count : (s + 1) * count], halo[2 * s : 2 * s + 2], steps)
            for s in range(seqs)
        ],
        0,
    )


def switch_body(
    seqs, norm_ref, halo_ref, gains_ref, full_ref, tw_ref, taps_ref, sect_ref, sw_ref, sh_ref, gate_ref
):
    width = norm_ref.shape[1] // BLOCKS
    edge = jnp.concatenate([halo_ref[s].astype(F32) for s in range(seqs)], 0)
    edge = jnp.concatenate([edge, jnp.zeros((16 - 2 * seqs, edge.shape[1]), F32)], 0)
    edge_norm = normalize_rows(edge)[0] * gains_ref[0:1, :]
    norm, halo = parts_of(norm_ref[...]), parts_of(edge_norm.astype(BF16))
    inner = [full_ref[a * width : (a + 1) * width, :][:, :width] for a in range(BLOCKS)]
    first = [mm(norm[a], inner[a]) for a in range(BLOCKS)]
    for a in range(BLOCKS):
        sect_ref[a] = first[a]
    rows = unit_rows(tw_ref)
    all_taps = parts_of(taps_ref[...][:, BLOCKS * width :])
    switch = mix(first, rows)
    edge = mix([mm(halo[a], inner[a]) for a in range(BLOCKS)], rows)
    for b in range(BLOCKS):
        sw_ref[b] = switch[b].astype(BF16)
        sh_ref[b] = edge[b].astype(BF16)
        now = switch[b].astype(BF16).astype(F32)
        before = edge[b].astype(BF16).astype(F32)
        taps = all_taps[b]
        gate_ref[b] = (
            taps[0:1] * now
            + taps[1:2] * per_sequence(earlier_rows, now, before, seqs, 1)
            + taps[2:3] * per_sequence(earlier_rows, now, before, seqs, 2)
        )


def loop(start, stop, body, carry, unrolled):
    if not unrolled:
        return lax.fori_loop(start, stop, body, carry)
    for step in range(start, stop):
        carry = body(step, carry)
    return carry


def bins_of(half):
    return [(slice(k, k + 128), slice(half + k, half + k + 128)) for k in range(0, half, 128)]


def convolve(spec_ref, b_ref, c_ref, x_ref, y_ref):
    pieces, rows, doubled = x_ref.shape
    span = spec_ref.shape[1]
    zero = jnp.zeros((span, 128), F32)
    parts = [slice(k, k + span) for k in range(0, rows, span)]
    for low, up in bins_of(doubled // 2):

        def outer(i, carry, low=low, up=up):
            def inner(j, totals):
                k = i - j
                a_now, b_now, c_now = spec_ref[k, :, low], b_ref[k, :, low], c_ref[k, :, low]
                out = []
                for s, at in enumerate(parts):
                    real, imag = x_ref[j, at, low], x_ref[j, at, up]
                    out.append(totals[2 * s] + a_now * real - b_now * imag)
                    out.append(totals[2 * s + 1] + b_now * real + c_now * imag)
                return tuple(out)

            totals = loop(0, i + 1, inner, (zero,) * (2 * len(parts)), pieces <= 8)
            for s, at in enumerate(parts):
                y_ref[i, at, low] = totals[2 * s]
                y_ref[i, at, up] = totals[2 * s + 1]
            return carry

        loop(0, pieces, outer, 0, pieces <= 8)


def correlate(spec_ref, b_ref, c_ref, g_ref, y_ref):
    pieces, rows, doubled = g_ref.shape
    span = spec_ref.shape[1]
    zero = jnp.zeros((span, 128), F32)
    parts = [slice(k, k + span) for k in range(0, rows, span)]
    for low, up in bins_of(doubled // 2):

        def outer(j, carry, low=low, up=up):
            def inner(i, totals):
                k = i - j
                a_now, b_now, c_now = spec_ref[k, :, low], b_ref[k, :, low], c_ref[k, :, low]
                out = []
                for s, at in enumerate(parts):
                    real, imag = g_ref[i, at, low], g_ref[i, at, up]
                    out.append(totals[2 * s] + a_now * real + b_now * imag)
                    out.append(totals[2 * s + 1] + c_now * imag - b_now * real)
                return tuple(out)

            totals = loop(j, pieces, inner, (zero,) * (2 * len(parts)), pieces <= 8)
            for s, at in enumerate(parts):
                y_ref[j, at, low] = totals[2 * s]
                y_ref[j, at, up] = totals[2 * s + 1]
            return carry

        loop(0, pieces, outer, 0, pieces <= 8)


def block_rows(piece_ref, block):
    pieces, _, width = piece_ref.shape
    each = block // width
    return jnp.concatenate(
        [
            jnp.concatenate([piece_ref[n + k] for k in range(each)], 1)
            for n in range(0, pieces, each)
        ],
        0,
    )


def conv_body(
    length, sect_ref, mix_ref, taps_ref, spec_ref, high_ref, low_ref, back_ref,
    out_ref, cin_ref, signal_ref, x_ref, y_ref, b_ref, c_ref,
):
    span = spec_ref.shape[1]
    lanes_now = time_rows(sect_ref, span).astype(BF16)
    signal = mm(mix_ref[...], lanes_now).astype(BF16)
    signal_ref[...] = signal
    signal = signal.astype(F32)
    conv_in = (
        taps_ref[:, 1:2] * signal
        + taps_ref[:, 2:3] * earlier_lanes(signal, 1, length)
        + taps_ref[:, 3:4] * earlier_lanes(signal, 2, length)
    )
    to_pieces(conv_in, cin_ref, length)
    spectrum(cin_ref[...].reshape(-1, cin_ref.shape[2]), high_ref, low_ref, x_ref)
    b_ref[...], c_ref[...] = nyquist_split(spec_ref[...])
    convolve(spec_ref, b_ref, c_ref, x_ref, y_ref)
    pieces, rows, doubled = y_ref.shape
    out = mm3(y_ref[...].reshape(pieces * rows, doubled), back_ref[...]).astype(BF16)
    width = out_ref.shape[2]
    each = doubled // 2 // width
    for n in range(pieces):
        for k in range(each):
            out_ref[n * each + k] = out[n * rows : (n + 1) * rows, k * width : (k + 1) * width]


def middle_body(
    fast, owned, seqs, me_ref, long_ref, gate_ref, tok_ref, cot_ref, gains_ref, full_ref, shrink_ref, pair_ref,
    tw_ref, spread_ref, sq_ref, perm_ref, layer_ref, lg_ref, swg_ref, res_ref, spg_ref, sqg_ref, twg_ref, gain_ref, edge_ref, *refs,
):
    *weight_outs, fg, fu, act, ug, hg, hid_ref, fgate_ref, fup_ref, sp_ref = refs
    for k in range(2):
        sp_ref[k] = unit_rows(spread_ref.at[k])
    rows, total = tok_ref.shape
    width = total // BLOCKS
    wide = fg.shape[2]
    tw_rows, sq_rows = unit_rows(tw_ref), unit_rows(sq_ref)
    gate = [gate_ref[b] for b in range(BLOCKS)]
    long_out = receive_pieces(long_ref, perm_ref)
    gated = [(gate[b] * long_out[b]).astype(BF16) for b in range(BLOCKS)]
    at = [slice(a * width, (a + 1) * width) for a in range(BLOCKS)]
    merge = [pair_ref[at[a], :][:, width:] for a in range(BLOCKS)]
    sect_merge = [mm(gated[a], merge[a]) for a in range(BLOCKS)]
    merged = mix(sect_merge, tw_rows)
    tokens = parts_of(tok_ref[...].astype(F32))
    residual = [tokens[b] + merged[b] for b in range(BLOCKS)]
    mean = sum(jnp.sum(r, -1, keepdims=True) for r in residual) / total
    centred = [r - mean for r in residual]
    variance = sum(jnp.sum(c * c, -1, keepdims=True) for c in centred) / total
    factor = lax.rsqrt(variance + 1e-05)
    normed = [c * factor for c in centred]
    gain = parts_of(gains_ref[1:2, :])
    norm_two = [(normed[a] * gain[a]).astype(BF16) for a in range(BLOCKS)]
    full_ref = full_ref.ready()
    for a in range(BLOCKS):
        fg[a] = mm(norm_two[a], full_ref[at[a], :wide])
        fu[a] = mm(norm_two[a], full_ref[at[a], wide : 2 * wide])

    step = 32
    lanes = 128

    def forward_lane(l, carry):
        here = pl.ds(pl.multiple_of(l * lanes, lanes), lanes)

        def forward_row(r, inner_carry):
            down = pl.ds(pl.multiple_of(r * step, step), step)
            gate_pre = mix([fg[a, down, here] for a in range(BLOCKS)], sp_ref[0, :, here])
            held = []
            for v in gate_pre:
                square = v * v
                half = 0.5 + 0.5 * jnp.tanh(v * (0.7978845608 + 0.0356774081 * square))
                active = v * half
                steep = 1.5957691216 + 0.2140644488 * square
                held.append((active, half + active * (1.0 - half) * steep))
            up_pre = mix([fu[a, down, here] for a in range(BLOCKS)], sp_ref[1, :, here])
            for b in range(BLOCKS):
                active, slope = held[b]
                hid_ref[b, down, here] = (active * up_pre[b]).astype(BF16)
                act[b, down, here] = active
                ug[b, down, here] = up_pre[b] * slope
            return inner_carry

        return lax.fori_loop(0, rows // step, forward_row, carry)

    lax.fori_loop(0, wide // lanes, forward_lane, 0)

    shrink_ref = shrink_ref.ready()
    shrink = [shrink_ref[a] for a in range(BLOCKS)]
    sect_down = [mm(hid_ref[a], shrink[a]) for a in range(BLOCKS)]
    lowered = mix(sect_down, sq_rows)
    layer_ref.ref[...] = jnp.concatenate(
        [(residual[b] + lowered[b]).astype(BF16) for b in range(BLOCKS)], 1
    )
    layer_ref.leave()
    upstream = parts_of(cot_ref.ready()[...].astype(F32))
    sqg_ref[...] = mix_grad(sect_down, upstream)
    back_down = unmix(upstream, sq_rows)
    back_down = [v.astype(BF16) for v in back_down]
    for a in range(BLOCKS):
        hg[a] = mm(back_down[a], shrink[a], NT)

    def backward_lane(l, carry):
        here = pl.ds(pl.multiple_of(l * lanes, lanes), lanes)
        zero = jnp.zeros((8, lanes), F32)
        for k, (held, slopes, out_ref) in enumerate(((fg, ug, fgate_ref), (fu, act, fup_ref))):

            def backward_row(r, sums, k=k, held=held, slopes=slopes, out_ref=out_ref):
                down = pl.ds(pl.multiple_of(r * step, step), step)
                grads = [hg[b, down, here] * slopes[b, down, here] for b in range(BLOCKS)]
                for a, value in enumerate(unmix(grads, sp_ref[k, :, here])):
                    out_ref[a, down, here] = value.astype(BF16)
                out = []
                for a in range(BLOCKS):
                    value = held[a, down, here]
                    for b in range(BLOCKS):
                        product = value * grads[b]
                        for n in range(0, step, 16):
                            pair = product[n : n + 8] + product[n + 8 : n + 16]
                            part = pair if n == 0 else part + pair
                        out.append(sums[4 * a + b] + part)
                return tuple(out)

            sums = lax.fori_loop(0, rows // step, backward_row, (zero,) * 16)
            for n in range(16):
                spg_ref[k, pl.ds(n, 1), here] = jnp.sum(sums[n], 0, keepdims=True)
        return carry

    lax.fori_loop(0, wide // lanes, backward_lane, 0)

    n2_grad = [
        mm(fgate_ref[a], full_ref[at[a], :wide], NT)
        + mm(fup_ref[a], full_ref[at[a], wide : 2 * wide], NT)
        for a in range(BLOCKS)
    ]
    scaled = [n2_grad[a] * gain[a] for a in range(BLOCKS)]
    plain = sum(jnp.sum(v, -1, keepdims=True) for v in scaled) / total
    joint = sum(jnp.sum(scaled[a] * normed[a], -1, keepdims=True) for a in range(BLOCKS)) / total
    res_grad = [
        upstream[a] + factor * (scaled[a] - plain - normed[a] * joint) for a in range(BLOCKS)
    ]
    gain_ref[...] = jnp.concatenate(
        [jnp.sum(n2_grad[a] * normed[a], 0, keepdims=True) for a in range(BLOCKS)], 0
    )
    for a in range(BLOCKS):
        res_ref.ref[a] = res_grad[a]
    res_ref.leave()
    twg_ref[...] = mix_grad(sect_merge, res_grad)
    back_merge = [v.astype(BF16) for v in unmix(res_grad, tw_rows)]
    long_grad = []
    for a in range(BLOCKS):
        gated_grad = mm(back_merge[a], merge[a], NT)
        long_grad.append((gated_grad * gate[a]).astype(BF16))
        now = (gated_grad * long_out[a]).astype(BF16)
        swg_ref.ref[a] = now
        share = rows // seqs
        edge_ref[a] = jnp.concatenate([now[s * share : s * share + 2] for s in range(seqs)], 0)
    swg_ref.leave()
    send_pieces(long_grad, perm_ref, lg_ref.ref)
    lg_ref.leave()

    for a in range(BLOCKS):
        from_hidden = mm(hid_ref[a], back_down[a], TN)
        group = BLOCKS * owned
        down = [
            jnp.concatenate(
                [
                    from_hidden[o + g * owned : o + (g + 1) * owned]
                    for o in range(0, wide, group)
                ],
                0,
            )
            for g in range(BLOCKS)
        ]
        held = jnp.concatenate(
            [mm(norm_two[a], fgate_ref[a], TN), mm(norm_two[a], fup_ref[a], TN)]
            + down
            + [mm(gated[a], back_merge[a], TN)],
            1,
        )

        def block_of(k, count, held=held):
            return held[k * count : (k + 1) * count]

        outs = weight_outs if fast else (weight_outs[0], owned)
        put_blocks(fast, me_ref, outs, a, block_of, width, 2 * wide)


def switch_back_body(
    fast, owned, seqs, me_ref, swg_ref, next_ref, sw_ref, sh_ref, sect_ref, full_ref, tw_ref, taps_ref,
    norm_ref, spg_ref, sqg_ref, mg_ref, gain_ref, n1_ref, small_ref, *outs,
):
    width = swg_ref.shape[2]
    all_taps = parts_of(taps_ref[...][:, BLOCKS * width :])
    back, taps_grad = [], []
    for b in range(BLOCKS):
        grad = swg_ref[b].astype(F32)
        after = next_ref[b].astype(F32)
        taps = all_taps[b]
        back.append(
            taps[0:1] * grad
            + taps[1:2] * per_sequence(later_rows, grad, after, seqs, 1)
            + taps[2:3] * per_sequence(later_rows, grad, after, seqs, 2)
        )
        now, before = sw_ref[b].astype(F32), sh_ref[b].astype(F32)
        shifted = [now] + [per_sequence(earlier_rows, now, before, seqs, m) for m in (1, 2)]
        taps_grad += [jnp.sum(value * grad, 0, keepdims=True) for value in shifted]
    tw_grad = mix_grad([sect_ref[a] for a in range(BLOCKS)], back)
    rest = [sqg_ref[...], mg_ref[...], tw_grad, jnp.concatenate([gain_ref[...]] + taps_grad, 0)]
    small = jnp.concatenate([spg_ref[0], spg_ref[1], jnp.concatenate(rest, 1)], 0)
    count = small_ref.shape[0]
    small_ref[...] = jnp.concatenate([small[:count], small[count:]], 1).astype(BF16)
    first = unmix(back, unit_rows(tw_ref))
    norm = parts_of(norm_ref[...])
    for a in range(BLOCKS):
        now = first[a].astype(BF16)
        n1_ref[a] = mm(now, full_ref[a * width : (a + 1) * width, :][:, :width], NT)
        held = mm(norm[a], now, TN)

        def block_of(k, count, held=held):
            return held[k * count : (k + 1) * count]

        put_blocks(fast, me_ref, outs if fast else (outs[0], owned), a, block_of, width, 0)


def apart_bits(me_ref, owner):
    apart = jnp.bitwise_xor(me_ref[0], owner)
    return [jnp.bitwise_and(lax.shift_right_logical(apart, n), 1) for n in range(5)]


def put_blocks(fast, me_ref, outs, a, block_of, width, start):
    rows = outs[0].shape[-2] if fast else outs[1]
    for k in range(width // rows):
        block = block_of(k, rows)
        if not fast:
            outs[0][a * width + k * rows : a * width + (k + 1) * rows, :] = block
            continue
        keep_ref, send_ref = outs
        block = block.astype(BF16)
        bits = apart_bits(me_ref, a * (width // rows) + k)
        deep = bits[3] * 2 + bits[4]
        for ref, core in ((keep_ref, 0), (send_ref, 1)):

            @pl.when(bits[1] == core)
            def _(ref=ref, block=block, bits=bits, deep=deep):
                if start:
                    ref[bits[0] * 8 + bits[2] * 4 + deep, :, :start] = block[:, :start]
                ref[bits[2] * 8 + bits[0] * 4 + deep, :, start:] = block[:, start:]


def conv_back_body(
    length, g_ref, mix_ref, taps_ref, spec_ref, high_ref, low_ref, back_ref,
    out_ref, cg_ref, sg_ref, x_ref, y_ref, b_ref, c_ref,
):
    span = spec_ref.shape[1]
    spectrum(block_rows(g_ref, x_ref.shape[2] // 2), high_ref, low_ref, x_ref)
    b_ref[...], c_ref[...] = nyquist_split(spec_ref[...])
    correlate(spec_ref, b_ref, c_ref, x_ref, y_ref)
    pieces, rows, doubled = y_ref.shape
    flat = mm3(y_ref[...].reshape(pieces * rows, doubled), back_ref[...])
    flat = flat.astype(BF16).astype(F32)
    grad = jnp.concatenate(
        [
            flat[n * rows + s * span : n * rows + (s + 1) * span]
            for s in range(rows // span)
            for n in range(pieces)
        ],
        1,
    )
    cg_ref[...] = grad.astype(BF16)
    signal_grad = (
        taps_ref[:, 1:2] * grad
        + taps_ref[:, 2:3] * later_lanes(grad, 1, length)
        + taps_ref[:, 3:4] * later_lanes(grad, 2, length)
    )
    sg_ref[...] = signal_grad
    to_pieces(mm(mix_ref[...].astype(F32), signal_grad, TN, HIGHEST), out_ref, length)


def filter_back_body(
    length, g_ref, cin_ref, sect_ref, signal_ref, cg_ref, sg_ref, s1, c1, s2, c2, read_ref, map_ref,
    damp_ref, feat_ref, high_ref, low_ref, back_ref, same_ref, pick_ref,
    out_ref, x_ref, b_ref, c_ref, gs_ref, p_ref,
):
    pieces, span, doubled = p_ref.shape
    half = doubled // 2
    spectrum(cin_ref[...].reshape(-1, half), high_ref, low_ref, x_ref)
    b_ref[...], c_ref[...] = nyquist_split(x_ref[...])
    spectrum(block_rows(g_ref, half), high_ref, low_ref, gs_ref)
    seqs = x_ref.shape[1] // span
    zero = jnp.zeros((span, 128), F32)
    parts = [slice(k, k + span) for k in range(0, seqs * span, span)]
    for low, up in bins_of(half):

        def outer(k, carry, low=low, up=up):
            def inner(j, totals):
                real, imag = totals
                for at in parts:
                    a_now, b_now, c_now = x_ref[j, at, low], b_ref[j, at, low], c_ref[j, at, low]
                    g_real, g_imag = gs_ref[j + k, at, low], gs_ref[j + k, at, up]
                    real = real + a_now * g_real + b_now * g_imag
                    imag = imag + c_now * g_imag - b_now * g_real
                return real, imag

            real, imag = loop(0, pieces - k, inner, (zero, zero), pieces <= 8)
            p_ref[k, :, low] = real
            p_ref[k, :, up] = imag
            return carry

        loop(0, pieces, outer, 0, pieces <= 8)
    flat = mm3(p_ref[...].reshape(pieces * span, doubled), back_ref[...])
    chunks = []
    for k in range(pieces):
        now = flat[k * span : (k + 1) * span, :half]
        if k + 1 < pieces:
            after = flat[(k + 1) * span : (k + 2) * span, half:]
            now = now + jnp.where(lane_of(after.shape) == 0, 0.0, after)
        chunks.append(now)
    response_grad = jnp.concatenate(chunks, 1)
    place = lane_of(response_grad.shape).astype(F32)
    response_grad = response_grad * jnp.exp(-place * damp_ref[:, 0:1])
    readout_grad = mm2(response_grad, s2[...], NT)
    pre_two = mm3(read_ref[...], response_grad) * c2[...].astype(F32)
    order = s1.shape[0]
    high = pre_two.astype(BF16)
    low = (pre_two - high.astype(F32)).astype(BF16)
    mapping_grad = mm(s1[...], low, NT) + mm(s1[...], high, NT)
    pre_one = mm3(map_ref[...], pre_two) * c1[...].astype(F32)
    lift_grad = mm3(feat_ref[...], pre_one, NT)

    sect = time_rows(sect_ref, span).astype(BF16)
    high = sg_ref[...].astype(BF16)
    low = (sg_ref[...] - high.astype(F32)).astype(BF16)
    tw = (mm(sect, low, NT) + mm(sect, high, NT)) * same_ref[...]
    tw = mm(pick_ref[...], tw, NN, HIGHEST)
    cg = cg_ref[...].astype(F32)
    signal = signal_ref[...].astype(F32)
    taps = []
    for m in range(3):
        moved = signal if m == 0 else earlier_lanes(signal, m, length)
        taps.append(jnp.sum(moved * cg, 1, keepdims=True))
    column = lane_of((span, 128))
    columns = sum(jnp.where(column == BLOCKS + m, taps[m], 0.0) for m in range(3))
    tw = tw + columns.T[: tw.shape[0], :span]
    tw = jnp.concatenate([tw, jnp.zeros((8, order - span), F32)], 1)
    out = jnp.concatenate([mapping_grad, lift_grad, readout_grad, tw], 0)
    out_ref[...] = out.astype(out_ref.dtype)


def last_body(
    fast, fg_ref, perm_ref, inner_ref, norm_ref, n1_ref, res_ref, tok_ref, gains_ref, out_ref, *pay
):
    width = inner_ref.shape[1]
    first = [v.astype(BF16) for v in receive_pieces(fg_ref, perm_ref)]
    norm = parts_of(norm_ref[...])
    normed, factor = normalize_rows(tok_ref[...].astype(F32))
    normed = parts_of(normed)
    gain = parts_of(gains_ref[0:1, :])
    grads = [
        mm(first[a], inner_ref[a * width : (a + 1) * width, :], NT) + n1_ref[a]
        for a in range(BLOCKS)
    ]
    scaled = [grads[a] * gain[a] for a in range(BLOCKS)]
    total = width * BLOCKS
    plain = sum(jnp.sum(v, -1, keepdims=True) for v in scaled) / total
    joint = sum(jnp.sum(scaled[a] * normed[a], -1, keepdims=True) for a in range(BLOCKS)) / total
    out_ref[...] = jnp.concatenate(
        [res_ref[a] + factor * (scaled[a] - plain - normed[a] * joint) for a in range(BLOCKS)], 1
    )
    gain_grad = [jnp.sum(grads[a] * normed[a], 0, keepdims=True) for a in range(BLOCKS)]
    weight = [mm(norm[a], first[a], TN) for a in range(BLOCKS)]
    if not fast:
        for a in range(BLOCKS):
            pay[0][a * width : (a + 1) * width, :] = weight[a]
            pay[1][a : a + 1, :] = gain_grad[a]
        return
    count, rows, _ = pay[0].shape
    share = count // BLOCKS
    held = (rows - 8) * 3 // 5
    flat = jnp.concatenate(gain_grad, 1)
    tail = [flat[:, k : k + 128] for k in range(0, total, 128)]
    tail = jnp.concatenate(tail + [jnp.zeros((8 - len(tail), 128), F32)], 0)
    for a in range(BLOCKS):
        for k in range(share):
            block = pack_rows(weight[a][k * held : (k + 1) * held])
            pay[0][a * share + k] = jnp.concatenate([block, tail], 0).astype(BF16)


def first_sum_body(
    keep_ref, got_ref, side_ref, side_got, small_ref, small_got, left_keep, left_send, right_keep, right_send
):
    n, _, cut = left_keep.shape
    n -= 1
    for k in range(2 * n):
        main = keep_ref[k].astype(F32) + got_ref[k].astype(F32)
        side = side_ref[k].astype(F32) + side_got[k].astype(F32)
        right = jnp.concatenate([main[:, cut:], side], 1).astype(BF16)
        left_out, right_out = (left_keep, right_keep) if k < n else (left_send, right_send)
        left_out[k % n] = main[:, :cut].astype(BF16)
        right_out[k % n] = right
    small = (small_ref[...].astype(F32) + small_got[...].astype(F32)).astype(BF16)
    left_keep[n] = small
    left_send[n] = small


def second_sum_body(
    left_ref, left_got, right_ref, right_got, left_keep, left_send, right_keep, right_send
):
    n = right_keep.shape[0]
    for k in range(2 * n):
        left = (left_ref[k].astype(F32) + left_got[k].astype(F32)).astype(BF16)
        right = (right_ref[k].astype(F32) + right_got[k].astype(F32)).astype(BF16)
        left_out, right_out = (left_keep, right_keep) if k < n else (left_send, right_send)
        left_out[k % n] = left
        right_out[k % n] = right
    small = (left_ref[2 * n].astype(F32) + left_got[2 * n].astype(F32)).astype(BF16)
    left_keep[n] = small
    left_send[n] = small


def third_sum_body(left_ref, left_got, right_ref, right_got, *outs):
    left = [(left_ref[k].astype(F32) + left_got[k].astype(F32)).astype(BF16) for k in range(5)]
    right = [(right_ref[k].astype(F32) + right_got[k].astype(F32)).astype(BF16) for k in range(4)]
    for k, out_ref in enumerate(outs):
        out_ref[...] = jnp.concatenate([left[k], right[k], left[4]], 1)


def weights_out_body(
    own_ref, one_ref, two_ref, three_ref, expand_ref, spread_ref, shrink_ref, mix_ref, rest_ref
):
    parts = [ref[...].astype(F32) for ref in (own_ref, one_ref, two_ref, three_ref)]
    held = (parts[0] + parts[1]) + (parts[2] + parts[3])
    owned, wide = expand_ref.shape[1:]
    width = mix_ref.shape[2]
    for k in range(2):
        expand_ref[k] = held[:, k * wide : (k + 1) * wide]
        start = 2 * wide + BLOCKS * width + k * width
        mix_ref[1 - k] = held[:, start : start + width]
    for g in range(BLOCKS):
        start = 2 * wide + g * width
        shrink_ref[g * owned : (g + 1) * owned, :] = held[:, start : start + width]
    start = 3 * wide + 2 * width
    small = jnp.concatenate([held[:, start : start + wide], held[:, start + wide :]], 0)
    for k in range(2):
        spread_ref[k] = small[16 * k : 16 * k + 16]
    for k in range(BLOCKS):
        rest_ref[k] = small[32:, k * width : (k + 1) * width]


def small_out_body(
    place_ref, own_ref, one_ref, two_ref, three_ref, rest_ref, perm_ref, twiddle_ref, kernel_ref, lift_ref, phase_ref, map_ref, read_ref, q_ref,
):
    order = map_ref.shape[0]
    m_rows, q_rows = order + 8, q_ref.shape[1]
    chans = q_rows - 8
    pieces = q_ref.shape[0]
    width = perm_ref.shape[2]
    parts = [ref[...] for ref in (own_ref, one_ref, two_ref, three_ref)]
    sums = [part[:m_rows].astype(F32) for part in parts]
    m_sum = (sums[0] + sums[1]) + (sums[2] + sums[3])
    map_ref[...] = m_sum[:order]
    lift_ref[...] = m_sum[order : order + lift_ref.shape[0]]
    phase_ref[...] = m_sum[order + lift_ref.shape[0] : order + lift_ref.shape[0] + 1]
    for k, outer in enumerate((0, 2, 1, 3)):
        for n, inner in enumerate((0, 4, 8, 12)):
            start = m_rows + n * q_rows
            q_ref[jnp.bitwise_xor(place_ref[0], outer ^ inner)] = parts[k][
                start : start + q_rows
            ].astype(F32)
    tall = jnp.concatenate([q_ref[n, :chans] for n in range(pieces)], 0).astype(BF16)
    broad = jnp.concatenate([q_ref[n, chans:, :chans] for n in range(pieces)], 1).astype(BF16)
    rest = [mm(broad, perm_ref[b]) for b in range(BLOCKS)]
    read_ref[...] = jnp.concatenate([mm(tall, perm_ref[b], TN) for b in range(BLOCKS)], 1)
    for a in range(BLOCKS):
        for b in range(BLOCKS):
            twiddle_ref[0, 4 * a + b : 4 * a + b + 1, :] = rest[b][a : a + 1]
    twiddle_ref[1] = rest_ref[2]
    twiddle_ref[2] = rest_ref[1]
    last = rest_ref[3]
    taps = [rest[b][BLOCKS : BLOCKS + 3] for b in range(BLOCKS)]
    taps += [last[BLOCKS + 3 * b : BLOCKS + 3 * b + 3] for b in range(BLOCKS)]
    kernel_ref[...] = jnp.concatenate(taps, 1)


def value_out_body(value_ref, mix_ref, rest_ref, gains_ref, mixing_ref):
    last = rest_ref[3]
    total = value_ref[0].astype(F32)
    for n in range(1, value_ref.shape[0]):
        total = total + value_ref[n].astype(F32)
    owned = mix_ref.shape[1]
    held = owned * 5 // 3
    mixing_ref[0] = unpack_rows(total, owned)
    mixing_ref[1] = mix_ref[0]
    mixing_ref[2] = mix_ref[1]
    one = jnp.concatenate([total[held + k : held + k + 1] for k in range(6)], 1)
    two = jnp.concatenate([last[a : a + 1] for a in range(BLOCKS)], 1)
    gains_ref[...] = jnp.concatenate([one, two], 0)


def hop(values, distance):
    pieces = lax.axis_size("seq")
    return lax.ppermute(values, "seq", [(n, n ^ distance) for n in range(pieces)])


def hop_y(values, distance=0):
    if not distance:
        return lax.ppermute(values, "batch", [(0, 1), (1, 0)])
    apart = 2 * distance + 1
    return lax.ppermute(values, BOTH, [(n, n ^ apart) for n in range(2 * lax.axis_size("seq"))])


def pair_sum(parts, kind):
    wide = [v.astype(F32) for v in parts]
    return ((wide[0] + wide[1]) + (wide[2] + wide[3])).astype(kind)


def held_until(values, *others):
    return lax.optimization_barrier((values, *others))[0]


def added(kept, came, at, kind):
    return (kept[at].astype(F32) + came[at].astype(F32)).astype(kind)


def per_device(
    tokens,
    cotangent,
    gains,
    mixing,
    twiddle,
    expand,
    spread,
    shrink,
    squeeze,
    kernel,
    lifting,
    phases,
    mapping,
    readout,
    damping,
):
    seqs, share, total = tokens.shape
    pieces, groups = lax.axis_size("seq"), lax.axis_size("batch")
    devices = pieces * groups
    place = lax.axis_index("seq")
    me = (place * groups + lax.axis_index("batch")).astype(jnp.int32).reshape(1)
    rows = seqs * share
    length = pieces * share
    width = total // BLOCKS
    wide = expand.shape[2]
    owned = mixing.shape[1]
    octet = devices // BLOCKS
    order = mapping.shape[0]
    fast = pieces == 16 and groups == 2 and owned % 8 == 0 and seqs == 2
    span = width // pieces
    chans = BLOCKS * span
    def exchange(values):
        return lax.all_to_all(values, "seq", 0, 0, tiled=True)

    block = 2 * share
    count = length // block
    table, table_back = packed_tables(block)
    high, low = split_table(table[:block])
    perm = spread_matrix(pieces, span)
    feats = feature_rows(length)
    same = np.tile(np.eye(span, dtype=np.float32), (BLOCKS, BLOCKS))
    pick = np.zeros((8, chans), np.float32)
    for a in range(BLOCKS):
        pick[a, a * span : (a + 1) * span] = 1.0

    shrink_own = shrink.reshape(BLOCKS, owned, width).swapaxes(0, 1).reshape(owned, BLOCKS * width)
    packed = jnp.concatenate(
        [expand[0], expand[1], shrink_own, mixing[1], mixing[2]], 1
    )
    if fast:
        z_got = [hop(packed, d) for d in (4, 8, 12)]
        own = pack_rows(held_until(mixing[0], packed))
        own = jnp.broadcast_to(own[None], (devices,) + own.shape)
        inner_part = lax.all_to_all(own, BOTH, 0, 0, tiled=True)
    else:
        inner_part = lax.all_gather(mixing[0], BOTH, axis=0, tiled=True)
        full = lax.all_gather(packed, BOTH, axis=0, tiled=True)
        full, pair = full[:, : 2 * wide], full[:, 3 * wide :]
        shrink_full = lax.all_gather(shrink, BOTH, axis=0, tiled=True).reshape(BLOCKS, wide, width)

    tok = tokens.reshape(rows, total)
    cot = cotangent.reshape(rows, total)
    (norm,) = call(norm_body, [((rows, total), BF16)], [tok, gains], 1)

    tw_units, sp_units = twiddle.transpose(0, 2, 3, 1), spread.transpose(0, 2, 3, 1)
    sq_units = squeeze.transpose(1, 2, 0)
    s1, c1, s2, c2, spec, read_own, columns, mix_own = call(
        filter_body,
        [((order, length), BF16)] * 4
        + [((count, chans, 2 * block), F32), ((order, chans), F32), ((chans, 8), F32)]
        + [((chans, chans), BF16)],
        [
            place.astype(jnp.int32).reshape(1), lifting, phases[None], mapping, readout, damping[None],
            kernel[:, :total], tw_units[0], perm, feats, table,
        ],
        7,
        scalars=1,
    )
    if fast:
        held = jnp.stack([packed] + z_got)
        left, right = held[:, :, :1408], held[:, :, 1408:]
        inner_part, left, right, _ = lax.optimization_barrier((inner_part, left, right, spec))

    blocks = (pieces, seqs * chans, share)
    inner, sect_out = call(
        functools.partial(value_body, fast),
        [((total, width), BF16), (blocks, BF16)],
        [inner_part, norm, perm],
        2,
    )
    sect_in = exchange(sect_out)
    tokens = held_until(tokens, sect_out)
    ahead = [(n, n + 1) for n in range(pieces - 1)]
    halo = lax.ppermute(tokens[:, share - 2 :], "seq", ahead)
    if fast:
        got = held_until((hop(left, 2), hop_y(right)), sect_out)
        left, right = jnp.concatenate([left, got[0]], 0), jnp.concatenate([right, got[1]], 0)
        got = (hop_y(left), hop(right, 2))
        left, right = jnp.concatenate([left, got[0]], 0), jnp.concatenate([right, got[1]], 0)
        sect_in, left, right, halo = lax.optimization_barrier((sect_in, left, right, halo))
    spectra = (count, seqs * chans, 2 * block)
    long_blocks = (count, seqs * chans, block)
    conv_scratch = [
        pltpu.VMEM(spectra, F32),
        pltpu.VMEM(spectra, F32),
        pltpu.VMEM((count, chans, block), F32),
        pltpu.VMEM((count, chans, block), F32),
    ]
    long_out, conv_in, signal = call(
        functools.partial(conv_body, length),
        [(blocks, BF16), (long_blocks, BF16), ((chans, seqs * length), BF16)],
        [sect_in, mix_own, columns, spec, high, low, table_back[:, :block]],
        7,
        scratch=conv_scratch,
    )
    long_in = exchange(long_out)
    if fast:
        got = held_until((hop(left, 1), hop(right, 1)), long_out)
        full, shrink_full, pair = call(
            gather_body,
            [((total, 2 * wide), BF16), ((BLOCKS, wide, width), BF16), ((total, 2 * width), BF16)],
            [me, left, got[0], right, got[1]],
            5,
            scalars=1,
        )

    quad = (BLOCKS, rows, width)
    sect_sw, switch, switch_edge, gate_seq = call(
        functools.partial(switch_body, seqs),
        [(quad, F32), (quad, BF16), ((BLOCKS, 16, width), BF16), (quad, F32)],
        [norm, halo, gains, pair, tw_units[1], kernel],
        1,
    )

    broad = (BLOCKS, rows, wide)
    if fast:
        half_devices = devices // 2
        weight_shapes = [((half_devices, owned, 3 * wide + width), BF16)] * 2
        side_shapes = [((half_devices, owned, width), BF16)] * 2
    else:
        weight_shapes = [((total, 3 * wide + width), F32)]
        side_shapes = [((total, width), F32)]
    (
        layer, lg_out, switch_grad, res_grad, spread_part, squeeze_part, merge_part, gain_part,
        first_rows, *main,
    ) = call(
        functools.partial(middle_body, fast, owned, seqs),
        [
            ((rows, total), BF16), (blocks, BF16), (quad, BF16), (quad, F32),
            ((2, 16, wide), F32), ((16, width), F32), ((16, width), F32), ((BLOCKS, width), F32),
            ((BLOCKS, 2 * seqs, width), BF16),
        ] + weight_shapes,
        [me, long_in, gate_seq, tok, cot, gains, full, shrink_full, pair, tw_units[2],
         sp_units, sq_units, perm],
        27,
        scratch=[pltpu.VMEM(broad, F32)] * 5
        + [pltpu.VMEM(broad, BF16)] * 3
        + [pltpu.VMEM((2, 16, wide), F32)],
        late=(4, 6, 7),
        early=(0, 1, 2, 3),
        scalars=1,
    )
    lg_in = exchange(lg_out)

    after = lax.ppermute(first_rows, "seq", [(to, at) for at, to in ahead])
    n1_sw, small, *side = call(
        functools.partial(switch_back_body, fast, owned, seqs),
        [(quad, F32), ((24, 2 * wide), BF16)] + side_shapes,
        [me, switch_grad, after, switch, switch_edge, sect_sw, pair, tw_units[1], kernel, norm,
         spread_part, squeeze_part, merge_part, gain_part],
        5,
        scalars=1,
    )
    if fast:
        got, side_got, small_got = hop(main[1], 1), hop(side[1], 1), hop(small, 1)
        def sum_shapes(n):
            left, right = ((n + 1, owned, 2 * wide), BF16), ((n, owned, wide + 2 * width), BF16)
            return [left, left, right, right]

        left, left_send, right, right_send = call(
            first_sum_body,
            sum_shapes(half_devices // 2),
            [main[0], got, side[0], side_got, small, small_got],
            4,
        )
        lg_in = held_until(lg_in, left, left_send, right, right_send)

    fg_out, conv_grad, signal_grad = call(
        functools.partial(conv_back_body, length),
        [(blocks, BF16), ((chans, seqs * length), BF16), ((chans, seqs * length), F32)],
        [lg_in, mix_own, columns, spec, high, low, table_back[:, :block]],
        8,
        scratch=conv_scratch,
    )
    fg_in = exchange(fg_out)

    if fast:
        got = held_until((hop_y(left_send), hop(right_send, 2)), fg_out)
        left, left_send, right, right_send = call(
            second_sum_body, sum_shapes(half_devices // 4), [left, got[0], right, got[1]], 3
        )
        lg_in = held_until(lg_in, left, left_send, right, right_send)

    q_rows = chans + 8
    m_rows = order + 8
    (both,) = call(
        functools.partial(filter_back_body, length),
        [((m_rows + q_rows, order), BF16 if fast else F32)],
        [
            lg_in, conv_in, sect_in, signal, conv_grad, signal_grad, s1, c1, s2, c2, read_own,
            mapping, columns, feats, high, low, table_back, same, pick,
        ],
        14,
        scratch=[
            pltpu.VMEM(spectra, F32),
            pltpu.VMEM(long_blocks, F32),
            pltpu.VMEM(long_blocks, F32),
            pltpu.VMEM(spectra, F32),
            pltpu.VMEM((count, chans, 2 * block), F32),
        ],
    )

    if fast:
        got = held_until((hop(left_send, 2), hop_y(right_send)), both)
        shape = ((owned, 5 * wide + 2 * width), BF16)
        own, *sends = call(third_sum_body, [shape] * 4, [left, got[0], right, got[1]], 2)
        z_got = [hop(sent, d) for sent, d in zip(sends, (8, 4, 12))]
        both = added(both, held_until(hop_y(both), own), slice(0, None), BF16)
        fg_in = held_until(fg_in, own, sends, both)

    if fast:
        last_shapes = [((devices, owned * 5 // 3 + 8, 128), BF16)]
    else:
        last_shapes = [((total, width), F32), ((BLOCKS, width), F32)]
    tokens_grad, *pay = call(
        functools.partial(last_body, fast),
        [((rows, total), F32)] + last_shapes,
        [fg_in, perm, inner, norm, n1_sw, res_grad, tok, gains],
        3,
    )
    if fast:
        value_parts = lax.all_to_all(pay[0], BOTH, 0, 0, tiled=True)
    else:
        value_grad = lax.psum_scatter(pay[0], BOTH, scatter_dimension=0, tiled=True)
        gain_one = lax.psum(pay[1], BOTH)

    if fast:
        got = [both] + held_until([hop(both, d) for d in (4, 8, 12)], tokens_grad, z_got)
        m_sum = pair_sum([g[:m_rows] for g in got], BF16)
        both = jnp.concatenate([m_sum] + [g[m_rows:] for g in got], 0)
        z_shapes = [((2, owned, wide), F32), ((2, 16, wide), F32), ((BLOCKS * owned, width), F32)]
        z_shapes += [((2, owned, width), F32), ((BLOCKS, 16, width), F32)]
        expand_grad, spread_sum, shrink_grad, mix_sum, rest_sum = call(
            weights_out_body, z_shapes, [own, *z_got], 4
        )
        got = [both] + held_until([hop(both, d) for d in (2, 1, 3)], rest_sum)
        out_shapes = [(3, 16, width), (3, 2 * total), lifting.shape, (1, order), mapping.shape]
        twiddle_sum, kernel_grad, lifting_grad, phases_grad, mapping_grad, readout_grad = call(
            small_out_body,
            [(shape, F32) for shape in (*out_shapes, readout.shape)],
            [place.astype(jnp.int32).reshape(1), *got, rest_sum, perm],
            3,
            scratch=[pltpu.VMEM((pieces, q_rows, order), F32)],
            scalars=1,
        )
        gains_grad, mixing_grad = call(
            value_out_body,
            [((2, total), F32), ((3, owned, width), F32)],
            [held_until(value_parts, twiddle_sum), mix_sum, rest_sum],
            1,
        )
        squeeze_sum = rest_sum[0]
    else:
        m_sum = lax.psum(both[:m_rows], BOTH)
        q_all = lax.all_gather(lax.psum(both[m_rows:], "batch"), "seq", axis=0, tiled=False)
        main_sum = lax.psum_scatter(main[0], BOTH, scatter_dimension=0, tiled=True)
        switch_own = lax.psum_scatter(side[0], BOTH, scatter_dimension=0, tiled=True)
        small = lax.psum(small.astype(F32), BOTH)
        small = jnp.concatenate([small[:, :wide], small[:, wide : 2 * wide]], 0)

        expand_grad = jnp.stack([main_sum[:, k * wide : (k + 1) * wide] for k in range(2)])
        shrink_grad = main_sum[:, 2 * wide : 3 * wide].reshape(owned, BLOCKS, width)
        shrink_grad = shrink_grad.swapaxes(0, 1).reshape(BLOCKS * owned, width)
        mixing_grad = jnp.stack([value_grad, switch_own, main_sum[:, 3 * wide :]])
        spread_sum = small[:32].reshape(2, 16, wide)
        squeeze_sum, merge_sum, switch_sum, tail_sum = small[32:].reshape(16, BLOCKS, width).swapaxes(0, 1)
        value_sum = q_all[:, chans : chans + BLOCKS, :chans].reshape(pieces, BLOCKS, BLOCKS, span)
        value_sum = value_sum.transpose(1, 2, 0, 3).reshape(16, width)
        twiddle_sum = jnp.stack([value_sum, switch_sum, merge_sum])
        taps_value = q_all[:, chans + BLOCKS : chans + BLOCKS + 3, :chans]
        taps_value = taps_value.reshape(pieces, 3, BLOCKS, span).transpose(1, 2, 0, 3)
        taps_sum = tail_sum[BLOCKS:].reshape(BLOCKS, 3, width).swapaxes(0, 1)
        kernel_grad = jnp.concatenate(
            [taps_value.reshape(3, total), taps_sum.reshape(3, total)], 1
        )
        readout_grad = q_all[:, :chans].reshape(pieces, BLOCKS, span, order)
        readout_grad = readout_grad.transpose(3, 1, 0, 2).reshape(order, total)
        gains_grad = jnp.stack([gain_one.reshape(total), tail_sum[:BLOCKS].reshape(total)])
        lifting_grad = m_sum[order : order + lifting.shape[0]]
        phases_grad = m_sum[order + lifting.shape[0]]
        mapping_grad = m_sum[:order]

    def of_units(rows_now):
        lead = rows_now.shape[:-2]
        shaped = rows_now.reshape(*lead, BLOCKS, BLOCKS, rows_now.shape[-1])
        return jnp.moveaxis(shaped, -1, -3)

    return (
        layer.reshape(seqs, share, total),
        tokens_grad.reshape(seqs, share, total),
        gains_grad,
        mixing_grad,
        of_units(twiddle_sum),
        expand_grad,
        of_units(spread_sum),
        shrink_grad,
        of_units(squeeze_sum),
        kernel_grad,
        lifting_grad,
        phases_grad.reshape(order),
        mapping_grad,
        readout_grad,
    )


def solution(mesh):
    return jax.shard_map(
        per_device,
        mesh=mesh,
        in_specs=(
            P("batch", "seq", None),
            P("batch", "seq", None),
            P(),
            P(None, ("seq", "batch"), None),
            P(),
            P(None, ("seq", "batch"), None),
            P(),
            P(("seq", "batch"), None),
            P(),
            P(),
            P(),
            P(),
            P(),
            P(),
            P(),
        ),
        out_specs=(
            P("batch", "seq", None),
            P("batch", "seq", None),
            P(),
            P(None, ("seq", "batch"), None),
            P(),
            P(None, ("seq", "batch"), None),
            P(),
            P(("seq", "batch"), None),
            P(),
            P(),
            P(),
            P(),
            P(),
            P(),
        ),
        check_vma=False,
    )
```

```python
import functools
import math

import jax
import jax.numpy as jnp
import numpy as np
from jax import lax
from jax.experimental import pallas as pl
from jax.experimental.pallas import tpu as pltpu
from jax.sharding import PartitionSpec as P

BLOCKS = 4
BOTH = ("seq", "batch")
F32 = jnp.float32
BF16 = jnp.bfloat16
HIGHEST = lax.Precision.HIGHEST
LIMIT = 52
NN = ((1,), (0,))
NT = ((1,), (1,))
TN = ((0,), (0,))


def mm(left, right, dims=NN, precision=None):
    return lax.dot_general(
        left, right, (dims, ((), ())), preferred_element_type=F32, precision=precision
    )


class Late:
    def __init__(self, source, held, done):
        self.held, self.waiting = held, pltpu.make_async_copy(source, held, done)
        self.waiting.start()

    def ready(self):
        if self.waiting is not None:
            self.waiting.wait()
            self.waiting = None
        return self.held


class Early:
    def __init__(self, target, held, done):
        self.ref, self.copy, self.left = held, pltpu.make_async_copy(held, target, done), False

    def leave(self):
        if not self.left:
            self.copy.start()
            self.left = True


def call(body, outs, operands, micros, scratch=(), scalars=0, limit=LIMIT, late=(), early=()):
    specs = [
        pl.BlockSpec(
            memory_space=pl.ANY if k in late else pltpu.SMEM if k < scalars else pltpu.VMEM
        )
        for k in range(len(operands))
    ]
    out_specs = [
        pl.BlockSpec(memory_space=pl.ANY if k in early else pltpu.VMEM) for k in range(len(outs))
    ]
    staging = [pltpu.VMEM(operands[k].shape, operands[k].dtype) for k in late]
    staging += [pltpu.VMEM(*outs[k]) for k in early]
    count = len(staging)

    def whole(*refs):
        refs = list(refs)
        held = refs[len(operands) + len(outs) :][:count]
        rest = refs[len(operands) + len(outs) + count :]
        if not count:
            body(*refs)
            return
        done, rest = rest[0], rest[1:]
        for n, k in enumerate(late):
            refs[k] = Late(refs[k], held[n], done.at[n])
        for n, k in enumerate(early):
            at = len(operands) + k
            refs[at] = Early(refs[at], held[len(late) + n], done.at[len(late) + n])
        body(*refs[: len(operands) + len(outs)], *rest)
        for k in early:
            refs[len(operands) + k].leave()
        for k in early:
            refs[len(operands) + k].copy.wait()
        for k in late:
            refs[k].ready()

    if count:
        staging.append(pltpu.SemaphoreType.DMA((count,)))
    return pl.pallas_call(
        whole,
        out_shape=[jax.ShapeDtypeStruct(shape, kind) for shape, kind in outs],
        in_specs=specs,
        out_specs=out_specs,
        scratch_shapes=staging + list(scratch),
        compiler_params=pltpu.CompilerParams(vmem_limit_bytes=limit << 20),
        cost_estimate=pl.CostEstimate(
            flops=int(micros * 0.8e9), bytes_accessed=1 << 16, transcendentals=0
        ),
    )(*operands)


def packed_tables(points):
    size = 2 * points
    place = np.arange(size)[:, None].astype(np.int64)
    bins = np.arange(points)[None, :]
    angle = 2.0 * np.pi / size * ((place * bins) % size)
    forward = np.concatenate([np.cos(angle), -np.sin(angle)], 1)
    forward[:, points] = np.where(np.arange(size) % 2 == 0, 1.0, -1.0)
    weight = np.where(np.arange(size) % points == 0, 1.0, 2.0) / size
    backward = (forward * weight[None, :]).T
    return forward.astype(np.float32), np.ascontiguousarray(backward).astype(np.float32)


def split_table(table):
    high = table.astype(jnp.bfloat16)
    low = (table - high.astype(np.float32)).astype(jnp.bfloat16)
    return high, low


def feature_rows(length):
    place = np.arange(length)
    rows = [place / length]
    for harmonic in (1, 2):
        angle = 2.0 * np.pi / length * ((harmonic * place) % length)
        rows += [np.cos(angle), np.sin(angle)]
    rows += [np.ones(length), np.zeros(length), np.zeros(length)]
    return np.stack(rows).astype(np.float32)


def spread_matrix(pieces, span):
    width = pieces * span
    out = np.zeros((BLOCKS, pieces, BLOCKS, span, width), np.float32)
    for b in range(BLOCKS):
        for piece in range(pieces):
            for k in range(span):
                out[b, piece, b, k, piece * span + k] = 1.0
    return out.reshape(BLOCKS, pieces * BLOCKS * span, width).astype(jnp.bfloat16)


def normalize_rows(values):
    centred = values - jnp.mean(values, -1, keepdims=True)
    factor = lax.rsqrt(jnp.mean(centred * centred, -1, keepdims=True) + 1e-05)
    return centred * factor, factor


def sincos(angle):
    turns = (angle * (2.0 / math.pi) + 12582912.0) - 12582912.0
    rest = (angle - turns * 1.5703125) - turns * 4.83826794896619e-4
    square = rest * rest
    sine = rest + rest * square * (
        -1.6666654611e-1 + square * (8.3321608736e-3 + square * -1.9515295891e-4)
    )
    cosine = (
        1.0
        - 0.5 * square
        + square
        * square
        * (4.166664568298827e-2 + square * (-1.388731625493765e-3 + square * 2.443315711809948e-5))
    )
    quarter = turns.astype(jnp.int32)
    odd = jnp.bitwise_and(quarter, 1) == 1
    sine_sign = (1 - jnp.bitwise_and(quarter, 2)).astype(F32)
    cosine_sign = (1 - jnp.bitwise_and(quarter + 1, 2)).astype(F32)
    return (
        jnp.where(odd, cosine, sine) * sine_sign,
        jnp.where(odd, sine, cosine) * cosine_sign,
    )


def parts_of(values):
    width = values.shape[1] // BLOCKS
    return [values[:, k * width : (k + 1) * width] for k in range(BLOCKS)]


def mix(sectioned, rows):
    return [
        sum(sectioned[a] * rows[4 * a + b : 4 * a + b + 1, :] for a in range(BLOCKS))
        for b in range(BLOCKS)
    ]


def unmix(upstream, rows):
    return [
        sum(upstream[b] * rows[4 * a + b : 4 * a + b + 1, :] for b in range(BLOCKS))
        for a in range(BLOCKS)
    ]


def mix_grad(sectioned, upstream):
    return jnp.concatenate(
        [
            jnp.sum(sectioned[a] * upstream[b], 0, keepdims=True)
            for a in range(BLOCKS)
            for b in range(BLOCKS)
        ],
        0,
    )


def lane_of(shape):
    return lax.broadcasted_iota(jnp.int32, shape, len(shape) - 1)


def row_of(shape):
    return lax.broadcasted_iota(jnp.int32, shape, 0)


def time_rows(block_ref, span):
    pieces, rows, _ = block_ref.shape
    return jnp.concatenate(
        [
            block_ref[n].astype(F32)[s * span : (s + 1) * span]
            for s in range(rows // span)
            for n in range(pieces)
        ],
        1,
    )


def later_lanes(values, steps, length):
    total = values.shape[1]
    moved = pltpu.roll(values, total - steps, 1)
    return jnp.where(lane_of(values.shape) % length < length - steps, moved, 0.0)


def earlier_lanes(values, steps, length):
    moved = pltpu.roll(values, steps, 1)
    return jnp.where(lane_of(values.shape) % length >= steps, moved, 0.0)


def to_pieces(lanes_now, out_ref, length):
    pieces, _, width = out_ref.shape
    seqs = lanes_now.shape[1] // length
    for n in range(pieces):
        out_ref[n] = jnp.concatenate(
            [
                lanes_now[:, s * length + n * width : s * length + (n + 1) * width]
                for s in range(seqs)
            ],
            0,
        ).astype(BF16)


def spectrum(flat, high_ref, low_ref, out_ref):
    out = mm(flat, high_ref[...]) + mm(flat, low_ref[...])
    out_ref[...] = out.reshape(out_ref.shape)


def mm2(left, right, dims=NN):
    left_high = left.astype(BF16)
    left_low = (left - left_high.astype(F32)).astype(BF16)
    return mm(left_low, right, dims) + mm(left_high, right, dims)


def mm3(left, right, dims=NN):
    left_high, right_high = left.astype(BF16), right.astype(BF16)
    left_low = (left - left_high.astype(F32)).astype(BF16)
    right_low = (right - right_high.astype(F32)).astype(BF16)
    return (
        mm(left_high, right_low, dims) + mm(left_low, right_high, dims)
    ) + mm(left_high, right_high, dims)


def nyquist_split(spec):
    half = spec.shape[-1] // 2
    real, imaginary = spec[..., :half], spec[..., half:]
    first = lane_of(real.shape) == 0
    return jnp.where(first, 0.0, imaginary), jnp.where(first, imaginary, real)


def norm_body(tok_ref, gains_ref, norm_ref):
    norm = normalize_rows(tok_ref[...].astype(F32))[0] * gains_ref[0:1, :]
    norm_ref[...] = norm.astype(BF16)


def unit_rows(ref):
    return jnp.concatenate([ref[a].astype(F32) for a in range(BLOCKS)], 0)


def filter_body(
    place_ref, lift_ref, phase_ref, map_ref, read_all, damp_all, taps_all, tw_ref, perm_ref, feat_ref,
    table_ref, s1, c1, s2, c2, spec_ref, read_ref, columns_ref, mix_ref,
):
    span = read_ref.shape[1]
    at = pl.ds(pl.multiple_of(place_ref[0] * span, span), span)
    chosen = [perm_ref[b, at, :] for b in range(BLOCKS)]
    width = perm_ref.shape[2]
    read_ref[...] = sum(
        mm(read_all[:, b * width : (b + 1) * width], chosen[b].astype(F32), NT, HIGHEST)
        for b in range(BLOCKS)
    )
    rows = jnp.concatenate([damp_all[...], taps_all[...], jnp.zeros((4, BLOCKS * width), F32)], 0)
    columns = sum(
        mm(chosen[b].astype(F32), rows[:, b * width : (b + 1) * width], NT, HIGHEST)
        for b in range(BLOCKS)
    )
    columns_ref[...] = columns
    factors = unit_rows(tw_ref)
    mix_ref[...] = sum(
        mm((chosen[b] * factors[4 * a + b : 4 * a + b + 1].astype(BF16)), chosen[a], NT)
        for a in range(BLOCKS)
        for b in range(BLOCKS)
    ).astype(BF16)
    lift = jnp.concatenate(
        [lift_ref[...], phase_ref[...], jnp.zeros((7 - lift_ref.shape[0], map_ref.shape[0]), F32)], 0
    )
    sine_one, cosine_one = sincos(mm(lift, feat_ref[...], TN, HIGHEST))
    s1[...] = sine_one.astype(BF16)
    c1[...] = cosine_one.astype(BF16)
    sine_two, cosine_two = sincos(mm(map_ref[...], sine_one, TN, HIGHEST))
    s2[...] = sine_two.astype(BF16)
    c2[...] = cosine_two.astype(BF16)
    shape = (read_ref.shape[1], sine_two.shape[1])
    place = lane_of(shape).astype(F32)
    response = mm(read_ref[...], sine_two, TN, HIGHEST) * jnp.exp(-place * columns[:, 0:1])
    pieces, span, doubled = spec_ref.shape
    width = doubled // 2
    zero = jnp.zeros((span, width), F32)
    rows = []
    for k in range(pieces):
        now = response[:, k * width : (k + 1) * width]
        before = response[:, (k - 1) * width : k * width] if k else zero
        rows.append(
            jnp.concatenate([now, jnp.where(lane_of(before.shape) == 0, 0.0, before)], 1)
        )
    spec = mm3(jnp.concatenate(rows, 0), table_ref[...])
    spec_ref[...] = spec.reshape(pieces, span, doubled)


def value_body(packed, *refs):
    if packed:
        held_ref, norm_ref, perm_ref, full_ref, out_ref = refs
        rows = held_ref.shape[1] * 3 // 5
        share = held_ref.shape[0] // BLOCKS
        inner = []
        for a in range(BLOCKS):
            blocks = []
            for k in range(a * share, (a + 1) * share):
                held = held_ref[k].astype(F32)
                blocks.append(unpack_rows(held, rows))
            inner.append(jnp.concatenate(blocks, 0).astype(BF16))
            full_ref[a * rows * share : (a + 1) * rows * share, :] = inner[a]
    else:
        inner_ref, norm_ref, perm_ref, full_ref, out_ref = refs
        full_ref[...] = inner_ref[...]
        width = full_ref.shape[1]
        inner = [full_ref[a * width : (a + 1) * width, :] for a in range(BLOCKS)]
    norm = parts_of(norm_ref[...])
    first = [mm(norm[a], inner[a]).astype(BF16) for a in range(BLOCKS)]
    send_pieces(first, perm_ref, out_ref)


def pack_rows(values):
    rows = values.shape[0]
    rest = [values[k : k + 8, 128:] for k in range(0, rows, 8)] + [jnp.zeros_like(values[:8, 128:])]
    pairs = [jnp.concatenate(rest[k : k + 2], 1) for k in range(0, rows // 8, 2)]
    return jnp.concatenate([values[:, :128]] + pairs, 0)


def unpack_rows(held, rows):
    rest = []
    for k in range(rows // 8):
        start = rows + 8 * (k // 2)
        rest.append(held[start : start + 8, 64 * (k % 2) : 64 * (k % 2) + 64])
    return jnp.concatenate([held[:rows], jnp.concatenate(rest, 0)], 1)


def gather_body(
    me_ref, left_own, left_other, right_own, right_other, wide_ref, shrink_ref, pair_ref
):
    rows, cut = left_own.shape[1:]
    width = shrink_ref.shape[2]
    first = wide_ref.shape[1]
    last = first + BLOCKS * width
    count = 2 * left_own.shape[0]
    per = 2 if rows % 16 else 1
    for k in range(0, count, per):
        blocks = []
        for owner in range(k, k + per):
            bits = apart_bits(me_ref, owner)
            deep = bits[3] + 2 * bits[4]
            left = bits[0] * 8 + bits[2] * 4 + deep
            right = bits[2] * 8 + bits[0] * 4 + deep
            near = bits[1] == 0
            blocks.append(
                jnp.concatenate(
                    [
                        jnp.where(near, left_own[left].astype(F32), left_other[left].astype(F32)),
                        jnp.where(
                            near, right_own[right].astype(F32), right_other[right].astype(F32)
                        ),
                    ],
                    1,
                )
            )
        block = jnp.concatenate(blocks, 0).astype(BF16)
        wide_ref[k * rows : (k + per) * rows, :] = block[:, :first]
        pair_ref[k * rows : (k + per) * rows, :] = block[:, last:]
        for n, block in enumerate(blocks):
            parts = [block[:, first + g * width : first + (g + 1) * width] for g in range(BLOCKS)]
            at = (k + n) * BLOCKS * rows
            here = slice(at % shrink_ref.shape[1], at % shrink_ref.shape[1] + BLOCKS * rows)
            shrink_ref[at // shrink_ref.shape[1], here, :] = jnp.concatenate(parts, 0).astype(BF16)


def send_pieces(parts, perm_ref, out_ref):
    pieces, rows, width = out_ref.shape
    seqs = parts[0].shape[0] // width
    span = rows // seqs
    turned = [
        sum(
            mm(perm_ref[k], parts[k][s * width : (s + 1) * width], NT) for k in range(BLOCKS)
        )
        for s in range(seqs)
    ]
    for n in range(pieces):
        out_ref[n] = jnp.concatenate(
            [turned[s][n * span : (n + 1) * span] for s in range(seqs)], 0
        ).astype(BF16)


def receive_pieces(in_ref, perm_ref):
    pieces, rows, width = in_ref.shape
    seqs = rows * pieces // (BLOCKS * perm_ref.shape[2])
    span = rows // seqs
    held = [in_ref[n].astype(F32) for n in range(pieces)]
    turned = [
        jnp.concatenate([h[s * span : (s + 1) * span] for h in held], 0).T.astype(BF16)
        for s in range(seqs)
    ]
    return [
        jnp.concatenate([mm(turned[s], perm_ref[k]) for s in range(seqs)], 0)
        for k in range(BLOCKS)
    ]


def earlier_rows(values, halo, steps):
    moved = pltpu.roll(values, steps, 0)
    row = row_of(values.shape)
    for k in range(steps):
        moved = jnp.where(row == k, halo[2 - steps + k : 3 - steps + k], moved)
    return moved


def later_rows(values, halo, steps):
    count = values.shape[0]
    moved = pltpu.roll(values, count - steps, 0)
    row = row_of(values.shape)
    for k in range(steps):
        moved = jnp.where(row == count - steps + k, halo[k : k + 1], moved)
    return moved


def per_sequence(function, values, halo, seqs, steps):
    count = values.shape[0] // seqs
    return jnp.concatenate(
        [
            function(values[s * count : (s + 1) * count], halo[2 * s : 2 * s + 2], steps)
            for s in range(seqs)
        ],
        0,
    )


def switch_body(
    seqs, norm_ref, halo_ref, gains_ref, full_ref, tw_ref, taps_ref, sect_ref, sw_ref, sh_ref, gate_ref
):
    width = norm_ref.shape[1] // BLOCKS
    edge = jnp.concatenate([halo_ref[s].astype(F32) for s in range(seqs)], 0)
    edge = jnp.concatenate([edge, jnp.zeros((16 - 2 * seqs, edge.shape[1]), F32)], 0)
    edge_norm = normalize_rows(edge)[0] * gains_ref[0:1, :]
    norm, halo = parts_of(norm_ref[...]), parts_of(edge_norm.astype(BF16))
    inner = [full_ref[a * width : (a + 1) * width, :][:, :width] for a in range(BLOCKS)]
    first = [mm(norm[a], inner[a]) for a in range(BLOCKS)]
    for a in range(BLOCKS):
        sect_ref[a] = first[a]
    rows = unit_rows(tw_ref)
    all_taps = parts_of(taps_ref[...][:, BLOCKS * width :])
    switch = mix(first, rows)
    edge = mix([mm(halo[a], inner[a]) for a in range(BLOCKS)], rows)
    for b in range(BLOCKS):
        sw_ref[b] = switch[b].astype(BF16)
        sh_ref[b] = edge[b].astype(BF16)
        now = switch[b].astype(BF16).astype(F32)
        before = edge[b].astype(BF16).astype(F32)
        taps = all_taps[b]
        gate_ref[b] = (
            taps[0:1] * now
            + taps[1:2] * per_sequence(earlier_rows, now, before, seqs, 1)
            + taps[2:3] * per_sequence(earlier_rows, now, before, seqs, 2)
        )


def loop(start, stop, body, carry, unrolled):
    if not unrolled:
        return lax.fori_loop(start, stop, body, carry)
    for step in range(start, stop):
        carry = body(step, carry)
    return carry


def bins_of(half):
    return [(slice(k, k + 128), slice(half + k, half + k + 128)) for k in range(0, half, 128)]


def convolve(spec_ref, b_ref, c_ref, x_ref, y_ref):
    pieces, rows, doubled = x_ref.shape
    span = spec_ref.shape[1]
    zero = jnp.zeros((span, 128), F32)
    parts = [slice(k, k + span) for k in range(0, rows, span)]
    for low, up in bins_of(doubled // 2):

        def outer(i, carry, low=low, up=up):
            def inner(j, totals):
                k = i - j
                a_now, b_now, c_now = spec_ref[k, :, low], b_ref[k, :, low], c_ref[k, :, low]
                out = []
                for s, at in enumerate(parts):
                    real, imag = x_ref[j, at, low], x_ref[j, at, up]
                    out.append(totals[2 * s] + a_now * real - b_now * imag)
                    out.append(totals[2 * s + 1] + b_now * real + c_now * imag)
                return tuple(out)

            totals = loop(0, i + 1, inner, (zero,) * (2 * len(parts)), pieces <= 8)
            for s, at in enumerate(parts):
                y_ref[i, at, low] = totals[2 * s]
                y_ref[i, at, up] = totals[2 * s + 1]
            return carry

        loop(0, pieces, outer, 0, pieces <= 8)


def correlate(spec_ref, b_ref, c_ref, g_ref, y_ref):
    pieces, rows, doubled = g_ref.shape
    span = spec_ref.shape[1]
    zero = jnp.zeros((span, 128), F32)
    parts = [slice(k, k + span) for k in range(0, rows, span)]
    for low, up in bins_of(doubled // 2):

        def outer(j, carry, low=low, up=up):
            def inner(i, totals):
                k = i - j
                a_now, b_now, c_now = spec_ref[k, :, low], b_ref[k, :, low], c_ref[k, :, low]
                out = []
                for s, at in enumerate(parts):
                    real, imag = g_ref[i, at, low], g_ref[i, at, up]
                    out.append(totals[2 * s] + a_now * real + b_now * imag)
                    out.append(totals[2 * s + 1] + c_now * imag - b_now * real)
                return tuple(out)

            totals = loop(j, pieces, inner, (zero,) * (2 * len(parts)), pieces <= 8)
            for s, at in enumerate(parts):
                y_ref[j, at, low] = totals[2 * s]
                y_ref[j, at, up] = totals[2 * s + 1]
            return carry

        loop(0, pieces, outer, 0, pieces <= 8)


def block_rows(piece_ref, block):
    pieces, _, width = piece_ref.shape
    each = block // width
    return jnp.concatenate(
        [
            jnp.concatenate([piece_ref[n + k] for k in range(each)], 1)
            for n in range(0, pieces, each)
        ],
        0,
    )


def conv_body(
    length, sect_ref, mix_ref, taps_ref, spec_ref, high_ref, low_ref, back_ref,
    out_ref, cin_ref, signal_ref, x_ref, y_ref, b_ref, c_ref,
):
    span = spec_ref.shape[1]
    lanes_now = time_rows(sect_ref, span).astype(BF16)
    signal = mm(mix_ref[...], lanes_now).astype(BF16)
    signal_ref[...] = signal
    signal = signal.astype(F32)
    conv_in = (
        taps_ref[:, 1:2] * signal
        + taps_ref[:, 2:3] * earlier_lanes(signal, 1, length)
        + taps_ref[:, 3:4] * earlier_lanes(signal, 2, length)
    )
    to_pieces(conv_in, cin_ref, length)
    spectrum(cin_ref[...].reshape(-1, cin_ref.shape[2]), high_ref, low_ref, x_ref)
    b_ref[...], c_ref[...] = nyquist_split(spec_ref[...])
    convolve(spec_ref, b_ref, c_ref, x_ref, y_ref)
    pieces, rows, doubled = y_ref.shape
    out = mm3(y_ref[...].reshape(pieces * rows, doubled), back_ref[...]).astype(BF16)
    width = out_ref.shape[2]
    each = doubled // 2 // width
    for n in range(pieces):
        for k in range(each):
            out_ref[n * each + k] = out[n * rows : (n + 1) * rows, k * width : (k + 1) * width]


def middle_body(
    fast, owned, seqs, me_ref, long_ref, gate_ref, tok_ref, cot_ref, gains_ref, full_ref, shrink_ref, pair_ref,
    tw_ref, spread_ref, sq_ref, perm_ref, layer_ref, lg_ref, swg_ref, res_ref, spg_ref, sqg_ref, twg_ref, gain_ref, edge_ref, *refs,
):
    *weight_outs, fg, fu, act, ug, hg, hid_ref, fgate_ref, fup_ref, sp_ref = refs
    for k in range(2):
        sp_ref[k] = unit_rows(spread_ref.at[k])
    rows, total = tok_ref.shape
    width = total // BLOCKS
    wide = fg.shape[2]
    tw_rows, sq_rows = unit_rows(tw_ref), unit_rows(sq_ref)
    gate = [gate_ref[b] for b in range(BLOCKS)]
    long_out = receive_pieces(long_ref, perm_ref)
    gated = [(gate[b] * long_out[b]).astype(BF16) for b in range(BLOCKS)]
    at = [slice(a * width, (a + 1) * width) for a in range(BLOCKS)]
    merge = [pair_ref[at[a], :][:, width:] for a in range(BLOCKS)]
    sect_merge = [mm(gated[a], merge[a]) for a in range(BLOCKS)]
    merged = mix(sect_merge, tw_rows)
    tokens = parts_of(tok_ref[...].astype(F32))
    residual = [tokens[b] + merged[b] for b in range(BLOCKS)]
    mean = sum(jnp.sum(r, -1, keepdims=True) for r in residual) / total
    centred = [r - mean for r in residual]
    variance = sum(jnp.sum(c * c, -1, keepdims=True) for c in centred) / total
    factor = lax.rsqrt(variance + 1e-05)
    normed = [c * factor for c in centred]
    gain = parts_of(gains_ref[1:2, :])
    norm_two = [(normed[a] * gain[a]).astype(BF16) for a in range(BLOCKS)]
    full_ref = full_ref.ready()
    for a in range(BLOCKS):
        fg[a] = mm(norm_two[a], full_ref[at[a], :wide])
        fu[a] = mm(norm_two[a], full_ref[at[a], wide : 2 * wide])

    step = 32
    lanes = 128

    def forward_lane(l, carry):
        here = pl.ds(pl.multiple_of(l * lanes, lanes), lanes)

        def forward_row(r, inner_carry):
            down = pl.ds(pl.multiple_of(r * step, step), step)
            gate_pre = mix([fg[a, down, here] for a in range(BLOCKS)], sp_ref[0, :, here])
            held = []
            for v in gate_pre:
                square = v * v
                half = 0.5 + 0.5 * jnp.tanh(v * (0.7978845608 + 0.0356774081 * square))
                active = v * half
                steep = 1.5957691216 + 0.2140644488 * square
                held.append((active, half + active * (1.0 - half) * steep))
            up_pre = mix([fu[a, down, here] for a in range(BLOCKS)], sp_ref[1, :, here])
            for b in range(BLOCKS):
                active, slope = held[b]
                hid_ref[b, down, here] = (active * up_pre[b]).astype(BF16)
                act[b, down, here] = active
                ug[b, down, here] = up_pre[b] * slope
            return inner_carry

        return lax.fori_loop(0, rows // step, forward_row, carry)

    lax.fori_loop(0, wide // lanes, forward_lane, 0)

    shrink_ref = shrink_ref.ready()
    shrink = [shrink_ref[a] for a in range(BLOCKS)]
    sect_down = [mm(hid_ref[a], shrink[a]) for a in range(BLOCKS)]
    lowered = mix(sect_down, sq_rows)
    layer_ref.ref[...] = jnp.concatenate(
        [(residual[b] + lowered[b]).astype(BF16) for b in range(BLOCKS)], 1
    )
    layer_ref.leave()
    upstream = parts_of(cot_ref.ready()[...].astype(F32))
    sqg_ref[...] = mix_grad(sect_down, upstream)
    back_down = unmix(upstream, sq_rows)
    back_down = [v.astype(BF16) for v in back_down]
    for a in range(BLOCKS):
        hg[a] = mm(back_down[a], shrink[a], NT)

    def backward_lane(l, carry):
        here = pl.ds(pl.multiple_of(l * lanes, lanes), lanes)
        zero = jnp.zeros((8, lanes), F32)
        for k, (held, slopes, out_ref) in enumerate(((fg, ug, fgate_ref), (fu, act, fup_ref))):

            def backward_row(r, sums, k=k, held=held, slopes=slopes, out_ref=out_ref):
                down = pl.ds(pl.multiple_of(r * step, step), step)
                grads = [hg[b, down, here] * slopes[b, down, here] for b in range(BLOCKS)]
                for a, value in enumerate(unmix(grads, sp_ref[k, :, here])):
                    out_ref[a, down, here] = value.astype(BF16)
                out = []
                for a in range(BLOCKS):
                    value = held[a, down, here]
                    for b in range(BLOCKS):
                        product = value * grads[b]
                        for n in range(0, step, 16):
                            pair = product[n : n + 8] + product[n + 8 : n + 16]
                            part = pair if n == 0 else part + pair
                        out.append(sums[4 * a + b] + part)
                return tuple(out)

            sums = lax.fori_loop(0, rows // step, backward_row, (zero,) * 16)
            for n in range(16):
                spg_ref[k, pl.ds(n, 1), here] = jnp.sum(sums[n], 0, keepdims=True)
        return carry

    lax.fori_loop(0, wide // lanes, backward_lane, 0)

    n2_grad = [
        mm(fgate_ref[a], full_ref[at[a], :wide], NT)
        + mm(fup_ref[a], full_ref[at[a], wide : 2 * wide], NT)
        for a in range(BLOCKS)
    ]
    scaled = [n2_grad[a] * gain[a] for a in range(BLOCKS)]
    plain = sum(jnp.sum(v, -1, keepdims=True) for v in scaled) / total
    joint = sum(jnp.sum(scaled[a] * normed[a], -1, keepdims=True) for a in range(BLOCKS)) / total
    res_grad = [
        upstream[a] + factor * (scaled[a] - plain - normed[a] * joint) for a in range(BLOCKS)
    ]
    gain_ref[...] = jnp.concatenate(
        [jnp.sum(n2_grad[a] * normed[a], 0, keepdims=True) for a in range(BLOCKS)], 0
    )
    for a in range(BLOCKS):
        res_ref.ref[a] = res_grad[a]
    res_ref.leave()
    twg_ref[...] = mix_grad(sect_merge, res_grad)
    back_merge = [v.astype(BF16) for v in unmix(res_grad, tw_rows)]
    long_grad = []
    for a in range(BLOCKS):
        gated_grad = mm(back_merge[a], merge[a], NT)
        long_grad.append((gated_grad * gate[a]).astype(BF16))
        now = (gated_grad * long_out[a]).astype(BF16)
        swg_ref.ref[a] = now
        share = rows // seqs
        edge_ref[a] = jnp.concatenate([now[s * share : s * share + 2] for s in range(seqs)], 0)
    swg_ref.leave()
    send_pieces(long_grad, perm_ref, lg_ref.ref)
    lg_ref.leave()

    for a in range(BLOCKS):
        from_hidden = mm(hid_ref[a], back_down[a], TN)
        group = BLOCKS * owned
        down = [
            jnp.concatenate(
                [
                    from_hidden[o + g * owned : o + (g + 1) * owned]
                    for o in range(0, wide, group)
                ],
                0,
            )
            for g in range(BLOCKS)
        ]
        held = jnp.concatenate(
            [mm(norm_two[a], fgate_ref[a], TN), mm(norm_two[a], fup_ref[a], TN)]
            + down
            + [mm(gated[a], back_merge[a], TN)],
            1,
        )

        def block_of(k, count, held=held):
            return held[k * count : (k + 1) * count]

        outs = weight_outs if fast else (weight_outs[0], owned)
        put_blocks(fast, me_ref, outs, a, block_of, width, 2 * wide)


def switch_back_body(
    fast, owned, seqs, me_ref, swg_ref, next_ref, sw_ref, sh_ref, sect_ref, full_ref, tw_ref, taps_ref,
    norm_ref, spg_ref, sqg_ref, mg_ref, gain_ref, n1_ref, small_ref, *outs,
):
    width = swg_ref.shape[2]
    all_taps = parts_of(taps_ref[...][:, BLOCKS * width :])
    back, taps_grad = [], []
    for b in range(BLOCKS):
        grad = swg_ref[b].astype(F32)
        after = next_ref[b].astype(F32)
        taps = all_taps[b]
        back.append(
            taps[0:1] * grad
            + taps[1:2] * per_sequence(later_rows, grad, after, seqs, 1)
            + taps[2:3] * per_sequence(later_rows, grad, after, seqs, 2)
        )
        now, before = sw_ref[b].astype(F32), sh_ref[b].astype(F32)
        shifted = [now] + [per_sequence(earlier_rows, now, before, seqs, m) for m in (1, 2)]
        taps_grad += [jnp.sum(value * grad, 0, keepdims=True) for value in shifted]
    tw_grad = mix_grad([sect_ref[a] for a in range(BLOCKS)], back)
    rest = [sqg_ref[...], mg_ref[...], tw_grad, jnp.concatenate([gain_ref[...]] + taps_grad, 0)]
    small = jnp.concatenate([spg_ref[0], spg_ref[1], jnp.concatenate(rest, 1)], 0)
    count = small_ref.shape[0]
    small_ref[...] = jnp.concatenate([small[:count], small[count:]], 1).astype(BF16)
    first = unmix(back, unit_rows(tw_ref))
    norm = parts_of(norm_ref[...])
    for a in range(BLOCKS):
        now = first[a].astype(BF16)
        n1_ref[a] = mm(now, full_ref[a * width : (a + 1) * width, :][:, :width], NT)
        held = mm(norm[a], now, TN)

        def block_of(k, count, held=held):
            return held[k * count : (k + 1) * count]

        put_blocks(fast, me_ref, outs if fast else (outs[0], owned), a, block_of, width, 0)


def apart_bits(me_ref, owner):
    apart = jnp.bitwise_xor(me_ref[0], owner)
    return [jnp.bitwise_and(lax.shift_right_logical(apart, n), 1) for n in range(5)]


def put_blocks(fast, me_ref, outs, a, block_of, width, start):
    rows = outs[0].shape[-2] if fast else outs[1]
    for k in range(width // rows):
        block = block_of(k, rows)
        if not fast:
            outs[0][a * width + k * rows : a * width + (k + 1) * rows, :] = block
            continue
        keep_ref, send_ref = outs
        block = block.astype(BF16)
        bits = apart_bits(me_ref, a * (width // rows) + k)
        deep = bits[3] * 2 + bits[4]
        for ref, core in ((keep_ref, 0), (send_ref, 1)):

            @pl.when(bits[1] == core)
            def _(ref=ref, block=block, bits=bits, deep=deep):
                if start:
                    ref[bits[0] * 8 + bits[2] * 4 + deep, :, :start] = block[:, :start]
                ref[bits[2] * 8 + bits[0] * 4 + deep, :, start:] = block[:, start:]


def conv_back_body(
    length, g_ref, mix_ref, taps_ref, spec_ref, high_ref, low_ref, back_ref,
    out_ref, cg_ref, sg_ref, x_ref, y_ref, b_ref, c_ref,
):
    span = spec_ref.shape[1]
    spectrum(block_rows(g_ref, x_ref.shape[2] // 2), high_ref, low_ref, x_ref)
    b_ref[...], c_ref[...] = nyquist_split(spec_ref[...])
    correlate(spec_ref, b_ref, c_ref, x_ref, y_ref)
    pieces, rows, doubled = y_ref.shape
    flat = mm3(y_ref[...].reshape(pieces * rows, doubled), back_ref[...])
    flat = flat.astype(BF16).astype(F32)
    grad = jnp.concatenate(
        [
            flat[n * rows + s * span : n * rows + (s + 1) * span]
            for s in range(rows // span)
            for n in range(pieces)
        ],
        1,
    )
    cg_ref[...] = grad.astype(BF16)
    signal_grad = (
        taps_ref[:, 1:2] * grad
        + taps_ref[:, 2:3] * later_lanes(grad, 1, length)
        + taps_ref[:, 3:4] * later_lanes(grad, 2, length)
    )
    sg_ref[...] = signal_grad
    to_pieces(mm(mix_ref[...].astype(F32), signal_grad, TN, HIGHEST), out_ref, length)


def filter_back_body(
    length, g_ref, cin_ref, sect_ref, signal_ref, cg_ref, sg_ref, s1, c1, s2, c2, read_ref, map_ref,
    damp_ref, feat_ref, high_ref, low_ref, back_ref, same_ref, pick_ref,
    out_ref, x_ref, b_ref, c_ref, gs_ref, p_ref,
):
    pieces, span, doubled = p_ref.shape
    half = doubled // 2
    spectrum(cin_ref[...].reshape(-1, half), high_ref, low_ref, x_ref)
    b_ref[...], c_ref[...] = nyquist_split(x_ref[...])
    spectrum(block_rows(g_ref, half), high_ref, low_ref, gs_ref)
    seqs = x_ref.shape[1] // span
    zero = jnp.zeros((span, 128), F32)
    parts = [slice(k, k + span) for k in range(0, seqs * span, span)]
    for low, up in bins_of(half):

        def outer(k, carry, low=low, up=up):
            def inner(j, totals):
                real, imag = totals
                for at in parts:
                    a_now, b_now, c_now = x_ref[j, at, low], b_ref[j, at, low], c_ref[j, at, low]
                    g_real, g_imag = gs_ref[j + k, at, low], gs_ref[j + k, at, up]
                    real = real + a_now * g_real + b_now * g_imag
                    imag = imag + c_now * g_imag - b_now * g_real
                return real, imag

            real, imag = loop(0, pieces - k, inner, (zero, zero), pieces <= 8)
            p_ref[k, :, low] = real
            p_ref[k, :, up] = imag
            return carry

        loop(0, pieces, outer, 0, pieces <= 8)
    flat = mm3(p_ref[...].reshape(pieces * span, doubled), back_ref[...])
    chunks = []
    for k in range(pieces):
        now = flat[k * span : (k + 1) * span, :half]
        if k + 1 < pieces:
            after = flat[(k + 1) * span : (k + 2) * span, half:]
            now = now + jnp.where(lane_of(after.shape) == 0, 0.0, after)
        chunks.append(now)
    response_grad = jnp.concatenate(chunks, 1)
    place = lane_of(response_grad.shape).astype(F32)
    response_grad = response_grad * jnp.exp(-place * damp_ref[:, 0:1])
    readout_grad = mm2(response_grad, s2[...], NT)
    pre_two = mm3(read_ref[...], response_grad) * c2[...].astype(F32)
    order = s1.shape[0]
    high = pre_two.astype(BF16)
    low = (pre_two - high.astype(F32)).astype(BF16)
    mapping_grad = mm(s1[...], low, NT) + mm(s1[...], high, NT)
    pre_one = mm3(map_ref[...], pre_two) * c1[...].astype(F32)
    lift_grad = mm3(feat_ref[...], pre_one, NT)

    sect = time_rows(sect_ref, span).astype(BF16)
    high = sg_ref[...].astype(BF16)
    low = (sg_ref[...] - high.astype(F32)).astype(BF16)
    tw = (mm(sect, low, NT) + mm(sect, high, NT)) * same_ref[...]
    tw = mm(pick_ref[...], tw, NN, HIGHEST)
    cg = cg_ref[...].astype(F32)
    signal = signal_ref[...].astype(F32)
    taps = []
    for m in range(3):
        moved = signal if m == 0 else earlier_lanes(signal, m, length)
        taps.append(jnp.sum(moved * cg, 1, keepdims=True))
    column = lane_of((span, 128))
    columns = sum(jnp.where(column == BLOCKS + m, taps[m], 0.0) for m in range(3))
    tw = tw + columns.T[: tw.shape[0], :span]
    tw = jnp.concatenate([tw, jnp.zeros((8, order - span), F32)], 1)
    out = jnp.concatenate([mapping_grad, lift_grad, readout_grad, tw], 0)
    out_ref[...] = out.astype(out_ref.dtype)


def last_body(
    fast, fg_ref, perm_ref, inner_ref, norm_ref, n1_ref, res_ref, tok_ref, gains_ref, out_ref, *pay
):
    width = inner_ref.shape[1]
    first = [v.astype(BF16) for v in receive_pieces(fg_ref, perm_ref)]
    norm = parts_of(norm_ref[...])
    normed, factor = normalize_rows(tok_ref[...].astype(F32))
    normed = parts_of(normed)
    gain = parts_of(gains_ref[0:1, :])
    grads = [
        mm(first[a], inner_ref[a * width : (a + 1) * width, :], NT) + n1_ref[a]
        for a in range(BLOCKS)
    ]
    scaled = [grads[a] * gain[a] for a in range(BLOCKS)]
    total = width * BLOCKS
    plain = sum(jnp.sum(v, -1, keepdims=True) for v in scaled) / total
    joint = sum(jnp.sum(scaled[a] * normed[a], -1, keepdims=True) for a in range(BLOCKS)) / total
    out_ref[...] = jnp.concatenate(
        [res_ref[a] + factor * (scaled[a] - plain - normed[a] * joint) for a in range(BLOCKS)], 1
    )
    gain_grad = [jnp.sum(grads[a] * normed[a], 0, keepdims=True) for a in range(BLOCKS)]
    weight = [mm(norm[a], first[a], TN) for a in range(BLOCKS)]
    if not fast:
        for a in range(BLOCKS):
            pay[0][a * width : (a + 1) * width, :] = weight[a]
            pay[1][a : a + 1, :] = gain_grad[a]
        return
    count, rows, _ = pay[0].shape
    share = count // BLOCKS
    held = (rows - 8) * 3 // 5
    flat = jnp.concatenate(gain_grad, 1)
    tail = [flat[:, k : k + 128] for k in range(0, total, 128)]
    tail = jnp.concatenate(tail + [jnp.zeros((8 - len(tail), 128), F32)], 0)
    for a in range(BLOCKS):
        for k in range(share):
            block = pack_rows(weight[a][k * held : (k + 1) * held])
            pay[0][a * share + k] = jnp.concatenate([block, tail], 0).astype(BF16)


def first_sum_body(
    keep_ref, got_ref, side_ref, side_got, small_ref, small_got, left_keep, left_send, right_keep, right_send
):
    n, _, cut = left_keep.shape
    n -= 1
    for k in range(2 * n):
        main = keep_ref[k].astype(F32) + got_ref[k].astype(F32)
        side = side_ref[k].astype(F32) + side_got[k].astype(F32)
        right = jnp.concatenate([main[:, cut:], side], 1).astype(BF16)
        left_out, right_out = (left_keep, right_keep) if k < n else (left_send, right_send)
        left_out[k % n] = main[:, :cut].astype(BF16)
        right_out[k % n] = right
    small = (small_ref[...].astype(F32) + small_got[...].astype(F32)).astype(BF16)
    left_keep[n] = small
    left_send[n] = small


def second_sum_body(
    left_ref, left_got, right_ref, right_got, left_keep, left_send, right_keep, right_send
):
    n = right_keep.shape[0]
    for k in range(2 * n):
        left = (left_ref[k].astype(F32) + left_got[k].astype(F32)).astype(BF16)
        right = (right_ref[k].astype(F32) + right_got[k].astype(F32)).astype(BF16)
        left_out, right_out = (left_keep, right_keep) if k < n else (left_send, right_send)
        left_out[k % n] = left
        right_out[k % n] = right
    small = (left_ref[2 * n].astype(F32) + left_got[2 * n].astype(F32)).astype(BF16)
    left_keep[n] = small
    left_send[n] = small


def third_sum_body(left_ref, left_got, right_ref, right_got, *outs):
    left = [(left_ref[k].astype(F32) + left_got[k].astype(F32)).astype(BF16) for k in range(5)]
    right = [(right_ref[k].astype(F32) + right_got[k].astype(F32)).astype(BF16) for k in range(4)]
    for k, out_ref in enumerate(outs):
        out_ref[...] = jnp.concatenate([left[k], right[k], left[4]], 1)


def weights_out_body(
    own_ref, one_ref, two_ref, three_ref, expand_ref, spread_ref, shrink_ref, mix_ref, rest_ref
):
    parts = [ref[...].astype(F32) for ref in (own_ref, one_ref, two_ref, three_ref)]
    held = (parts[0] + parts[1]) + (parts[2] + parts[3])
    owned, wide = expand_ref.shape[1:]
    width = mix_ref.shape[2]
    for k in range(2):
        expand_ref[k] = held[:, k * wide : (k + 1) * wide]
        start = 2 * wide + BLOCKS * width + k * width
        mix_ref[1 - k] = held[:, start : start + width]
    for g in range(BLOCKS):
        start = 2 * wide + g * width
        shrink_ref[g * owned : (g + 1) * owned, :] = held[:, start : start + width]
    start = 3 * wide + 2 * width
    small = jnp.concatenate([held[:, start : start + wide], held[:, start + wide :]], 0)
    for k in range(2):
        spread_ref[k] = small[16 * k : 16 * k + 16]
    for k in range(BLOCKS):
        rest_ref[k] = small[32:, k * width : (k + 1) * width]


def small_out_body(
    place_ref, own_ref, one_ref, two_ref, three_ref, rest_ref, perm_ref, twiddle_ref, kernel_ref, lift_ref, phase_ref, map_ref, read_ref, q_ref,
):
    order = map_ref.shape[0]
    m_rows, q_rows = order + 8, q_ref.shape[1]
    chans = q_rows - 8
    pieces = q_ref.shape[0]
    width = perm_ref.shape[2]
    parts = [ref[...] for ref in (own_ref, one_ref, two_ref, three_ref)]
    sums = [part[:m_rows].astype(F32) for part in parts]
    m_sum = (sums[0] + sums[1]) + (sums[2] + sums[3])
    map_ref[...] = m_sum[:order]
    lift_ref[...] = m_sum[order : order + lift_ref.shape[0]]
    phase_ref[...] = m_sum[order + lift_ref.shape[0] : order + lift_ref.shape[0] + 1]
    for k, outer in enumerate((0, 2, 1, 3)):
        for n, inner in enumerate((0, 4, 8, 12)):
            start = m_rows + n * q_rows
            q_ref[jnp.bitwise_xor(place_ref[0], outer ^ inner)] = parts[k][
                start : start + q_rows
            ].astype(F32)
    tall = jnp.concatenate([q_ref[n, :chans] for n in range(pieces)], 0).astype(BF16)
    broad = jnp.concatenate([q_ref[n, chans:, :chans] for n in range(pieces)], 1).astype(BF16)
    rest = [mm(broad, perm_ref[b]) for b in range(BLOCKS)]
    read_ref[...] = jnp.concatenate([mm(tall, perm_ref[b], TN) for b in range(BLOCKS)], 1)
    for a in range(BLOCKS):
        for b in range(BLOCKS):
            twiddle_ref[0, 4 * a + b : 4 * a + b + 1, :] = rest[b][a : a + 1]
    twiddle_ref[1] = rest_ref[2]
    twiddle_ref[2] = rest_ref[1]
    last = rest_ref[3]
    taps = [rest[b][BLOCKS : BLOCKS + 3] for b in range(BLOCKS)]
    taps += [last[BLOCKS + 3 * b : BLOCKS + 3 * b + 3] for b in range(BLOCKS)]
    kernel_ref[...] = jnp.concatenate(taps, 1)


def value_out_body(value_ref, mix_ref, rest_ref, gains_ref, mixing_ref):
    last = rest_ref[3]
    total = value_ref[0].astype(F32)
    for n in range(1, value_ref.shape[0]):
        total = total + value_ref[n].astype(F32)
    owned = mix_ref.shape[1]
    held = owned * 5 // 3
    mixing_ref[0] = unpack_rows(total, owned)
    mixing_ref[1] = mix_ref[0]
    mixing_ref[2] = mix_ref[1]
    one = jnp.concatenate([total[held + k : held + k + 1] for k in range(6)], 1)
    two = jnp.concatenate([last[a : a + 1] for a in range(BLOCKS)], 1)
    gains_ref[...] = jnp.concatenate([one, two], 0)


def hop(values, distance):
    pieces = lax.axis_size("seq")
    return lax.ppermute(values, "seq", [(n, n ^ distance) for n in range(pieces)])


def hop_y(values, distance=0):
    if not distance:
        return lax.ppermute(values, "batch", [(0, 1), (1, 0)])
    apart = 2 * distance + 1
    return lax.ppermute(values, BOTH, [(n, n ^ apart) for n in range(2 * lax.axis_size("seq"))])


def pair_sum(parts, kind):
    wide = [v.astype(F32) for v in parts]
    return ((wide[0] + wide[1]) + (wide[2] + wide[3])).astype(kind)


def held_until(values, *others):
    return lax.optimization_barrier((values, *others))[0]


def added(kept, came, at, kind):
    return (kept[at].astype(F32) + came[at].astype(F32)).astype(kind)


def per_device(
    tokens,
    cotangent,
    gains,
    mixing,
    twiddle,
    expand,
    spread,
    shrink,
    squeeze,
    kernel,
    lifting,
    phases,
    mapping,
    readout,
    damping,
):
    seqs, share, total = tokens.shape
    pieces, groups = lax.axis_size("seq"), lax.axis_size("batch")
    devices = pieces * groups
    place = lax.axis_index("seq")
    me = (place * groups + lax.axis_index("batch")).astype(jnp.int32).reshape(1)
    rows = seqs * share
    length = pieces * share
    width = total // BLOCKS
    wide = expand.shape[2]
    owned = mixing.shape[1]
    octet = devices // BLOCKS
    order = mapping.shape[0]
    fast = pieces == 16 and groups == 2 and owned % 8 == 0 and seqs == 2
    span = width // pieces
    chans = BLOCKS * span
    def exchange(values):
        return lax.all_to_all(values, "seq", 0, 0, tiled=True)

    block = 2 * share
    count = length // block
    table, table_back = packed_tables(block)
    high, low = split_table(table[:block])
    perm = spread_matrix(pieces, span)
    feats = feature_rows(length)
    same = np.tile(np.eye(span, dtype=np.float32), (BLOCKS, BLOCKS))
    pick = np.zeros((8, chans), np.float32)
    for a in range(BLOCKS):
        pick[a, a * span : (a + 1) * span] = 1.0

    shrink_own = shrink.reshape(BLOCKS, owned, width).swapaxes(0, 1).reshape(owned, BLOCKS * width)
    packed = jnp.concatenate(
        [expand[0], expand[1], shrink_own, mixing[1], mixing[2]], 1
    )
    if fast:
        z_got = [hop(packed, d) for d in (4, 8, 12)]
        own = pack_rows(held_until(mixing[0], packed))
        own = jnp.broadcast_to(own[None], (devices,) + own.shape)
        inner_part = lax.all_to_all(own, BOTH, 0, 0, tiled=True)
    else:
        inner_part = lax.all_gather(mixing[0], BOTH, axis=0, tiled=True)
        full = lax.all_gather(packed, BOTH, axis=0, tiled=True)
        full, pair = full[:, : 2 * wide], full[:, 3 * wide :]
        shrink_full = lax.all_gather(shrink, BOTH, axis=0, tiled=True).reshape(BLOCKS, wide, width)

    tok = tokens.reshape(rows, total)
    cot = cotangent.reshape(rows, total)
    (norm,) = call(norm_body, [((rows, total), BF16)], [tok, gains], 1)

    tw_units, sp_units = twiddle.transpose(0, 2, 3, 1), spread.transpose(0, 2, 3, 1)
    sq_units = squeeze.transpose(1, 2, 0)
    s1, c1, s2, c2, spec, read_own, columns, mix_own = call(
        filter_body,
        [((order, length), BF16)] * 4
        + [((count, chans, 2 * block), F32), ((order, chans), F32), ((chans, 8), F32)]
        + [((chans, chans), BF16)],
        [
            place.astype(jnp.int32).reshape(1), lifting, phases[None], mapping, readout, damping[None],
            kernel[:, :total], tw_units[0], perm, feats, table,
        ],
        7,
        scalars=1,
    )
    if fast:
        held = jnp.stack([packed] + z_got)
        left, right = held[:, :, :1408], held[:, :, 1408:]
        inner_part, left, right, _ = lax.optimization_barrier((inner_part, left, right, spec))

    blocks = (pieces, seqs * chans, share)
    inner, sect_out = call(
        functools.partial(value_body, fast),
        [((total, width), BF16), (blocks, BF16)],
        [inner_part, norm, perm],
        2,
    )
    sect_in = exchange(sect_out)
    tokens = held_until(tokens, sect_out)
    ahead = [(n, n + 1) for n in range(pieces - 1)]
    halo = lax.ppermute(tokens[:, share - 2 :], "seq", ahead)
    if fast:
        got = held_until((hop(left, 2), hop_y(right)), sect_out)
        left, right = jnp.concatenate([left, got[0]], 0), jnp.concatenate([right, got[1]], 0)
        got = (hop_y(left), hop(right, 2))
        left, right = jnp.concatenate([left, got[0]], 0), jnp.concatenate([right, got[1]], 0)
        sect_in, left, right, halo = lax.optimization_barrier((sect_in, left, right, halo))
    spectra = (count, seqs * chans, 2 * block)
    long_blocks = (count, seqs * chans, block)
    conv_scratch = [
        pltpu.VMEM(spectra, F32),
        pltpu.VMEM(spectra, F32),
        pltpu.VMEM((count, chans, block), F32),
        pltpu.VMEM((count, chans, block), F32),
    ]
    long_out, conv_in, signal = call(
        functools.partial(conv_body, length),
        [(blocks, BF16), (long_blocks, BF16), ((chans, seqs * length), BF16)],
        [sect_in, mix_own, columns, spec, high, low, table_back[:, :block]],
        7,
        scratch=conv_scratch,
    )
    long_in = exchange(long_out)
    if fast:
        got = held_until((hop(left, 1), hop(right, 1)), long_out)
        full, shrink_full, pair = call(
            gather_body,
            [((total, 2 * wide), BF16), ((BLOCKS, wide, width), BF16), ((total, 2 * width), BF16)],
            [me, left, got[0], right, got[1]],
            5,
            scalars=1,
        )

    quad = (BLOCKS, rows, width)
    sect_sw, switch, switch_edge, gate_seq = call(
        functools.partial(switch_body, seqs),
        [(quad, F32), (quad, BF16), ((BLOCKS, 16, width), BF16), (quad, F32)],
        [norm, halo, gains, pair, tw_units[1], kernel],
        1,
    )

    broad = (BLOCKS, rows, wide)
    if fast:
        half_devices = devices // 2
        weight_shapes = [((half_devices, owned, 3 * wide + width), BF16)] * 2
        side_shapes = [((half_devices, owned, width), BF16)] * 2
    else:
        weight_shapes = [((total, 3 * wide + width), F32)]
        side_shapes = [((total, width), F32)]
    (
        layer, lg_out, switch_grad, res_grad, spread_part, squeeze_part, merge_part, gain_part,
        first_rows, *main,
    ) = call(
        functools.partial(middle_body, fast, owned, seqs),
        [
            ((rows, total), BF16), (blocks, BF16), (quad, BF16), (quad, F32),
            ((2, 16, wide), F32), ((16, width), F32), ((16, width), F32), ((BLOCKS, width), F32),
            ((BLOCKS, 2 * seqs, width), BF16),
        ] + weight_shapes,
        [me, long_in, gate_seq, tok, cot, gains, full, shrink_full, pair, tw_units[2],
         sp_units, sq_units, perm],
        27,
        scratch=[pltpu.VMEM(broad, F32)] * 5
        + [pltpu.VMEM(broad, BF16)] * 3
        + [pltpu.VMEM((2, 16, wide), F32)],
        late=(4, 6, 7),
        early=(0, 1, 2, 3),
        scalars=1,
    )
    lg_in = exchange(lg_out)

    after = lax.ppermute(first_rows, "seq", [(to, at) for at, to in ahead])
    n1_sw, small, *side = call(
        functools.partial(switch_back_body, fast, owned, seqs),
        [(quad, F32), ((24, 2 * wide), BF16)] + side_shapes,
        [me, switch_grad, after, switch, switch_edge, sect_sw, pair, tw_units[1], kernel, norm,
         spread_part, squeeze_part, merge_part, gain_part],
        5,
        scalars=1,
    )
    if fast:
        got, side_got, small_got = hop(main[1], 1), hop(side[1], 1), hop(small, 1)
        def sum_shapes(n):
            left, right = ((n + 1, owned, 2 * wide), BF16), ((n, owned, wide + 2 * width), BF16)
            return [left, left, right, right]

        left, left_send, right, right_send = call(
            first_sum_body,
            sum_shapes(half_devices // 2),
            [main[0], got, side[0], side_got, small, small_got],
            4,
        )
        lg_in = held_until(lg_in, left, left_send, right, right_send)

    fg_out, conv_grad, signal_grad = call(
        functools.partial(conv_back_body, length),
        [(blocks, BF16), ((chans, seqs * length), BF16), ((chans, seqs * length), F32)],
        [lg_in, mix_own, columns, spec, high, low, table_back[:, :block]],
        8,
        scratch=conv_scratch,
    )
    fg_in = exchange(fg_out)

    if fast:
        got = held_until((hop_y(left_send), hop(right_send, 2)), fg_out)
        left, left_send, right, right_send = call(
            second_sum_body, sum_shapes(half_devices // 4), [left, got[0], right, got[1]], 3
        )
        lg_in = held_until(lg_in, left, left_send, right, right_send)

    q_rows = chans + 8
    m_rows = order + 8
    (both,) = call(
        functools.partial(filter_back_body, length),
        [((m_rows + q_rows, order), BF16 if fast else F32)],
        [
            lg_in, conv_in, sect_in, signal, conv_grad, signal_grad, s1, c1, s2, c2, read_own,
            mapping, columns, feats, high, low, table_back, same, pick,
        ],
        14,
        scratch=[
            pltpu.VMEM(spectra, F32),
            pltpu.VMEM(long_blocks, F32),
            pltpu.VMEM(long_blocks, F32),
            pltpu.VMEM(spectra, F32),
            pltpu.VMEM((count, chans, 2 * block), F32),
        ],
    )

    if fast:
        got = held_until((hop(left_send, 2), hop_y(right_send)), both)
        shape = ((owned, 5 * wide + 2 * width), BF16)
        own, *sends = call(third_sum_body, [shape] * 4, [left, got[0], right, got[1]], 2)
        z_got = [hop(sent, d) for sent, d in zip(sends, (8, 4, 12))]
        both = added(both, held_until(hop_y(both), own), slice(0, None), BF16)
        fg_in = held_until(fg_in, own, sends, both)

    if fast:
        last_shapes = [((devices, owned * 5 // 3 + 8, 128), BF16)]
    else:
        last_shapes = [((total, width), F32), ((BLOCKS, width), F32)]
    tokens_grad, *pay = call(
        functools.partial(last_body, fast),
        [((rows, total), F32)] + last_shapes,
        [fg_in, perm, inner, norm, n1_sw, res_grad, tok, gains],
        3,
    )
    if fast:
        value_parts = lax.all_to_all(pay[0], BOTH, 0, 0, tiled=True)
    else:
        value_grad = lax.psum_scatter(pay[0], BOTH, scatter_dimension=0, tiled=True)
        gain_one = lax.psum(pay[1], BOTH)

    if fast:
        got = [both] + held_until([hop(both, d) for d in (4, 8, 12)], tokens_grad, z_got)
        m_sum = pair_sum([g[:m_rows] for g in got], BF16)
        both = jnp.concatenate([m_sum] + [g[m_rows:] for g in got], 0)
        z_shapes = [((2, owned, wide), F32), ((2, 16, wide), F32), ((BLOCKS * owned, width), F32)]
        z_shapes += [((2, owned, width), F32), ((BLOCKS, 16, width), F32)]
        expand_grad, spread_sum, shrink_grad, mix_sum, rest_sum = call(
            weights_out_body, z_shapes, [own, *z_got], 4
        )
        got = [both] + held_until([hop(both, d) for d in (2, 1, 3)], rest_sum)
        out_shapes = [(3, 16, width), (3, 2 * total), lifting.shape, (1, order), mapping.shape]
        twiddle_sum, kernel_grad, lifting_grad, phases_grad, mapping_grad, readout_grad = call(
            small_out_body,
            [(shape, F32) for shape in (*out_shapes, readout.shape)],
            [place.astype(jnp.int32).reshape(1), *got, rest_sum, perm],
            3,
            scratch=[pltpu.VMEM((pieces, q_rows, order), F32)],
            scalars=1,
        )
        gains_grad, mixing_grad = call(
            value_out_body,
            [((2, total), F32), ((3, owned, width), F32)],
            [held_until(value_parts, twiddle_sum), mix_sum, rest_sum],
            1,
        )
        squeeze_sum = rest_sum[0]
    else:
        m_sum = lax.psum(both[:m_rows], BOTH)
        q_all = lax.all_gather(lax.psum(both[m_rows:], "batch"), "seq", axis=0, tiled=False)
        main_sum = lax.psum_scatter(main[0], BOTH, scatter_dimension=0, tiled=True)
        switch_own = lax.psum_scatter(side[0], BOTH, scatter_dimension=0, tiled=True)
        small = lax.psum(small.astype(F32), BOTH)
        small = jnp.concatenate([small[:, :wide], small[:, wide : 2 * wide]], 0)

        expand_grad = jnp.stack([main_sum[:, k * wide : (k + 1) * wide] for k in range(2)])
        shrink_grad = main_sum[:, 2 * wide : 3 * wide].reshape(owned, BLOCKS, width)
        shrink_grad = shrink_grad.swapaxes(0, 1).reshape(BLOCKS * owned, width)
        mixing_grad = jnp.stack([value_grad, switch_own, main_sum[:, 3 * wide :]])
        spread_sum = small[:32].reshape(2, 16, wide)
        squeeze_sum, merge_sum, switch_sum, tail_sum = small[32:].reshape(16, BLOCKS, width).swapaxes(0, 1)
        value_sum = q_all[:, chans : chans + BLOCKS, :chans].reshape(pieces, BLOCKS, BLOCKS, span)
        value_sum = value_sum.transpose(1, 2, 0, 3).reshape(16, width)
        twiddle_sum = jnp.stack([value_sum, switch_sum, merge_sum])
        taps_value = q_all[:, chans + BLOCKS : chans + BLOCKS + 3, :chans]
        taps_value = taps_value.reshape(pieces, 3, BLOCKS, span).transpose(1, 2, 0, 3)
        taps_sum = tail_sum[BLOCKS:].reshape(BLOCKS, 3, width).swapaxes(0, 1)
        kernel_grad = jnp.concatenate(
            [taps_value.reshape(3, total), taps_sum.reshape(3, total)], 1
        )
        readout_grad = q_all[:, :chans].reshape(pieces, BLOCKS, span, order)
        readout_grad = readout_grad.transpose(3, 1, 0, 2).reshape(order, total)
        gains_grad = jnp.stack([gain_one.reshape(total), tail_sum[:BLOCKS].reshape(total)])
        lifting_grad = m_sum[order : order + lifting.shape[0]]
        phases_grad = m_sum[order + lifting.shape[0]]
        mapping_grad = m_sum[:order]

    def of_units(rows_now):
        lead = rows_now.shape[:-2]
        shaped = rows_now.reshape(*lead, BLOCKS, BLOCKS, rows_now.shape[-1])
        return jnp.moveaxis(shaped, -1, -3)

    return (
        layer.reshape(seqs, share, total),
        tokens_grad.reshape(seqs, share, total),
        gains_grad,
        mixing_grad,
        of_units(twiddle_sum),
        expand_grad,
        of_units(spread_sum),
        shrink_grad,
        of_units(squeeze_sum),
        kernel_grad,
        lifting_grad,
        phases_grad.reshape(order),
        mapping_grad,
        readout_grad,
    )


def solution(mesh):
    return jax.shard_map(
        per_device,
        mesh=mesh,
        in_specs=(
            P("batch", "seq", None),
            P("batch", "seq", None),
            P(),
            P(None, ("seq", "batch"), None),
            P(),
            P(None, ("seq", "batch"), None),
            P(),
            P(("seq", "batch"), None),
            P(),
            P(),
            P(),
            P(),
            P(),
            P(),
            P(),
        ),
        out_specs=(
            P("batch", "seq", None),
            P("batch", "seq", None),
            P(),
            P(None, ("seq", "batch"), None),
            P(),
            P(None, ("seq", "batch"), None),
            P(),
            P(("seq", "batch"), None),
            P(),
            P(),
            P(),
            P(),
            P(),
            P(),
        ),
        check_vma=False,
    )
```

```python
import functools
import math

import jax
import jax.numpy as jnp
import numpy as np
from jax import lax
from jax.experimental import pallas as pl
from jax.experimental.pallas import tpu as pltpu
from jax.sharding import PartitionSpec as P

BLOCKS = 4
BOTH = ("seq", "batch")
F32 = jnp.float32
BF16 = jnp.bfloat16
HIGHEST = lax.Precision.HIGHEST
LIMIT = 52
NN = ((1,), (0,))
NT = ((1,), (1,))
TN = ((0,), (0,))


def mm(left, right, dims=NN, precision=None):
    return lax.dot_general(
        left, right, (dims, ((), ())), preferred_element_type=F32, precision=precision
    )


class Late:
    def __init__(self, source, held, done):
        self.held, self.waiting = held, pltpu.make_async_copy(source, held, done)
        self.waiting.start()

    def ready(self):
        if self.waiting is not None:
            self.waiting.wait()
            self.waiting = None
        return self.held


class Early:
    def __init__(self, target, held, done):
        self.ref, self.copy, self.left = held, pltpu.make_async_copy(held, target, done), False

    def leave(self):
        if not self.left:
            self.copy.start()
            self.left = True


def call(body, outs, operands, micros, scratch=(), scalars=0, limit=LIMIT, late=(), early=()):
    specs = [
        pl.BlockSpec(
            memory_space=pl.ANY if k in late else pltpu.SMEM if k < scalars else pltpu.VMEM
        )
        for k in range(len(operands))
    ]
    out_specs = [
        pl.BlockSpec(memory_space=pl.ANY if k in early else pltpu.VMEM) for k in range(len(outs))
    ]
    staging = [pltpu.VMEM(operands[k].shape, operands[k].dtype) for k in late]
    staging += [pltpu.VMEM(*outs[k]) for k in early]
    count = len(staging)

    def whole(*refs):
        refs = list(refs)
        held = refs[len(operands) + len(outs) :][:count]
        rest = refs[len(operands) + len(outs) + count :]
        if not count:
            body(*refs)
            return
        done, rest = rest[0], rest[1:]
        for n, k in enumerate(late):
            refs[k] = Late(refs[k], held[n], done.at[n])
        for n, k in enumerate(early):
            at = len(operands) + k
            refs[at] = Early(refs[at], held[len(late) + n], done.at[len(late) + n])
        body(*refs[: len(operands) + len(outs)], *rest)
        for k in early:
            refs[len(operands) + k].leave()
        for k in early:
            refs[len(operands) + k].copy.wait()
        for k in late:
            refs[k].ready()

    if count:
        staging.append(pltpu.SemaphoreType.DMA((count,)))
    return pl.pallas_call(
        whole,
        out_shape=[jax.ShapeDtypeStruct(shape, kind) for shape, kind in outs],
        in_specs=specs,
        out_specs=out_specs,
        scratch_shapes=staging + list(scratch),
        compiler_params=pltpu.CompilerParams(vmem_limit_bytes=limit << 20),
        cost_estimate=pl.CostEstimate(
            flops=int(micros * 0.8e9), bytes_accessed=1 << 16, transcendentals=0
        ),
    )(*operands)


def packed_tables(points):
    size = 2 * points
    place = np.arange(size)[:, None].astype(np.int64)
    bins = np.arange(points)[None, :]
    angle = 2.0 * np.pi / size * ((place * bins) % size)
    forward = np.concatenate([np.cos(angle), -np.sin(angle)], 1)
    forward[:, points] = np.where(np.arange(size) % 2 == 0, 1.0, -1.0)
    weight = np.where(np.arange(size) % points == 0, 1.0, 2.0) / size
    backward = (forward * weight[None, :]).T
    return forward.astype(np.float32), np.ascontiguousarray(backward).astype(np.float32)


def split_table(table):
    high = table.astype(jnp.bfloat16)
    low = (table - high.astype(np.float32)).astype(jnp.bfloat16)
    return high, low


def feature_rows(length):
    place = np.arange(length)
    rows = [place / length]
    for harmonic in (1, 2):
        angle = 2.0 * np.pi / length * ((harmonic * place) % length)
        rows += [np.cos(angle), np.sin(angle)]
    rows += [np.ones(length), np.zeros(length), np.zeros(length)]
    return np.stack(rows).astype(np.float32)


def spread_matrix(pieces, span):
    width = pieces * span
    out = np.zeros((BLOCKS, pieces, BLOCKS, span, width), np.float32)
    for b in range(BLOCKS):
        for piece in range(pieces):
            for k in range(span):
                out[b, piece, b, k, piece * span + k] = 1.0
    return out.reshape(BLOCKS, pieces * BLOCKS * span, width).astype(jnp.bfloat16)


def normalize_rows(values):
    centred = values - jnp.mean(values, -1, keepdims=True)
    factor = lax.rsqrt(jnp.mean(centred * centred, -1, keepdims=True) + 1e-05)
    return centred * factor, factor


def sincos(angle):
    turns = (angle * (2.0 / math.pi) + 12582912.0) - 12582912.0
    rest = (angle - turns * 1.5703125) - turns * 4.83826794896619e-4
    square = rest * rest
    sine = rest + rest * square * (
        -1.6666654611e-1 + square * (8.3321608736e-3 + square * -1.9515295891e-4)
    )
    cosine = (
        1.0
        - 0.5 * square
        + square
        * square
        * (4.166664568298827e-2 + square * (-1.388731625493765e-3 + square * 2.443315711809948e-5))
    )
    quarter = turns.astype(jnp.int32)
    odd = jnp.bitwise_and(quarter, 1) == 1
    sine_sign = (1 - jnp.bitwise_and(quarter, 2)).astype(F32)
    cosine_sign = (1 - jnp.bitwise_and(quarter + 1, 2)).astype(F32)
    return (
        jnp.where(odd, cosine, sine) * sine_sign,
        jnp.where(odd, sine, cosine) * cosine_sign,
    )


def parts_of(values):
    width = values.shape[1] // BLOCKS
    return [values[:, k * width : (k + 1) * width] for k in range(BLOCKS)]


def mix(sectioned, rows):
    return [
        sum(sectioned[a] * rows[4 * a + b : 4 * a + b + 1, :] for a in range(BLOCKS))
        for b in range(BLOCKS)
    ]


def unmix(upstream, rows):
    return [
        sum(upstream[b] * rows[4 * a + b : 4 * a + b + 1, :] for b in range(BLOCKS))
        for a in range(BLOCKS)
    ]


def mix_grad(sectioned, upstream):
    return jnp.concatenate(
        [
            jnp.sum(sectioned[a] * upstream[b], 0, keepdims=True)
            for a in range(BLOCKS)
            for b in range(BLOCKS)
        ],
        0,
    )


def lane_of(shape):
    return lax.broadcasted_iota(jnp.int32, shape, len(shape) - 1)


def row_of(shape):
    return lax.broadcasted_iota(jnp.int32, shape, 0)


def time_rows(block_ref, span):
    pieces, rows, _ = block_ref.shape
    return jnp.concatenate(
        [
            block_ref[n].astype(F32)[s * span : (s + 1) * span]
            for s in range(rows // span)
            for n in range(pieces)
        ],
        1,
    )


def later_lanes(values, steps, length):
    total = values.shape[1]
    moved = pltpu.roll(values, total - steps, 1)
    return jnp.where(lane_of(values.shape) % length < length - steps, moved, 0.0)


def earlier_lanes(values, steps, length):
    moved = pltpu.roll(values, steps, 1)
    return jnp.where(lane_of(values.shape) % length >= steps, moved, 0.0)


def to_pieces(lanes_now, out_ref, length):
    pieces, _, width = out_ref.shape
    seqs = lanes_now.shape[1] // length
    for n in range(pieces):
        out_ref[n] = jnp.concatenate(
            [
                lanes_now[:, s * length + n * width : s * length + (n + 1) * width]
                for s in range(seqs)
            ],
            0,
        ).astype(BF16)


def spectrum(flat, high_ref, low_ref, out_ref):
    out = mm(flat, high_ref[...]) + mm(flat, low_ref[...])
    out_ref[...] = out.reshape(out_ref.shape)


def mm2(left, right, dims=NN):
    left_high = left.astype(BF16)
    left_low = (left - left_high.astype(F32)).astype(BF16)
    return mm(left_low, right, dims) + mm(left_high, right, dims)


def mm3(left, right, dims=NN):
    left_high, right_high = left.astype(BF16), right.astype(BF16)
    left_low = (left - left_high.astype(F32)).astype(BF16)
    right_low = (right - right_high.astype(F32)).astype(BF16)
    return (
        mm(left_high, right_low, dims) + mm(left_low, right_high, dims)
    ) + mm(left_high, right_high, dims)


def nyquist_split(spec):
    half = spec.shape[-1] // 2
    real, imaginary = spec[..., :half], spec[..., half:]
    first = lane_of(real.shape) == 0
    return jnp.where(first, 0.0, imaginary), jnp.where(first, imaginary, real)


def norm_body(tok_ref, gains_ref, norm_ref):
    norm = normalize_rows(tok_ref[...].astype(F32))[0] * gains_ref[0:1, :]
    norm_ref[...] = norm.astype(BF16)


def unit_rows(ref):
    return jnp.concatenate([ref[a].astype(F32) for a in range(BLOCKS)], 0)


def filter_body(
    place_ref, lift_ref, phase_ref, map_ref, read_all, damp_all, taps_all, tw_ref, perm_ref, feat_ref,
    table_ref, s1, c1, s2, c2, spec_ref, read_ref, columns_ref, mix_ref,
):
    span = read_ref.shape[1]
    at = pl.ds(pl.multiple_of(place_ref[0] * span, span), span)
    chosen = [perm_ref[b, at, :] for b in range(BLOCKS)]
    width = perm_ref.shape[2]
    read_ref[...] = sum(
        mm(read_all[:, b * width : (b + 1) * width], chosen[b].astype(F32), NT, HIGHEST)
        for b in range(BLOCKS)
    )
    rows = jnp.concatenate([damp_all[...], taps_all[...], jnp.zeros((4, BLOCKS * width), F32)], 0)
    columns = sum(
        mm(chosen[b].astype(F32), rows[:, b * width : (b + 1) * width], NT, HIGHEST)
        for b in range(BLOCKS)
    )
    columns_ref[...] = columns
    factors = unit_rows(tw_ref)
    mix_ref[...] = sum(
        mm((chosen[b] * factors[4 * a + b : 4 * a + b + 1].astype(BF16)), chosen[a], NT)
        for a in range(BLOCKS)
        for b in range(BLOCKS)
    ).astype(BF16)
    lift = jnp.concatenate(
        [lift_ref[...], phase_ref[...], jnp.zeros((7 - lift_ref.shape[0], map_ref.shape[0]), F32)], 0
    )
    sine_one, cosine_one = sincos(mm(lift, feat_ref[...], TN, HIGHEST))
    s1[...] = sine_one.astype(BF16)
    c1[...] = cosine_one.astype(BF16)
    sine_two, cosine_two = sincos(mm(map_ref[...], sine_one, TN, HIGHEST))
    s2[...] = sine_two.astype(BF16)
    c2[...] = cosine_two.astype(BF16)
    shape = (read_ref.shape[1], sine_two.shape[1])
    place = lane_of(shape).astype(F32)
    response = mm(read_ref[...], sine_two, TN, HIGHEST) * jnp.exp(-place * columns[:, 0:1])
    pieces, span, doubled = spec_ref.shape
    width = doubled // 2
    zero = jnp.zeros((span, width), F32)
    rows = []
    for k in range(pieces):
        now = response[:, k * width : (k + 1) * width]
        before = response[:, (k - 1) * width : k * width] if k else zero
        rows.append(
            jnp.concatenate([now, jnp.where(lane_of(before.shape) == 0, 0.0, before)], 1)
        )
    spec = mm3(jnp.concatenate(rows, 0), table_ref[...])
    spec_ref[...] = spec.reshape(pieces, span, doubled)


def value_body(packed, *refs):
    if packed:
        held_ref, norm_ref, perm_ref, full_ref, out_ref = refs
        rows = held_ref.shape[1] * 3 // 5
        share = held_ref.shape[0] // BLOCKS
        inner = []
        for a in range(BLOCKS):
            blocks = []
            for k in range(a * share, (a + 1) * share):
                held = held_ref[k].astype(F32)
                blocks.append(unpack_rows(held, rows))
            inner.append(jnp.concatenate(blocks, 0).astype(BF16))
            full_ref[a * rows * share : (a + 1) * rows * share, :] = inner[a]
    else:
        inner_ref, norm_ref, perm_ref, full_ref, out_ref = refs
        full_ref[...] = inner_ref[...]
        width = full_ref.shape[1]
        inner = [full_ref[a * width : (a + 1) * width, :] for a in range(BLOCKS)]
    norm = parts_of(norm_ref[...])
    first = [mm(norm[a], inner[a]).astype(BF16) for a in range(BLOCKS)]
    send_pieces(first, perm_ref, out_ref)


def pack_rows(values):
    rows = values.shape[0]
    rest = [values[k : k + 8, 128:] for k in range(0, rows, 8)] + [jnp.zeros_like(values[:8, 128:])]
    pairs = [jnp.concatenate(rest[k : k + 2], 1) for k in range(0, rows // 8, 2)]
    return jnp.concatenate([values[:, :128]] + pairs, 0)


def unpack_rows(held, rows):
    rest = []
    for k in range(rows // 8):
        start = rows + 8 * (k // 2)
        rest.append(held[start : start + 8, 64 * (k % 2) : 64 * (k % 2) + 64])
    return jnp.concatenate([held[:rows], jnp.concatenate(rest, 0)], 1)


def gather_body(
    me_ref, left_own, left_other, right_own, right_other, wide_ref, shrink_ref, pair_ref
):
    rows, cut = left_own.shape[1:]
    width = shrink_ref.shape[2]
    first = wide_ref.shape[1]
    last = first + BLOCKS * width
    count = 2 * left_own.shape[0]
    per = 2 if rows % 16 else 1
    for k in range(0, count, per):
        blocks = []
        for owner in range(k, k + per):
            bits = apart_bits(me_ref, owner)
            deep = bits[3] + 2 * bits[4]
            left = bits[0] * 8 + bits[2] * 4 + deep
            right = bits[2] * 8 + bits[0] * 4 + deep
            near = bits[1] == 0
            blocks.append(
                jnp.concatenate(
                    [
                        jnp.where(near, left_own[left].astype(F32), left_other[left].astype(F32)),
                        jnp.where(
                            near, right_own[right].astype(F32), right_other[right].astype(F32)
                        ),
                    ],
                    1,
                )
            )
        block = jnp.concatenate(blocks, 0).astype(BF16)
        wide_ref[k * rows : (k + per) * rows, :] = block[:, :first]
        pair_ref[k * rows : (k + per) * rows, :] = block[:, last:]
        for n, block in enumerate(blocks):
            parts = [block[:, first + g * width : first + (g + 1) * width] for g in range(BLOCKS)]
            at = (k + n) * BLOCKS * rows
            here = slice(at % shrink_ref.shape[1], at % shrink_ref.shape[1] + BLOCKS * rows)
            shrink_ref[at // shrink_ref.shape[1], here, :] = jnp.concatenate(parts, 0).astype(BF16)


def send_pieces(parts, perm_ref, out_ref):
    pieces, rows, width = out_ref.shape
    seqs = parts[0].shape[0] // width
    span = rows // seqs
    turned = [
        sum(
            mm(perm_ref[k], parts[k][s * width : (s + 1) * width], NT) for k in range(BLOCKS)
        )
        for s in range(seqs)
    ]
    for n in range(pieces):
        out_ref[n] = jnp.concatenate(
            [turned[s][n * span : (n + 1) * span] for s in range(seqs)], 0
        ).astype(BF16)


def receive_pieces(in_ref, perm_ref):
    pieces, rows, width = in_ref.shape
    seqs = rows * pieces // (BLOCKS * perm_ref.shape[2])
    span = rows // seqs
    held = [in_ref[n].astype(F32) for n in range(pieces)]
    turned = [
        jnp.concatenate([h[s * span : (s + 1) * span] for h in held], 0).T.astype(BF16)
        for s in range(seqs)
    ]
    return [
        jnp.concatenate([mm(turned[s], perm_ref[k]) for s in range(seqs)], 0)
        for k in range(BLOCKS)
    ]


def earlier_rows(values, halo, steps):
    moved = pltpu.roll(values, steps, 0)
    row = row_of(values.shape)
    for k in range(steps):
        moved = jnp.where(row == k, halo[2 - steps + k : 3 - steps + k], moved)
    return moved


def later_rows(values, halo, steps):
    count = values.shape[0]
    moved = pltpu.roll(values, count - steps, 0)
    row = row_of(values.shape)
    for k in range(steps):
        moved = jnp.where(row == count - steps + k, halo[k : k + 1], moved)
    return moved


def per_sequence(function, values, halo, seqs, steps):
    count = values.shape[0] // seqs
    return jnp.concatenate(
        [
            function(values[s * count : (s + 1) * count], halo[2 * s : 2 * s + 2], steps)
            for s in range(seqs)
        ],
        0,
    )


def switch_body(
    seqs, norm_ref, halo_ref, gains_ref, full_ref, tw_ref, taps_ref, sect_ref, sw_ref, sh_ref, gate_ref
):
    width = norm_ref.shape[1] // BLOCKS
    edge = jnp.concatenate([halo_ref[s].astype(F32) for s in range(seqs)], 0)
    edge = jnp.concatenate([edge, jnp.zeros((16 - 2 * seqs, edge.shape[1]), F32)], 0)
    edge_norm = normalize_rows(edge)[0] * gains_ref[0:1, :]
    norm, halo = parts_of(norm_ref[...]), parts_of(edge_norm.astype(BF16))
    inner = [full_ref[a * width : (a + 1) * width, :][:, :width] for a in range(BLOCKS)]
    first = [mm(norm[a], inner[a]) for a in range(BLOCKS)]
    for a in range(BLOCKS):
        sect_ref[a] = first[a]
    rows = unit_rows(tw_ref)
    all_taps = parts_of(taps_ref[...][:, BLOCKS * width :])
    switch = mix(first, rows)
    edge = mix([mm(halo[a], inner[a]) for a in range(BLOCKS)], rows)
    for b in range(BLOCKS):
        sw_ref[b] = switch[b].astype(BF16)
        sh_ref[b] = edge[b].astype(BF16)
        now = switch[b].astype(BF16).astype(F32)
        before = edge[b].astype(BF16).astype(F32)
        taps = all_taps[b]
        gate_ref[b] = (
            taps[0:1] * now
            + taps[1:2] * per_sequence(earlier_rows, now, before, seqs, 1)
            + taps[2:3] * per_sequence(earlier_rows, now, before, seqs, 2)
        )


def loop(start, stop, body, carry, unrolled):
    if not unrolled:
        return lax.fori_loop(start, stop, body, carry)
    for step in range(start, stop):
        carry = body(step, carry)
    return carry


def bins_of(half):
    return [(slice(k, k + 128), slice(half + k, half + k + 128)) for k in range(0, half, 128)]


def convolve(spec_ref, b_ref, c_ref, x_ref, y_ref):
    pieces, rows, doubled = x_ref.shape
    span = spec_ref.shape[1]
    zero = jnp.zeros((span, 128), F32)
    parts = [slice(k, k + span) for k in range(0, rows, span)]
    for low, up in bins_of(doubled // 2):

        def outer(i, carry, low=low, up=up):
            def inner(j, totals):
                k = i - j
                a_now, b_now, c_now = spec_ref[k, :, low], b_ref[k, :, low], c_ref[k, :, low]
                out = []
                for s, at in enumerate(parts):
                    real, imag = x_ref[j, at, low], x_ref[j, at, up]
                    out.append(totals[2 * s] + a_now * real - b_now * imag)
                    out.append(totals[2 * s + 1] + b_now * real + c_now * imag)
                return tuple(out)

            totals = loop(0, i + 1, inner, (zero,) * (2 * len(parts)), pieces <= 8)
            for s, at in enumerate(parts):
                y_ref[i, at, low] = totals[2 * s]
                y_ref[i, at, up] = totals[2 * s + 1]
            return carry

        loop(0, pieces, outer, 0, pieces <= 8)


def correlate(spec_ref, b_ref, c_ref, g_ref, y_ref):
    pieces, rows, doubled = g_ref.shape
    span = spec_ref.shape[1]
    zero = jnp.zeros((span, 128), F32)
    parts = [slice(k, k + span) for k in range(0, rows, span)]
    for low, up in bins_of(doubled // 2):

        def outer(j, carry, low=low, up=up):
            def inner(i, totals):
                k = i - j
                a_now, b_now, c_now = spec_ref[k, :, low], b_ref[k, :, low], c_ref[k, :, low]
                out = []
                for s, at in enumerate(parts):
                    real, imag = g_ref[i, at, low], g_ref[i, at, up]
                    out.append(totals[2 * s] + a_now * real + b_now * imag)
                    out.append(totals[2 * s + 1] + c_now * imag - b_now * real)
                return tuple(out)

            totals = loop(j, pieces, inner, (zero,) * (2 * len(parts)), pieces <= 8)
            for s, at in enumerate(parts):
                y_ref[j, at, low] = totals[2 * s]
                y_ref[j, at, up] = totals[2 * s + 1]
            return carry

        loop(0, pieces, outer, 0, pieces <= 8)


def block_rows(piece_ref, block):
    pieces, _, width = piece_ref.shape
    each = block // width
    return jnp.concatenate(
        [
            jnp.concatenate([piece_ref[n + k] for k in range(each)], 1)
            for n in range(0, pieces, each)
        ],
        0,
    )


def conv_body(
    length, sect_ref, mix_ref, taps_ref, spec_ref, high_ref, low_ref, back_ref,
    out_ref, cin_ref, signal_ref, x_ref, y_ref, b_ref, c_ref,
):
    span = spec_ref.shape[1]
    lanes_now = time_rows(sect_ref, span).astype(BF16)
    signal = mm(mix_ref[...], lanes_now).astype(BF16)
    signal_ref[...] = signal
    signal = signal.astype(F32)
    conv_in = (
        taps_ref[:, 1:2] * signal
        + taps_ref[:, 2:3] * earlier_lanes(signal, 1, length)
        + taps_ref[:, 3:4] * earlier_lanes(signal, 2, length)
    )
    to_pieces(conv_in, cin_ref, length)
    spectrum(cin_ref[...].reshape(-1, cin_ref.shape[2]), high_ref, low_ref, x_ref)
    b_ref[...], c_ref[...] = nyquist_split(spec_ref[...])
    convolve(spec_ref, b_ref, c_ref, x_ref, y_ref)
    pieces, rows, doubled = y_ref.shape
    out = mm3(y_ref[...].reshape(pieces * rows, doubled), back_ref[...]).astype(BF16)
    width = out_ref.shape[2]
    each = doubled // 2 // width
    for n in range(pieces):
        for k in range(each):
            out_ref[n * each + k] = out[n * rows : (n + 1) * rows, k * width : (k + 1) * width]


def middle_body(
    fast, owned, seqs, me_ref, long_ref, gate_ref, tok_ref, cot_ref, gains_ref, full_ref, shrink_ref, pair_ref,
    tw_ref, spread_ref, sq_ref, perm_ref, layer_ref, lg_ref, swg_ref, res_ref, spg_ref, sqg_ref, twg_ref, gain_ref, edge_ref, *refs,
):
    *weight_outs, fg, fu, act, ug, hg, hid_ref, fgate_ref, fup_ref, sp_ref = refs
    for k in range(2):
        sp_ref[k] = unit_rows(spread_ref.at[k])
    rows, total = tok_ref.shape
    width = total // BLOCKS
    wide = fg.shape[2]
    tw_rows, sq_rows = unit_rows(tw_ref), unit_rows(sq_ref)
    gate = [gate_ref[b] for b in range(BLOCKS)]
    long_out = receive_pieces(long_ref, perm_ref)
    gated = [(gate[b] * long_out[b]).astype(BF16) for b in range(BLOCKS)]
    at = [slice(a * width, (a + 1) * width) for a in range(BLOCKS)]
    merge = [pair_ref[at[a], :][:, width:] for a in range(BLOCKS)]
    sect_merge = [mm(gated[a], merge[a]) for a in range(BLOCKS)]
    merged = mix(sect_merge, tw_rows)
    tokens = parts_of(tok_ref[...].astype(F32))
    residual = [tokens[b] + merged[b] for b in range(BLOCKS)]
    mean = sum(jnp.sum(r, -1, keepdims=True) for r in residual) / total
    centred = [r - mean for r in residual]
    variance = sum(jnp.sum(c * c, -1, keepdims=True) for c in centred) / total
    factor = lax.rsqrt(variance + 1e-05)
    normed = [c * factor for c in centred]
    gain = parts_of(gains_ref[1:2, :])
    norm_two = [(normed[a] * gain[a]).astype(BF16) for a in range(BLOCKS)]
    full_ref = full_ref.ready()
    for a in range(BLOCKS):
        fg[a] = mm(norm_two[a], full_ref[at[a], :wide])
        fu[a] = mm(norm_two[a], full_ref[at[a], wide : 2 * wide])

    step = 64
    lanes = 128

    def forward_lane(l, carry):
        here = pl.ds(pl.multiple_of(l * lanes, lanes), lanes)

        def forward_row(r, inner_carry):
            down = pl.ds(pl.multiple_of(r * step, step), step)
            gate_pre = mix([fg[a, down, here] for a in range(BLOCKS)], sp_ref[0, :, here])
            held = []
            for v in gate_pre:
                square = v * v
                half = 0.5 + 0.5 * jnp.tanh(v * (0.7978845608 + 0.0356774081 * square))
                active = v * half
                steep = 1.5957691216 + 0.2140644488 * square
                held.append((active, half + active * (1.0 - half) * steep))
            up_pre = mix([fu[a, down, here] for a in range(BLOCKS)], sp_ref[1, :, here])
            for b in range(BLOCKS):
                active, slope = held[b]
                hid_ref[b, down, here] = (active * up_pre[b]).astype(BF16)
                act[b, down, here] = active
                ug[b, down, here] = up_pre[b] * slope
            return inner_carry

        return lax.fori_loop(0, rows // step, forward_row, carry, unroll=4)

    lax.fori_loop(0, wide // lanes, forward_lane, 0)

    shrink_ref = shrink_ref.ready()
    shrink = [shrink_ref[a] for a in range(BLOCKS)]
    sect_down = [mm(hid_ref[a], shrink[a]) for a in range(BLOCKS)]
    lowered = mix(sect_down, sq_rows)
    layer_ref.ref[...] = jnp.concatenate(
        [(residual[b] + lowered[b]).astype(BF16) for b in range(BLOCKS)], 1
    )
    layer_ref.leave()
    upstream = parts_of(cot_ref.ready()[...].astype(F32))
    sqg_ref[...] = mix_grad(sect_down, upstream)
    back_down = unmix(upstream, sq_rows)
    back_down = [v.astype(BF16) for v in back_down]
    for a in range(BLOCKS):
        hg[a] = mm(back_down[a], shrink[a], NT)

    def backward_lane(l, carry):
        here = pl.ds(pl.multiple_of(l * lanes, lanes), lanes)
        zero = jnp.zeros((8, lanes), F32)
        for k, (held, slopes, out_ref) in enumerate(((fg, ug, fgate_ref), (fu, act, fup_ref))):

            def backward_row(r, sums, k=k, held=held, slopes=slopes, out_ref=out_ref):
                down = pl.ds(pl.multiple_of(r * step, step), step)
                grads = [hg[b, down, here] * slopes[b, down, here] for b in range(BLOCKS)]
                for a, value in enumerate(unmix(grads, sp_ref[k, :, here])):
                    out_ref[a, down, here] = value.astype(BF16)
                out = []
                for a in range(BLOCKS):
                    value = held[a, down, here]
                    for b in range(BLOCKS):
                        product = value * grads[b]
                        for n in range(0, step, 16):
                            pair = product[n : n + 8] + product[n + 8 : n + 16]
                            part = pair if n == 0 else part + pair
                        out.append(sums[4 * a + b] + part)
                return tuple(out)

            sums = lax.fori_loop(0, rows // step, backward_row, (zero,) * 16, unroll=4)
            for n in range(16):
                spg_ref[k, pl.ds(n, 1), here] = jnp.sum(sums[n], 0, keepdims=True)
        return carry

    lax.fori_loop(0, wide // lanes, backward_lane, 0)

    n2_grad = [
        mm(fgate_ref[a], full_ref[at[a], :wide], NT)
        + mm(fup_ref[a], full_ref[at[a], wide : 2 * wide], NT)
        for a in range(BLOCKS)
    ]
    scaled = [n2_grad[a] * gain[a] for a in range(BLOCKS)]
    plain = sum(jnp.sum(v, -1, keepdims=True) for v in scaled) / total
    joint = sum(jnp.sum(scaled[a] * normed[a], -1, keepdims=True) for a in range(BLOCKS)) / total
    res_grad = [
        upstream[a] + factor * (scaled[a] - plain - normed[a] * joint) for a in range(BLOCKS)
    ]
    gain_ref[...] = jnp.concatenate(
        [jnp.sum(n2_grad[a] * normed[a], 0, keepdims=True) for a in range(BLOCKS)], 0
    )
    for a in range(BLOCKS):
        res_ref.ref[a] = res_grad[a]
    res_ref.leave()
    twg_ref[...] = mix_grad(sect_merge, res_grad)
    back_merge = [v.astype(BF16) for v in unmix(res_grad, tw_rows)]
    long_grad = []
    for a in range(BLOCKS):
        gated_grad = mm(back_merge[a], merge[a], NT)
        long_grad.append((gated_grad * gate[a]).astype(BF16))
        now = (gated_grad * long_out[a]).astype(BF16)
        swg_ref.ref[a] = now
        share = rows // seqs
        edge_ref[a] = jnp.concatenate([now[s * share : s * share + 2] for s in range(seqs)], 0)
    swg_ref.leave()
    send_pieces(long_grad, perm_ref, lg_ref.ref)
    lg_ref.leave()

    for a in range(BLOCKS):
        from_hidden = mm(hid_ref[a], back_down[a], TN)
        group = BLOCKS * owned
        down = [
            jnp.concatenate(
                [
                    from_hidden[o + g * owned : o + (g + 1) * owned]
                    for o in range(0, wide, group)
                ],
                0,
            )
            for g in range(BLOCKS)
        ]
        held = jnp.concatenate(
            [mm(norm_two[a], fgate_ref[a], TN), mm(norm_two[a], fup_ref[a], TN)]
            + down
            + [mm(gated[a], back_merge[a], TN)],
            1,
        )

        def block_of(k, count, held=held):
            return held[k * count : (k + 1) * count]

        outs = weight_outs if fast else (weight_outs[0], owned)
        put_blocks(fast, me_ref, outs, a, block_of, width, 2 * wide)


def switch_back_body(
    fast, owned, seqs, me_ref, swg_ref, next_ref, sw_ref, sh_ref, sect_ref, full_ref, tw_ref, taps_ref,
    norm_ref, spg_ref, sqg_ref, mg_ref, gain_ref, n1_ref, small_ref, *outs,
):
    width = swg_ref.shape[2]
    all_taps = parts_of(taps_ref[...][:, BLOCKS * width :])
    back, taps_grad = [], []
    for b in range(BLOCKS):
        grad = swg_ref[b].astype(F32)
        after = next_ref[b].astype(F32)
        taps = all_taps[b]
        back.append(
            taps[0:1] * grad
            + taps[1:2] * per_sequence(later_rows, grad, after, seqs, 1)
            + taps[2:3] * per_sequence(later_rows, grad, after, seqs, 2)
        )
        now, before = sw_ref[b].astype(F32), sh_ref[b].astype(F32)
        shifted = [now] + [per_sequence(earlier_rows, now, before, seqs, m) for m in (1, 2)]
        taps_grad += [jnp.sum(value * grad, 0, keepdims=True) for value in shifted]
    tw_grad = mix_grad([sect_ref[a] for a in range(BLOCKS)], back)
    rest = [sqg_ref[...], mg_ref[...], tw_grad, jnp.concatenate([gain_ref[...]] + taps_grad, 0)]
    small = jnp.concatenate([spg_ref[0], spg_ref[1], jnp.concatenate(rest, 1)], 0)
    count = small_ref.shape[0]
    small_ref[...] = jnp.concatenate([small[:count], small[count:]], 1).astype(BF16)
    first = unmix(back, unit_rows(tw_ref))
    norm = parts_of(norm_ref[...])
    for a in range(BLOCKS):
        now = first[a].astype(BF16)
        n1_ref[a] = mm(now, full_ref[a * width : (a + 1) * width, :][:, :width], NT)
        held = mm(norm[a], now, TN)

        def block_of(k, count, held=held):
            return held[k * count : (k + 1) * count]

        put_blocks(fast, me_ref, outs if fast else (outs[0], owned), a, block_of, width, 0)


def apart_bits(me_ref, owner):
    apart = jnp.bitwise_xor(me_ref[0], owner)
    return [jnp.bitwise_and(lax.shift_right_logical(apart, n), 1) for n in range(5)]


def put_blocks(fast, me_ref, outs, a, block_of, width, start):
    rows = outs[0].shape[-2] if fast else outs[1]
    for k in range(width // rows):
        block = block_of(k, rows)
        if not fast:
            outs[0][a * width + k * rows : a * width + (k + 1) * rows, :] = block
            continue
        keep_ref, send_ref = outs
        block = block.astype(BF16)
        bits = apart_bits(me_ref, a * (width // rows) + k)
        deep = bits[3] * 2 + bits[4]
        for ref, core in ((keep_ref, 0), (send_ref, 1)):

            @pl.when(bits[1] == core)
            def _(ref=ref, block=block, bits=bits, deep=deep):
                if start:
                    ref[bits[0] * 8 + bits[2] * 4 + deep, :, :start] = block[:, :start]
                ref[bits[2] * 8 + bits[0] * 4 + deep, :, start:] = block[:, start:]


def conv_back_body(
    length, g_ref, mix_ref, taps_ref, spec_ref, high_ref, low_ref, back_ref,
    out_ref, cg_ref, sg_ref, x_ref, y_ref, b_ref, c_ref,
):
    span = spec_ref.shape[1]
    spectrum(block_rows(g_ref, x_ref.shape[2] // 2), high_ref, low_ref, x_ref)
    b_ref[...], c_ref[...] = nyquist_split(spec_ref[...])
    correlate(spec_ref, b_ref, c_ref, x_ref, y_ref)
    pieces, rows, doubled = y_ref.shape
    flat = mm3(y_ref[...].reshape(pieces * rows, doubled), back_ref[...])
    flat = flat.astype(BF16).astype(F32)
    grad = jnp.concatenate(
        [
            flat[n * rows + s * span : n * rows + (s + 1) * span]
            for s in range(rows // span)
            for n in range(pieces)
        ],
        1,
    )
    cg_ref[...] = grad.astype(BF16)
    signal_grad = (
        taps_ref[:, 1:2] * grad
        + taps_ref[:, 2:3] * later_lanes(grad, 1, length)
        + taps_ref[:, 3:4] * later_lanes(grad, 2, length)
    )
    sg_ref[...] = signal_grad
    to_pieces(mm(mix_ref[...].astype(F32), signal_grad, TN, HIGHEST), out_ref, length)


def filter_back_body(
    length, g_ref, cin_ref, sect_ref, signal_ref, cg_ref, sg_ref, s1, c1, s2, c2, read_ref, map_ref,
    damp_ref, feat_ref, high_ref, low_ref, back_ref, same_ref, pick_ref,
    out_ref, x_ref, b_ref, c_ref, gs_ref, p_ref,
):
    pieces, span, doubled = p_ref.shape
    half = doubled // 2
    spectrum(cin_ref[...].reshape(-1, half), high_ref, low_ref, x_ref)
    b_ref[...], c_ref[...] = nyquist_split(x_ref[...])
    spectrum(block_rows(g_ref, half), high_ref, low_ref, gs_ref)
    seqs = x_ref.shape[1] // span
    zero = jnp.zeros((span, 128), F32)
    parts = [slice(k, k + span) for k in range(0, seqs * span, span)]
    for low, up in bins_of(half):

        def outer(k, carry, low=low, up=up):
            def inner(j, totals):
                real, imag = totals
                for at in parts:
                    a_now, b_now, c_now = x_ref[j, at, low], b_ref[j, at, low], c_ref[j, at, low]
                    g_real, g_imag = gs_ref[j + k, at, low], gs_ref[j + k, at, up]
                    real = real + a_now * g_real + b_now * g_imag
                    imag = imag + c_now * g_imag - b_now * g_real
                return real, imag

            real, imag = loop(0, pieces - k, inner, (zero, zero), pieces <= 8)
            p_ref[k, :, low] = real
            p_ref[k, :, up] = imag
            return carry

        loop(0, pieces, outer, 0, pieces <= 8)
    flat = mm3(p_ref[...].reshape(pieces * span, doubled), back_ref[...])
    chunks = []
    for k in range(pieces):
        now = flat[k * span : (k + 1) * span, :half]
        if k + 1 < pieces:
            after = flat[(k + 1) * span : (k + 2) * span, half:]
            now = now + jnp.where(lane_of(after.shape) == 0, 0.0, after)
        chunks.append(now)
    response_grad = jnp.concatenate(chunks, 1)
    place = lane_of(response_grad.shape).astype(F32)
    response_grad = response_grad * jnp.exp(-place * damp_ref[:, 0:1])
    readout_grad = mm2(response_grad, s2[...], NT)
    pre_two = mm3(read_ref[...], response_grad) * c2[...].astype(F32)
    order = s1.shape[0]
    high = pre_two.astype(BF16)
    low = (pre_two - high.astype(F32)).astype(BF16)
    mapping_grad = mm(s1[...], low, NT) + mm(s1[...], high, NT)
    pre_one = mm3(map_ref[...], pre_two) * c1[...].astype(F32)
    lift_grad = mm3(feat_ref[...], pre_one, NT)

    sect = time_rows(sect_ref, span).astype(BF16)
    high = sg_ref[...].astype(BF16)
    low = (sg_ref[...] - high.astype(F32)).astype(BF16)
    tw = (mm(sect, low, NT) + mm(sect, high, NT)) * same_ref[...]
    tw = mm(pick_ref[...], tw, NN, HIGHEST)
    cg = cg_ref[...].astype(F32)
    signal = signal_ref[...].astype(F32)
    taps = []
    for m in range(3):
        moved = signal if m == 0 else earlier_lanes(signal, m, length)
        taps.append(jnp.sum(moved * cg, 1, keepdims=True))
    column = lane_of((span, 128))
    columns = sum(jnp.where(column == BLOCKS + m, taps[m], 0.0) for m in range(3))
    tw = tw + columns.T[: tw.shape[0], :span]
    tw = jnp.concatenate([tw, jnp.zeros((8, order - span), F32)], 1)
    out = jnp.concatenate([mapping_grad, lift_grad, readout_grad, tw], 0)
    out_ref[...] = out.astype(out_ref.dtype)


def last_body(
    fast, fg_ref, perm_ref, inner_ref, norm_ref, n1_ref, res_ref, tok_ref, gains_ref, out_ref, *pay
):
    width = inner_ref.shape[1]
    first = [v.astype(BF16) for v in receive_pieces(fg_ref, perm_ref)]
    norm = parts_of(norm_ref[...])
    normed, factor = normalize_rows(tok_ref[...].astype(F32))
    normed = parts_of(normed)
    gain = parts_of(gains_ref[0:1, :])
    grads = [
        mm(first[a], inner_ref[a * width : (a + 1) * width, :], NT) + n1_ref[a]
        for a in range(BLOCKS)
    ]
    scaled = [grads[a] * gain[a] for a in range(BLOCKS)]
    total = width * BLOCKS
    plain = sum(jnp.sum(v, -1, keepdims=True) for v in scaled) / total
    joint = sum(jnp.sum(scaled[a] * normed[a], -1, keepdims=True) for a in range(BLOCKS)) / total
    out_ref[...] = jnp.concatenate(
        [res_ref[a] + factor * (scaled[a] - plain - normed[a] * joint) for a in range(BLOCKS)], 1
    )
    gain_grad = [jnp.sum(grads[a] * normed[a], 0, keepdims=True) for a in range(BLOCKS)]
    weight = [mm(norm[a], first[a], TN) for a in range(BLOCKS)]
    if not fast:
        for a in range(BLOCKS):
            pay[0][a * width : (a + 1) * width, :] = weight[a]
            pay[1][a : a + 1, :] = gain_grad[a]
        return
    count, rows, _ = pay[0].shape
    share = count // BLOCKS
    held = (rows - 8) * 3 // 5
    flat = jnp.concatenate(gain_grad, 1)
    tail = [flat[:, k : k + 128] for k in range(0, total, 128)]
    tail = jnp.concatenate(tail + [jnp.zeros((8 - len(tail), 128), F32)], 0)
    for a in range(BLOCKS):
        for k in range(share):
            block = pack_rows(weight[a][k * held : (k + 1) * held])
            pay[0][a * share + k] = jnp.concatenate([block, tail], 0).astype(BF16)


def first_sum_body(
    keep_ref, got_ref, side_ref, side_got, small_ref, small_got, left_keep, left_send, right_keep, right_send
):
    n, _, cut = left_keep.shape
    n -= 1
    for k in range(2 * n):
        main = keep_ref[k].astype(F32) + got_ref[k].astype(F32)
        side = side_ref[k].astype(F32) + side_got[k].astype(F32)
        right = jnp.concatenate([main[:, cut:], side], 1).astype(BF16)
        left_out, right_out = (left_keep, right_keep) if k < n else (left_send, right_send)
        left_out[k % n] = main[:, :cut].astype(BF16)
        right_out[k % n] = right
    small = (small_ref[...].astype(F32) + small_got[...].astype(F32)).astype(BF16)
    left_keep[n] = small
    left_send[n] = small


def second_sum_body(
    left_ref, left_got, right_ref, right_got, left_keep, left_send, right_keep, right_send
):
    n = right_keep.shape[0]
    for k in range(2 * n):
        left = (left_ref[k].astype(F32) + left_got[k].astype(F32)).astype(BF16)
        right = (right_ref[k].astype(F32) + right_got[k].astype(F32)).astype(BF16)
        left_out, right_out = (left_keep, right_keep) if k < n else (left_send, right_send)
        left_out[k % n] = left
        right_out[k % n] = right
    small = (left_ref[2 * n].astype(F32) + left_got[2 * n].astype(F32)).astype(BF16)
    left_keep[n] = small
    left_send[n] = small


def third_sum_body(left_ref, left_got, right_ref, right_got, *outs):
    left = [(left_ref[k].astype(F32) + left_got[k].astype(F32)).astype(BF16) for k in range(5)]
    right = [(right_ref[k].astype(F32) + right_got[k].astype(F32)).astype(BF16) for k in range(4)]
    for k, out_ref in enumerate(outs):
        out_ref[...] = jnp.concatenate([left[k], right[k], left[4]], 1)


def weights_out_body(
    own_ref, one_ref, two_ref, three_ref, expand_ref, spread_ref, shrink_ref, mix_ref, rest_ref
):
    parts = [ref[...].astype(F32) for ref in (own_ref, one_ref, two_ref, three_ref)]
    held = (parts[0] + parts[1]) + (parts[2] + parts[3])
    owned, wide = expand_ref.shape[1:]
    width = mix_ref.shape[2]
    for k in range(2):
        expand_ref[k] = held[:, k * wide : (k + 1) * wide]
        start = 2 * wide + BLOCKS * width + k * width
        mix_ref[1 - k] = held[:, start : start + width]
    for g in range(BLOCKS):
        start = 2 * wide + g * width
        shrink_ref[g * owned : (g + 1) * owned, :] = held[:, start : start + width]
    start = 3 * wide + 2 * width
    small = jnp.concatenate([held[:, start : start + wide], held[:, start + wide :]], 0)
    for k in range(2):
        spread_ref[k] = small[16 * k : 16 * k + 16]
    for k in range(BLOCKS):
        rest_ref[k] = small[32:, k * width : (k + 1) * width]


def small_out_body(
    place_ref, own_ref, one_ref, two_ref, three_ref, rest_ref, perm_ref, twiddle_ref, kernel_ref, lift_ref, phase_ref, map_ref, read_ref, q_ref,
):
    order = map_ref.shape[0]
    m_rows, q_rows = order + 8, q_ref.shape[1]
    chans = q_rows - 8
    pieces = q_ref.shape[0]
    width = perm_ref.shape[2]
    parts = [ref[...] for ref in (own_ref, one_ref, two_ref, three_ref)]
    sums = [part[:m_rows].astype(F32) for part in parts]
    m_sum = (sums[0] + sums[1]) + (sums[2] + sums[3])
    map_ref[...] = m_sum[:order]
    lift_ref[...] = m_sum[order : order + lift_ref.shape[0]]
    phase_ref[...] = m_sum[order + lift_ref.shape[0] : order + lift_ref.shape[0] + 1]
    for k, outer in enumerate((0, 2, 1, 3)):
        for n, inner in enumerate((0, 4, 8, 12)):
            start = m_rows + n * q_rows
            q_ref[jnp.bitwise_xor(place_ref[0], outer ^ inner)] = parts[k][
                start : start + q_rows
            ].astype(F32)
    tall = jnp.concatenate([q_ref[n, :chans] for n in range(pieces)], 0).astype(BF16)
    broad = jnp.concatenate([q_ref[n, chans:, :chans] for n in range(pieces)], 1).astype(BF16)
    rest = [mm(broad, perm_ref[b]) for b in range(BLOCKS)]
    read_ref[...] = jnp.concatenate([mm(tall, perm_ref[b], TN) for b in range(BLOCKS)], 1)
    for a in range(BLOCKS):
        for b in range(BLOCKS):
            twiddle_ref[0, 4 * a + b : 4 * a + b + 1, :] = rest[b][a : a + 1]
    twiddle_ref[1] = rest_ref[2]
    twiddle_ref[2] = rest_ref[1]
    last = rest_ref[3]
    taps = [rest[b][BLOCKS : BLOCKS + 3] for b in range(BLOCKS)]
    taps += [last[BLOCKS + 3 * b : BLOCKS + 3 * b + 3] for b in range(BLOCKS)]
    kernel_ref[...] = jnp.concatenate(taps, 1)


def value_out_body(value_ref, mix_ref, rest_ref, gains_ref, mixing_ref):
    last = rest_ref[3]
    total = value_ref[0].astype(F32)
    for n in range(1, value_ref.shape[0]):
        total = total + value_ref[n].astype(F32)
    owned = mix_ref.shape[1]
    held = owned * 5 // 3
    mixing_ref[0] = unpack_rows(total, owned)
    mixing_ref[1] = mix_ref[0]
    mixing_ref[2] = mix_ref[1]
    one = jnp.concatenate([total[held + k : held + k + 1] for k in range(6)], 1)
    two = jnp.concatenate([last[a : a + 1] for a in range(BLOCKS)], 1)
    gains_ref[...] = jnp.concatenate([one, two], 0)


def hop(values, distance):
    pieces = lax.axis_size("seq")
    return lax.ppermute(values, "seq", [(n, n ^ distance) for n in range(pieces)])


def hop_y(values, distance=0):
    if not distance:
        return lax.ppermute(values, "batch", [(0, 1), (1, 0)])
    apart = 2 * distance + 1
    return lax.ppermute(values, BOTH, [(n, n ^ apart) for n in range(2 * lax.axis_size("seq"))])


def pair_sum(parts, kind):
    wide = [v.astype(F32) for v in parts]
    return ((wide[0] + wide[1]) + (wide[2] + wide[3])).astype(kind)


def held_until(values, *others):
    return lax.optimization_barrier((values, *others))[0]


def added(kept, came, at, kind):
    return (kept[at].astype(F32) + came[at].astype(F32)).astype(kind)


def per_device(
    tokens,
    cotangent,
    gains,
    mixing,
    twiddle,
    expand,
    spread,
    shrink,
    squeeze,
    kernel,
    lifting,
    phases,
    mapping,
    readout,
    damping,
):
    seqs, share, total = tokens.shape
    pieces, groups = lax.axis_size("seq"), lax.axis_size("batch")
    devices = pieces * groups
    place = lax.axis_index("seq")
    me = (place * groups + lax.axis_index("batch")).astype(jnp.int32).reshape(1)
    rows = seqs * share
    length = pieces * share
    width = total // BLOCKS
    wide = expand.shape[2]
    owned = mixing.shape[1]
    octet = devices // BLOCKS
    order = mapping.shape[0]
    fast = pieces == 16 and groups == 2 and owned % 8 == 0 and seqs == 2
    span = width // pieces
    chans = BLOCKS * span
    def exchange(values):
        return lax.all_to_all(values, "seq", 0, 0, tiled=True)

    block = 2 * share
    count = length // block
    table, table_back = packed_tables(block)
    high, low = split_table(table[:block])
    perm = spread_matrix(pieces, span)
    feats = feature_rows(length)
    same = np.tile(np.eye(span, dtype=np.float32), (BLOCKS, BLOCKS))
    pick = np.zeros((8, chans), np.float32)
    for a in range(BLOCKS):
        pick[a, a * span : (a + 1) * span] = 1.0

    shrink_own = shrink.reshape(BLOCKS, owned, width).swapaxes(0, 1).reshape(owned, BLOCKS * width)
    packed = jnp.concatenate(
        [expand[0], expand[1], shrink_own, mixing[1], mixing[2]], 1
    )
    if fast:
        z_got = [hop(packed, d) for d in (4, 8, 12)]
        own = pack_rows(held_until(mixing[0], packed))
        own = jnp.broadcast_to(own[None], (devices,) + own.shape)
        inner_part = lax.all_to_all(own, BOTH, 0, 0, tiled=True)
    else:
        inner_part = lax.all_gather(mixing[0], BOTH, axis=0, tiled=True)
        full = lax.all_gather(packed, BOTH, axis=0, tiled=True)
        full, pair = full[:, : 2 * wide], full[:, 3 * wide :]
        shrink_full = lax.all_gather(shrink, BOTH, axis=0, tiled=True).reshape(BLOCKS, wide, width)

    tok = tokens.reshape(rows, total)
    cot = cotangent.reshape(rows, total)
    (norm,) = call(norm_body, [((rows, total), BF16)], [tok, gains], 1)

    tw_units, sp_units = twiddle.transpose(0, 2, 3, 1), spread.transpose(0, 2, 3, 1)
    sq_units = squeeze.transpose(1, 2, 0)
    s1, c1, s2, c2, spec, read_own, columns, mix_own = call(
        filter_body,
        [((order, length), BF16)] * 4
        + [((count, chans, 2 * block), F32), ((order, chans), F32), ((chans, 8), F32)]
        + [((chans, chans), BF16)],
        [
            place.astype(jnp.int32).reshape(1), lifting, phases[None], mapping, readout, damping[None],
            kernel[:, :total], tw_units[0], perm, feats, table,
        ],
        7,
        scalars=1,
    )
    if fast:
        held = jnp.stack([packed] + z_got)
        left, right = held[:, :, :1408], held[:, :, 1408:]
        inner_part, left, right, _ = lax.optimization_barrier((inner_part, left, right, spec))

    blocks = (pieces, seqs * chans, share)
    inner, sect_out = call(
        functools.partial(value_body, fast),
        [((total, width), BF16), (blocks, BF16)],
        [inner_part, norm, perm],
        2,
    )
    sect_in = exchange(sect_out)
    tokens = held_until(tokens, sect_out)
    ahead = [(n, n + 1) for n in range(pieces - 1)]
    halo = lax.ppermute(tokens[:, share - 2 :], "seq", ahead)
    if fast:
        got = held_until((hop(left, 2), hop_y(right)), sect_out)
        left, right = jnp.concatenate([left, got[0]], 0), jnp.concatenate([right, got[1]], 0)
        got = (hop_y(left), hop(right, 2))
        left, right = jnp.concatenate([left, got[0]], 0), jnp.concatenate([right, got[1]], 0)
        sect_in, left, right, halo = lax.optimization_barrier((sect_in, left, right, halo))
    spectra = (count, seqs * chans, 2 * block)
    long_blocks = (count, seqs * chans, block)
    conv_scratch = [
        pltpu.VMEM(spectra, F32),
        pltpu.VMEM(spectra, F32),
        pltpu.VMEM((count, chans, block), F32),
        pltpu.VMEM((count, chans, block), F32),
    ]
    long_out, conv_in, signal = call(
        functools.partial(conv_body, length),
        [(blocks, BF16), (long_blocks, BF16), ((chans, seqs * length), BF16)],
        [sect_in, mix_own, columns, spec, high, low, table_back[:, :block]],
        7,
        scratch=conv_scratch,
    )
    long_in = exchange(long_out)
    if fast:
        got = held_until((hop(left, 1), hop(right, 1)), long_out)
        full, shrink_full, pair = call(
            gather_body,
            [((total, 2 * wide), BF16), ((BLOCKS, wide, width), BF16), ((total, 2 * width), BF16)],
            [me, left, got[0], right, got[1]],
            5,
            scalars=1,
        )

    quad = (BLOCKS, rows, width)
    sect_sw, switch, switch_edge, gate_seq = call(
        functools.partial(switch_body, seqs),
        [(quad, F32), (quad, BF16), ((BLOCKS, 16, width), BF16), (quad, F32)],
        [norm, halo, gains, pair, tw_units[1], kernel],
        1,
    )

    broad = (BLOCKS, rows, wide)
    if fast:
        half_devices = devices // 2
        weight_shapes = [((half_devices, owned, 3 * wide + width), BF16)] * 2
        side_shapes = [((half_devices, owned, width), BF16)] * 2
    else:
        weight_shapes = [((total, 3 * wide + width), F32)]
        side_shapes = [((total, width), F32)]
    (
        layer, lg_out, switch_grad, res_grad, spread_part, squeeze_part, merge_part, gain_part,
        first_rows, *main,
    ) = call(
        functools.partial(middle_body, fast, owned, seqs),
        [
            ((rows, total), BF16), (blocks, BF16), (quad, BF16), (quad, F32),
            ((2, 16, wide), F32), ((16, width), F32), ((16, width), F32), ((BLOCKS, width), F32),
            ((BLOCKS, 2 * seqs, width), BF16),
        ] + weight_shapes,
        [me, long_in, gate_seq, tok, cot, gains, full, shrink_full, pair, tw_units[2],
         sp_units, sq_units, perm],
        27,
        scratch=[pltpu.VMEM(broad, F32)] * 5
        + [pltpu.VMEM(broad, BF16)] * 3
        + [pltpu.VMEM((2, 16, wide), F32)],
        late=(4, 6, 7),
        early=(0, 1, 2, 3),
        scalars=1,
    )
    lg_in = exchange(lg_out)

    after = lax.ppermute(first_rows, "seq", [(to, at) for at, to in ahead])
    n1_sw, small, *side = call(
        functools.partial(switch_back_body, fast, owned, seqs),
        [(quad, F32), ((24, 2 * wide), BF16)] + side_shapes,
        [me, switch_grad, after, switch, switch_edge, sect_sw, pair, tw_units[1], kernel, norm,
         spread_part, squeeze_part, merge_part, gain_part],
        5,
        scalars=1,
    )
    if fast:
        got, side_got, small_got = hop(main[1], 1), hop(side[1], 1), hop(small, 1)
        def sum_shapes(n):
            left, right = ((n + 1, owned, 2 * wide), BF16), ((n, owned, wide + 2 * width), BF16)
            return [left, left, right, right]

        left, left_send, right, right_send = call(
            first_sum_body,
            sum_shapes(half_devices // 2),
            [main[0], got, side[0], side_got, small, small_got],
            4,
        )
        lg_in = held_until(lg_in, left, left_send, right, right_send)

    fg_out, conv_grad, signal_grad = call(
        functools.partial(conv_back_body, length),
        [(blocks, BF16), ((chans, seqs * length), BF16), ((chans, seqs * length), F32)],
        [lg_in, mix_own, columns, spec, high, low, table_back[:, :block]],
        8,
        scratch=conv_scratch,
    )
    fg_in = exchange(fg_out)

    if fast:
        got = held_until((hop_y(left_send), hop(right_send, 2)), fg_out)
        left, left_send, right, right_send = call(
            second_sum_body, sum_shapes(half_devices // 4), [left, got[0], right, got[1]], 3
        )
        lg_in = held_until(lg_in, left, left_send, right, right_send)

    q_rows = chans + 8
    m_rows = order + 8
    (both,) = call(
        functools.partial(filter_back_body, length),
        [((m_rows + q_rows, order), BF16 if fast else F32)],
        [
            lg_in, conv_in, sect_in, signal, conv_grad, signal_grad, s1, c1, s2, c2, read_own,
            mapping, columns, feats, high, low, table_back, same, pick,
        ],
        14,
        scratch=[
            pltpu.VMEM(spectra, F32),
            pltpu.VMEM(long_blocks, F32),
            pltpu.VMEM(long_blocks, F32),
            pltpu.VMEM(spectra, F32),
            pltpu.VMEM((count, chans, 2 * block), F32),
        ],
    )

    if fast:
        got = held_until((hop(left_send, 2), hop_y(right_send)), both)
        shape = ((owned, 5 * wide + 2 * width), BF16)
        own, *sends = call(third_sum_body, [shape] * 4, [left, got[0], right, got[1]], 2)
        z_got = [hop(sent, d) for sent, d in zip(sends, (8, 4, 12))]
        both = added(both, held_until(hop_y(both), own), slice(0, None), BF16)
        fg_in = held_until(fg_in, own, sends, both)

    if fast:
        last_shapes = [((devices, owned * 5 // 3 + 8, 128), BF16)]
    else:
        last_shapes = [((total, width), F32), ((BLOCKS, width), F32)]
    tokens_grad, *pay = call(
        functools.partial(last_body, fast),
        [((rows, total), F32)] + last_shapes,
        [fg_in, perm, inner, norm, n1_sw, res_grad, tok, gains],
        3,
    )
    if fast:
        value_parts = lax.all_to_all(pay[0], BOTH, 0, 0, tiled=True)
    else:
        value_grad = lax.psum_scatter(pay[0], BOTH, scatter_dimension=0, tiled=True)
        gain_one = lax.psum(pay[1], BOTH)

    if fast:
        got = [both] + held_until([hop(both, d) for d in (4, 8, 12)], tokens_grad, z_got)
        m_sum = pair_sum([g[:m_rows] for g in got], BF16)
        both = jnp.concatenate([m_sum] + [g[m_rows:] for g in got], 0)
        z_shapes = [((2, owned, wide), F32), ((2, 16, wide), F32), ((BLOCKS * owned, width), F32)]
        z_shapes += [((2, owned, width), F32), ((BLOCKS, 16, width), F32)]
        expand_grad, spread_sum, shrink_grad, mix_sum, rest_sum = call(
            weights_out_body, z_shapes, [own, *z_got], 4
        )
        got = [both] + held_until([hop(both, d) for d in (2, 1, 3)], rest_sum)
        out_shapes = [(3, 16, width), (3, 2 * total), lifting.shape, (1, order), mapping.shape]
        twiddle_sum, kernel_grad, lifting_grad, phases_grad, mapping_grad, readout_grad = call(
            small_out_body,
            [(shape, F32) for shape in (*out_shapes, readout.shape)],
            [place.astype(jnp.int32).reshape(1), *got, rest_sum, perm],
            3,
            scratch=[pltpu.VMEM((pieces, q_rows, order), F32)],
            scalars=1,
        )
        gains_grad, mixing_grad = call(
            value_out_body,
            [((2, total), F32), ((3, owned, width), F32)],
            [held_until(value_parts, twiddle_sum), mix_sum, rest_sum],
            1,
        )
        squeeze_sum = rest_sum[0]
    else:
        m_sum = lax.psum(both[:m_rows], BOTH)
        q_all = lax.all_gather(lax.psum(both[m_rows:], "batch"), "seq", axis=0, tiled=False)
        main_sum = lax.psum_scatter(main[0], BOTH, scatter_dimension=0, tiled=True)
        switch_own = lax.psum_scatter(side[0], BOTH, scatter_dimension=0, tiled=True)
        small = lax.psum(small.astype(F32), BOTH)
        small = jnp.concatenate([small[:, :wide], small[:, wide : 2 * wide]], 0)

        expand_grad = jnp.stack([main_sum[:, k * wide : (k + 1) * wide] for k in range(2)])
        shrink_grad = main_sum[:, 2 * wide : 3 * wide].reshape(owned, BLOCKS, width)
        shrink_grad = shrink_grad.swapaxes(0, 1).reshape(BLOCKS * owned, width)
        mixing_grad = jnp.stack([value_grad, switch_own, main_sum[:, 3 * wide :]])
        spread_sum = small[:32].reshape(2, 16, wide)
        squeeze_sum, merge_sum, switch_sum, tail_sum = small[32:].reshape(16, BLOCKS, width).swapaxes(0, 1)
        value_sum = q_all[:, chans : chans + BLOCKS, :chans].reshape(pieces, BLOCKS, BLOCKS, span)
        value_sum = value_sum.transpose(1, 2, 0, 3).reshape(16, width)
        twiddle_sum = jnp.stack([value_sum, switch_sum, merge_sum])
        taps_value = q_all[:, chans + BLOCKS : chans + BLOCKS + 3, :chans]
        taps_value = taps_value.reshape(pieces, 3, BLOCKS, span).transpose(1, 2, 0, 3)
        taps_sum = tail_sum[BLOCKS:].reshape(BLOCKS, 3, width).swapaxes(0, 1)
        kernel_grad = jnp.concatenate(
            [taps_value.reshape(3, total), taps_sum.reshape(3, total)], 1
        )
        readout_grad = q_all[:, :chans].reshape(pieces, BLOCKS, span, order)
        readout_grad = readout_grad.transpose(3, 1, 0, 2).reshape(order, total)
        gains_grad = jnp.stack([gain_one.reshape(total), tail_sum[:BLOCKS].reshape(total)])
        lifting_grad = m_sum[order : order + lifting.shape[0]]
        phases_grad = m_sum[order + lifting.shape[0]]
        mapping_grad = m_sum[:order]

    def of_units(rows_now):
        lead = rows_now.shape[:-2]
        shaped = rows_now.reshape(*lead, BLOCKS, BLOCKS, rows_now.shape[-1])
        return jnp.moveaxis(shaped, -1, -3)

    return (
        layer.reshape(seqs, share, total),
        tokens_grad.reshape(seqs, share, total),
        gains_grad,
        mixing_grad,
        of_units(twiddle_sum),
        expand_grad,
        of_units(spread_sum),
        shrink_grad,
        of_units(squeeze_sum),
        kernel_grad,
        lifting_grad,
        phases_grad.reshape(order),
        mapping_grad,
        readout_grad,
    )


def solution(mesh):
    return jax.shard_map(
        per_device,
        mesh=mesh,
        in_specs=(
            P("batch", "seq", None),
            P("batch", "seq", None),
            P(),
            P(None, ("seq", "batch"), None),
            P(),
            P(None, ("seq", "batch"), None),
            P(),
            P(("seq", "batch"), None),
            P(),
            P(),
            P(),
            P(),
            P(),
            P(),
            P(),
        ),
        out_specs=(
            P("batch", "seq", None),
            P("batch", "seq", None),
            P(),
            P(None, ("seq", "batch"), None),
            P(),
            P(None, ("seq", "batch"), None),
            P(),
            P(("seq", "batch"), None),
            P(),
            P(),
            P(),
            P(),
            P(),
            P(),
        ),
        check_vma=False,
    )
```
